32 devices in a mesh: item: 4 (over y, x), head: 8 (over z, core).
Axes of the slice: x: 2, y: 2, z: 4, core: 2. Of those that a mesh axis runs over, the one named last changes fastest.
Arguments:
- layer_input: bfloat16 [8192, 2048], P(('item', 'head')), may hold values from -6 to 6
- lengths: int32 [8], P('item'), may hold values from 256 to 1024, as said below
- norm_gain: bfloat16 [2048], replicated, may hold values from 0.5 to 1.5
- w_query: bfloat16 [2048, 2048], P(None, 'head'), may hold values from -0.125 to 0.125
- w_key: bfloat16 [2048, 2048], P(None, 'head'), may hold values from -0.125 to 0.125
- w_value: bfloat16 [2048, 4096], P(None, 'head'), may hold values from -0.125 to 0.125
- w_outgate: bfloat16 [2048, 4096], P(None, 'head'), may hold values from -0.125 to 0.125
- w_decay: bfloat16 [2048, 16], P(None, 'head'), may hold values from -0.125 to 0.125
- w_write: bfloat16 [2048, 16], P(None, 'head'), may hold values from -0.125 to 0.125
- conv_query: bfloat16 [4, 2048], P(None, 'head'), may hold values from -3 to 3
- conv_key: bfloat16 [4, 2048], P(None, 'head'), may hold values from -3 to 3
- conv_value: bfloat16 [4, 4096], P(None, 'head'), may hold values from -3 to 3
- decay_log: float32 [16], P('head'), may hold values from -7 to -2.5
- out_gain: bfloat16 [256], replicated, may hold values from 0.5 to 1.5
- w_out: bfloat16 [4096, 2048], P('head'), may hold values from -0.125 to 0.125
- ffn_gain: bfloat16 [2048], replicated, may hold values from 0.5 to 1.5
- w_gate: bfloat16 [2048, 5632], P(None, 'head'), may hold values from -0.125 to 0.125
- w_up: bfloat16 [2048, 5632], P(None, 'head'), may hold values from -0.125 to 0.125
- w_down: bfloat16 [5632, 2048], P('head'), may hold values from -0.109375 to 0.109375
- cotangent: bfloat16 [8192, 2048], P(('item', 'head')), may hold values from -6 to 6
Outputs:
- output: bfloat16 [8192, 2048], P(('item', 'head'))
- input_grad: float32 [8192, 2048], P(('item', 'head'))
- grad_norm_gain: float32 [2048], replicated
- grad_w_query: float32 [2048, 2048], P(None, 'head')
- grad_w_key: float32 [2048, 2048], P(None, 'head')
- grad_w_value: float32 [2048, 4096], P(None, 'head')
- grad_w_outgate: float32 [2048, 4096], P(None, 'head')
- grad_w_decay: float32 [2048, 16], P(None, 'head')
- grad_w_write: float32 [2048, 16], P(None, 'head')
- grad_conv_query: float32 [4, 2048], P(None, 'head')
- grad_conv_key: float32 [4, 2048], P(None, 'head')
- grad_conv_value: float32 [4, 4096], P(None, 'head')
- grad_decay_log: float32 [16], P('head')
- grad_out_gain: float32 [256], replicated
- grad_w_out: float32 [4096, 2048], P('head')
- grad_ffn_gain: float32 [2048], replicated
- grad_w_gate: float32 [2048, 5632], P(None, 'head')
- grad_w_up: float32 [2048, 5632], P(None, 'head')
- grad_w_down: float32 [5632, 2048], P('head')
The draws below stay inside these ranges and needn't reach their ends.
Inputs may be any that keep to these rules, and one draw needn't show every extreme that they name: `lengths`: exactly one sequence in all holds 1024 live tokens.
All inputs are finite; a program needn't handle non-finite values.
Results may differ from the reference program's by a relative error of at most 0.017.
Values may be sent and summed in bfloat16 or wider, within the bound.
A program may use at most 320 MiB of HBM per device.

```python
from functools import partial
import jax
import jax.numpy as jnp
from jax import lax

D = 2048
H = 16
DK = 128
DV = 256
FF = 5632
BLOCK = 64
CONV = 4
SEQ_LEN = 1024
TOKENS = 8192
SEQS = 8


def draw_lengths(key, part):
    base = jax.random.randint(jax.random.fold_in(key, 11), (SEQS,), SEQ_LEN // 4, SEQ_LEN)
    pick = jax.random.randint(jax.random.fold_in(key, 12), (1,), 0, SEQS)
    full = jnp.arange(SEQS, dtype=jnp.int32) == pick
    return jnp.where(full, SEQ_LEN, base).astype(jnp.int32)


def block_levels(key, shape, cuts, low, top_value):
    factor_of = 1.0
    for dim, shards_of in cuts:
        steps = jax.random.uniform(jax.random.fold_in(jax.random.fold_in(key, 6), dim), (shards_of,), jnp.float32, low / len(cuts), top_value / len(cuts))
        factor_of = factor_of * jnp.repeat(jnp.exp(steps), shape[dim] // shards_of).reshape((-1,) + (1,) * (len(shape) - 1 - dim))
    return factor_of


def noise(stream_key, extent, deviation, limit, cuts=(), kind=jnp.bfloat16):
    drawn = jax.random.normal(stream_key, extent, jnp.float32) * deviation
    if len(cuts) > 0:
        drawn = block_levels(stream_key, extent, cuts, -0.22, 0.18) * drawn
    return jnp.clip(drawn, min=-limit, max=limit).astype(kind)


def setup_inputs(seed: int = 0) -> dict:
    streams_of = jax.random.split(jax.random.key(seed), 21)
    layer_input = noise(streams_of[0], (TOKENS, D), 1.0, 6.0, ((0, 32),))
    lengths = draw_lengths(jax.random.fold_in(streams_of[20], 71), 0)
    norm_gain = jnp.clip(1.0 + 0.1 * jax.random.normal(streams_of[2], (D,), jnp.float32), 0.5, 1.5).astype(jnp.bfloat16)
    w_query = noise(streams_of[3], (D, H * DK), D ** -0.5, 0.125, ((1, 8),))
    w_key = noise(streams_of[4], (D, H * DK), D ** -0.5, 0.125, ((1, 8),))
    w_value = noise(streams_of[5], (D, H * DV), D ** -0.5, 0.125, ((1, 8),))
    w_outgate = noise(streams_of[6], (D, H * DV), D ** -0.5, 0.125, ((1, 8),))
    w_decay = noise(streams_of[7], (D, H), D ** -0.5, 0.125, ((1, 8),))
    w_write = noise(streams_of[8], (D, H), D ** -0.5, 0.125, ((1, 8),))
    conv_query = noise(streams_of[9], (CONV, H * DK), 0.5, 3.0, ((1, 8),))
    conv_key = noise(streams_of[10], (CONV, H * DK), 0.5, 3.0, ((1, 8),))
    conv_value = noise(streams_of[11], (CONV, H * DV), 0.5, 3.0, ((1, 8),))
    decay_log = jnp.clip(-7.0 + 4.5 * jax.random.uniform(streams_of[12], (H,), jnp.float32) ** block_levels(streams_of[12], (H,), ((0, 8),), -0.2, 0.2), -7.0, -2.5)
    out_gain = jnp.clip(1.0 + 0.1 * jax.random.normal(streams_of[13], (DV,), jnp.float32), 0.5, 1.5).astype(jnp.bfloat16)
    w_out = noise(streams_of[14], (H * DV, D), (H * DV // 2) ** -0.5, 0.125, ((0, 8),))
    ffn_gain = jnp.clip(1.0 + 0.1 * jax.random.normal(streams_of[15], (D,), jnp.float32), 0.5, 1.5).astype(jnp.bfloat16)
    w_gate = noise(streams_of[16], (D, FF), D ** -0.5, 0.125, ((1, 8),))
    w_up = noise(streams_of[17], (D, FF), D ** -0.5, 0.125, ((1, 8),))
    w_down = noise(streams_of[18], (FF, D), (FF // 2) ** -0.5, 0.109375, ((0, 8),))
    cotangent = noise(streams_of[19], (TOKENS, D), 1.0, 6.0, ((0, 32),))
    return dict(layer_input=layer_input, lengths=lengths, norm_gain=norm_gain, w_query=w_query, w_key=w_key, w_value=w_value, w_outgate=w_outgate, w_decay=w_decay, w_write=w_write, conv_query=conv_query, conv_key=conv_key, conv_value=conv_value, decay_log=decay_log, out_gain=out_gain, w_out=w_out, ffn_gain=ffn_gain, w_gate=w_gate, w_up=w_up, w_down=w_down, cotangent=cotangent)


HIGHEST = lax.Precision.HIGHEST

@jax.custom_vjp
def low(v):
    return lax.optimization_barrier(v.astype(jnp.bfloat16)).astype(jnp.float32)

@jax.custom_vjp
def low_back(v):
    return v

def low_keep(v):
    return (low(v), None)

def low_pass(kept, grad):
    return (grad,)

def back_keep(v):
    return (v, None)

def back_low(kept, grad):
    return (low(grad),)
low.defvjp(low_keep, low_pass)
low_back.defvjp(back_keep, back_low)

def product(left, right):
    return jnp.dot(left.astype(jnp.float32), right.astype(jnp.float32), precision=HIGHEST, preferred_element_type=jnp.float32)

def root_scale(values, gain):
    return values * lax.rsqrt(lax.optimization_barrier(jnp.mean(values * values, axis=-1, keepdims=True)) + 1e-05) * gain

def short_conv(values, kernel):
    width = kernel.shape[0]
    length = values.shape[1]
    padded = jnp.pad(values, ((0, 0), (width - 1, 0), (0, 0)))
    total = jnp.zeros_like(values)
    for offset in range(width):
        total = total + kernel[offset] * padded[:, offset:offset + length]
    return jax.nn.silu(total)

def block_step(state, pieces):
    query, key_block, value, log_decay, write = pieces
    size = query.shape[0]
    rows = lax.broadcasted_iota(jnp.int32, (size, size), 0)
    columns = lax.broadcasted_iota(jnp.int32, (size, size), 1)
    lower = rows > columns
    causal = rows >= columns
    running = jnp.cumsum(log_decay)
    spread = running[:, None] - running[None, :]
    decay = jnp.exp(jnp.where(causal, spread, 0.0))
    start_decay = jnp.exp(running)
    keys_keys = product(key_block, key_block.T)
    system = jnp.eye(size, dtype=jnp.float32) + jnp.where(lower, decay * keys_keys, 0.0) * write[:, None]
    target = write[:, None] * (value - start_decay[:, None] * product(key_block, state.T))
    update = jax.scipy.linalg.solve_triangular(system, target, lower=True, unit_diagonal=True)
    weights = jnp.where(causal, decay * product(query, key_block.T), 0.0)
    output = start_decay[:, None] * product(query, state.T) + product(weights, update)
    final = running[-1]
    state = jnp.exp(final) * state + product((update * jnp.exp(final - running)[:, None]).T, key_block)
    return (state, output)

def delta_rule(query, keys, values, log_decay, write):
    count = query.shape[0] // BLOCK
    pieces = (query.reshape(count, BLOCK, -1), keys.reshape(count, BLOCK, -1), values.reshape(count, BLOCK, -1), log_decay.reshape(count, BLOCK), write.reshape(count, BLOCK))
    state = jnp.zeros((values.shape[-1], query.shape[-1]), jnp.float32)
    state, outputs = lax.scan(jax.checkpoint(block_step), state, pieces)
    return outputs.reshape(query.shape[0], -1)

def mixer(raw_query, raw_key, raw_value, raw_decay, raw_write, raw_outgate, conv_query, conv_key, conv_value, decay_log, out_gain, mask):
    tokens = raw_query.shape[0]
    heads = decay_log.shape[0]
    slots = tokens // SEQ_LEN

    def conv_heads(values, kernel, width):
        return short_conv(values.reshape(slots, SEQ_LEN, -1), kernel).reshape(slots, SEQ_LEN, heads, width)
    query = conv_heads(raw_query, conv_query, DK)
    keys = conv_heads(raw_key, conv_key, DK)
    values = conv_heads(raw_value, conv_value, DV)
    query = query * lax.rsqrt(lax.optimization_barrier(jnp.sum(query * query, axis=-1, keepdims=True)) + 1e-06) * DK ** (-0.5)
    keys = keys * lax.rsqrt(lax.optimization_barrier(jnp.sum(keys * keys, axis=-1, keepdims=True)) + 1e-06)
    live = mask.reshape(slots, SEQ_LEN, 1)
    log_decay = -jnp.exp(decay_log) * jax.nn.softplus(raw_decay.reshape(slots, SEQ_LEN, heads)) * live
    write = jax.nn.sigmoid(raw_write.reshape(slots, SEQ_LEN, heads)) * live
    per_head = jax.vmap(delta_rule, in_axes=(1, 1, 1, 1, 1), out_axes=1)
    per_slot = jax.vmap(per_head)
    output = per_slot(query, keys, values, log_decay, write) * live[..., None]
    output = root_scale(output, out_gain)
    gate = jax.nn.silu(raw_outgate.reshape(slots, SEQ_LEN, heads, DV))
    return (output * gate).reshape(tokens, heads * DV)

def layer(layer_input, norm_gain, w_query, w_key, w_value, w_outgate, w_decay, w_write, conv_query, conv_key, conv_value, decay_log, out_gain, w_out, ffn_gain, w_gate, w_up, w_down, mask):
    normed = low(root_scale(layer_input, norm_gain))
    raw_query = low_back(product(normed, w_query))
    raw_key = low_back(product(normed, w_key))
    raw_value = low_back(product(normed, w_value))
    raw_outgate = low_back(product(normed, w_outgate))
    raw_decay = low_back(product(normed, w_decay))
    raw_write = low_back(product(normed, w_write))
    mixed = low(mixer(raw_query, raw_key, raw_value, raw_decay, raw_write, raw_outgate, conv_query, conv_key, conv_value, decay_log, out_gain, mask))
    attended = low_back(product(mixed, w_out))
    resid = layer_input + attended
    normed_two = low(root_scale(resid, ffn_gain))
    gate = low_back(product(normed_two, w_gate))
    up = low_back(product(normed_two, w_up))
    hidden = low(jax.nn.silu(gate) * up)
    return resid + low_back(product(hidden, w_down))

def reference(layer_input, lengths, norm_gain, w_query, w_key, w_value, w_outgate, w_decay, w_write, conv_query, conv_key, conv_value, decay_log, out_gain, w_out, ffn_gain, w_gate, w_up, w_down, cotangent):
    position = jnp.arange(SEQ_LEN, dtype=jnp.int32)
    mask = (position[None, :] < lengths[:, None]).astype(jnp.float32).reshape(-1)
    params = [p.astype(jnp.float32) for p in (layer_input, norm_gain, w_query, w_key, w_value, w_outgate, w_decay, w_write, conv_query, conv_key, conv_value, decay_log, out_gain, w_out, ffn_gain, w_gate, w_up, w_down)]
    result, pullback = jax.vjp(partial(layer, mask=mask), *params)
    grads = pullback(cotangent.astype(jnp.float32))
    return (result.astype(jnp.bfloat16), grads[0], grads[1], grads[2], grads[3], grads[4], grads[5], grads[6], grads[7], grads[8], grads[9], grads[10], grads[11], grads[12], grads[13], grads[14], grads[15], grads[16], grads[17])
```

```python
import jax
import jax.numpy as jnp
from jax import lax
from jax.experimental import pallas as pl
from jax.experimental.pallas import tpu as pltpu
from jax.sharding import PartitionSpec as P

DK = 128
DV = 256
SEQ_LEN = 1024
CHUNK = 128
F32 = jnp.float32
BF16 = jnp.bfloat16


def mm(left, right, ta=False, tb=False):
    return lax.dot_general(
        left.astype(BF16),
        right.astype(BF16),
        (((0 if ta else 1,), (1 if tb else 0,)), ((), ())),
        preferred_element_type=F32,
    )


def split(value):
    high = value.astype(BF16)
    return high, (value - high.astype(F32)).astype(BF16)


def mm3(left, right):
    lh, ll = left
    rh, rl = right
    return mm(lh, rh) + (mm(lh, rl) + mm(ll, rh))


def sigmoid(x):
    return 1.0 / (1.0 + jnp.exp(-x))


def grids():
    rows = lax.broadcasted_iota(jnp.int32, (CHUNK, CHUNK), 0)
    cols = lax.broadcasted_iota(jnp.int32, (CHUNK, CHUNK), 1)
    return rows, cols


def to_row(col, eye):
    return jnp.sum(jnp.where(eye, col, 0.0), axis=0, keepdims=True)


def inverses(mats, rows, cols):
    eye = jnp.where(rows == cols, 1.0, 0.0)
    near = rows // 16 == cols // 16
    n1 = [jnp.where(near, -a, 0.0) for a in mats]
    n1s = [split(n) for n in n1]
    n2 = [mm3(n, n) for n in n1s]
    n2s = [split(n) for n in n2]
    n3 = [mm3(a, b) for a, b in zip(n1s, n2s)]
    n4s = [split(mm3(n, n)) for n in n2s]
    p1 = [eye + a + b + c for a, b, c in zip(n1, n2, n3)]
    p2 = [p + mm3(split(p), n) for p, n in zip(p1, n4s)]
    n8s = [split(mm3(n, n)) for n in n4s]
    x = [p + mm3(split(p), n) for p, n in zip(p2, n8s)]
    size = 16
    while size < CHUNK:
        pair = (rows // (2 * size) == cols // (2 * size)) & (rows // size != cols // size)
        xs = [split(v) for v in x]
        b = [split(jnp.where(pair, a, 0.0)) for a in mats]
        bx = [split(mm3(u, v)) for u, v in zip(b, xs)]
        x = [v - mm3(vs, w) for v, vs, w in zip(x, xs, bx)]
        size *= 2
    return x


def lead(ref):
    return ref[...].astype(F32)


def decays(ld, eye, causal):
    row = to_row(ld, eye)
    g = jnp.sum(jnp.where(causal, row, 0.0), axis=1, keepdims=True)
    grow = to_row(g, eye)
    d = jnp.where(causal, jnp.exp(jnp.where(causal, g - grow, 0.0)), 0.0)
    last = g[CHUNK - 1 : CHUNK, :]
    return d, jnp.exp(g), jnp.exp(last - g), jnp.exp(last)


def live_mask(len_ref, s, c):
    spot = lax.broadcasted_iota(jnp.int32, (CHUNK, 1), 0) + c * CHUNK
    return jnp.where(spot < len_ref[s], 1.0, 0.0)


def softplus(x):
    return jnp.maximum(x, 0.0) + jnp.log1p(jnp.exp(-jnp.abs(x)))


def mix_fwd_kernel(
    len_ref, proj_ref, conv_ref, dl_ref, gain_ref,
    mixed_ref, pre_ref, o_ref, u_ref, t_ref, s_ref, buf, state,
):
    c = pl.program_id(0)
    seqs, _, raws = buf.shape
    heads = dl_ref.shape[1]
    qw, gate_at, dw_at = heads * DK, raws, raws + heads * DV

    @pl.when(c == 0)
    def _():
        buf[:, 0:8, :] = jnp.zeros((seqs, 8, raws), F32)
        state[...] = jnp.zeros_like(state)

    rows, cols = grids()
    eye = rows == cols
    causal = rows >= cols
    lower = rows > cols
    rate = jnp.exp(dl_ref[...])
    st = []
    for s in range(seqs):
        buf[s, 8 : 8 + CHUNK, :] = proj_ref[s, :, 0:raws]
        pre = conv_ref[0:1, :] * buf[s, 5 : 5 + CHUNK, :]
        for j in range(1, 4):
            pre = pre + conv_ref[j : j + 1, :] * buf[s, 5 + j : 5 + j + CHUNK, :]
        pre_ref[s] = pre
        buf[s, 0:8, :] = buf[s, CHUNK : CHUNK + 8, :]
        act = pre * sigmoid(pre)
        mask = live_mask(len_ref, s, c)
        x = proj_ref[s, :, dw_at : dw_at + 2 * heads]
        ld2 = -rate * softplus(x[:, :heads]) * mask
        be2 = sigmoid(x[:, heads:]) * mask
        for h in range(heads):
            q = act[:, h * DK : (h + 1) * DK]
            k = act[:, qw + h * DK : qw + (h + 1) * DK]
            v = act[:, 2 * qw + h * DV : 2 * qw + (h + 1) * DV]
            q = q * (lax.rsqrt(jnp.sum(q * q, axis=1, keepdims=True) + 1e-06) * DK ** (-0.5))
            k = k * lax.rsqrt(jnp.sum(k * k, axis=1, keepdims=True) + 1e-06)
            be = be2[:, h : h + 1]
            d, ga, e, el = decays(ld2[:, h : h + 1], eye, causal)
            qb = q.astype(BF16)
            kb = k.astype(BF16)
            qk = jnp.concatenate([qb, kb], axis=0)
            both = mm(qk, kb, tb=True)
            w = d * both[:CHUNK]
            a = jnp.where(lower, d * both[CHUNK:], 0.0) * be
            st.append((s, h, mask, v, be, ga, e, el, qk, kb, w, a))
    inv = inverses([z[-1] for z in st], rows, cols)
    for i, (s, h, mask, v, be, ga, e, el, qk, kb, w, a) in enumerate(st):
        t = inv[i].astype(BF16)
        old = state[i]
        oldb = old.astype(BF16)
        s_ref[i] = oldb
        t_ref[i] = t
        qks = mm(qk, oldb)
        r = be * (v - ga * qks[CHUNK:])
        u = mm(t, r)
        ub = u.astype(BF16)
        u_ref[s, :, h * DV : (h + 1) * DV] = ub
        o = ga * qks[:CHUNK] + mm(w, ub)
        state[i] = el * old + mm(kb, e * u, ta=True)
        o = o * mask
        o_ref[s, :, h * DV : (h + 1) * DV] = o
        rg = proj_ref[s, :, gate_at + h * DV : gate_at + (h + 1) * DV]
        n = o * lax.rsqrt(jnp.mean(o * o, axis=1, keepdims=True) + 1e-05) * gain_ref[...]
        mixed_ref[s, :, h * DV : (h + 1) * DV] = (n * (rg * sigmoid(rg))).astype(BF16)


def mix_bwd_kernel(
    len_ref, proj_ref, conv_ref, dl_ref, gain_ref,
    gm_ref, pre_ref, o_ref, u_ref, t_ref, s_ref,
    gp_ref, gconv_ref, gdl_ref, ggain_ref, buf, dstate,
):
    step = pl.program_id(0)
    c = pl.num_programs(0) - 1 - step
    seqs, _, raws = buf.shape
    heads = dl_ref.shape[1]
    qw, gate_at, dw_at = heads * DK, raws, raws + heads * DV

    @pl.when(step == 0)
    def _():
        buf[:, CHUNK : CHUNK + 8, :] = jnp.zeros((seqs, 8, raws), F32)
        dstate[...] = jnp.zeros_like(dstate)
        gconv_ref[...] = jnp.zeros_like(gconv_ref)
        gdl_ref[...] = jnp.zeros_like(gdl_ref)
        ggain_ref[...] = jnp.zeros_like(ggain_ref)

    rows, cols = grids()
    eye = rows == cols
    causal = rows >= cols
    lower = rows > cols
    later = rows <= cols
    rate = jnp.exp(dl_ref[...])
    gain = gain_ref[...]
    for s in range(seqs):
        mask = live_mask(len_ref, s, c)
        x = proj_ref[s, :, dw_at : dw_at + 2 * heads]
        soft = -rate * mask
        ld2 = soft * softplus(x[:, :heads])
        sg = sigmoid(x)
        be2 = sg[:, heads:] * mask
        dlds = []
        dbes = []
        for h in range(heads):
            i = heads * s + h
            vs = slice(h * DV, (h + 1) * DV)
            gm = gm_ref[s, :, vs]
            o = o_ref[s, :, vs]
            rg = proj_ref[s, :, gate_at + h * DV : gate_at + (h + 1) * DV]
            sr = sigmoid(rg)
            r = lax.rsqrt(jnp.mean(o * o, axis=1, keepdims=True) + 1e-05)
            un = o * r
            gsg = gm * sr
            gp_ref[s, :, gate_at + h * DV : gate_at + (h + 1) * DV] = (
                gsg * (un * gain) * (1.0 + rg * (1.0 - sr))
            ).astype(BF16)
            dn = gsg * rg
            dnu = dn * un
            ggain_ref[...] += jnp.sum(dnu.reshape(CHUNK // 8, 8, DV), axis=0)
            do = (r * mask) * (dn * gain - un * jnp.mean(dnu * gain, axis=1, keepdims=True))
            pq = pre_ref[s, :, h * DK : (h + 1) * DK]
            pk = pre_ref[s, :, qw + h * DK : qw + (h + 1) * DK]
            pv = pre_ref[s, :, 2 * qw + h * DV : 2 * qw + (h + 1) * DV]
            sq = sigmoid(pq)
            sk = sigmoid(pk)
            sv = sigmoid(pv)
            q = pq * sq
            k = pk * sk
            v = pv * sv
            rq = lax.rsqrt(jnp.sum(q * q, axis=1, keepdims=True) + 1e-06)
            rk = lax.rsqrt(jnp.sum(k * k, axis=1, keepdims=True) + 1e-06)
            q = q * rq
            k = k * rk
            scale = DK ** (-0.5)
            be = be2[:, h : h + 1]
            d, ga, e, el = decays(ld2[:, h : h + 1], eye, causal)
            qb = (q * scale).astype(BF16)
            kb = k.astype(BF16)
            qk = jnp.concatenate([qb, kb], axis=0)
            both = mm(qk, kb, tb=True)
            w = d * both[:CHUNK]
            ab = jnp.where(lower, d * both[CHUNK:], 0.0)
            a = ab * be
            t = t_ref[i]
            st = s_ref[i]
            u = u_ref[s, :, vs]
            dh = dstate[i]
            dhb = dh.astype(BF16)
            qks = mm(qk, st)
            dob = do.astype(BF16)
            kdh = e * mm(kb, dhb)
            ubar = mm(w, dob, ta=True) + kdh
            rbar = mm(t, ubar, ta=True)
            rb = rbar.astype(BF16)
            uu = mm(jnp.concatenate([dob, rb], axis=0), u, tb=True)
            wbar = jnp.where(causal, uu[:CHUNK], 0.0)
            abar = -jnp.where(lower, uu[CHUNK:], 0.0)
            gks = ga * qks[CHUNK:]
            dv = be * rbar
            y = -ga * dv
            z = ga * do
            zy = jnp.concatenate([z.astype(BF16), y.astype(BF16)], axis=0)
            zys = mm(zy, st, tb=True)
            p = (wbar * d).astype(BF16)
            m = abar * d * be
            eu = e * u.astype(F32)
            dq = zys[:CHUNK] + mm(p, kb)
            dk = (
                zys[CHUNK:]
                + mm(p, qb, ta=True)
                + mm(m, kb)
                + mm(m, kb, ta=True)
                + mm(eu, dhb, tb=True)
            )
            dstate[i] = el * dh + mm(qk, zy, ta=True)
            ee = wbar * w + abar * a
            f = jnp.sum(u.astype(F32) * kdh, axis=1, keepdims=True)
            dbe = jnp.sum(rbar * (v - gks), axis=1, keepdims=True) + jnp.sum(
                abar * ab, axis=1, keepdims=True
            )
            dgc = (
                jnp.sum(ee, axis=1, keepdims=True)
                + jnp.sum(z * qks[:CHUNK] - dv * gks, axis=1, keepdims=True)
                - f
            )
            dgr = to_row(dgc, eye) - jnp.sum(ee, axis=0, keepdims=True)
            total = jnp.sum(f, axis=0, keepdims=True) + el * jnp.sum(
                jnp.sum(st.astype(F32) * dh, axis=1, keepdims=True), axis=0, keepdims=True
            )
            dld = jnp.sum(jnp.where(later, dgr, 0.0), axis=1, keepdims=True) + total
            dlds.append(dld)
            dbes.append(dbe)
            dq = dq * scale
            dqa = rq * (dq - q * jnp.sum(q * dq, axis=1, keepdims=True))
            dka = rk * (dk - k * jnp.sum(k * dk, axis=1, keepdims=True))
            buf[s, 0:CHUNK, h * DK : (h + 1) * DK] = dqa * sq * (1.0 + pq * (1.0 - sq))
            buf[s, 0:CHUNK, qw + h * DK : qw + (h + 1) * DK] = dka * sk * (1.0 + pk * (1.0 - sk))
            buf[s, 0:CHUNK, 2 * qw + h * DV : 2 * qw + (h + 1) * DV] = dv * sv * (1.0 + pv * (1.0 - sv))
        dld2 = jnp.concatenate(dlds, axis=1) if heads > 1 else dlds[0]
        dbe2 = jnp.concatenate(dbes, axis=1) if heads > 1 else dbes[0]
        gp_ref[s, :, dw_at : dw_at + 2 * heads] = jnp.concatenate(
            [dld2 * soft * sg[:, :heads], dbe2 * be2 * (1.0 - sg[:, heads:])], axis=1
        ).astype(BF16)
        gdl_ref[...] += jnp.sum(dld2 * ld2, axis=0, keepdims=True)
        raw = proj_ref[s, :, 0:raws]
        draw = None
        for j in range(4):
            shifted = buf[s, 3 - j : 3 - j + CHUNK, :]
            gconv_ref[j] += jnp.sum((raw * shifted).reshape(CHUNK // 8, 8, raws), axis=0)
            term = conv_ref[j : j + 1, :] * shifted
            draw = term if draw is None else draw + term
        gp_ref[s, :, 0:raws] = draw.astype(BF16)
        buf[s, CHUNK : CHUNK + 8, :] = buf[s, 0:8, :]


def mixer_fwd(lengths, proj, conv, dl, gain):
    count = SEQ_LEN // CHUNK
    seqs, _, width = proj.shape
    heads = dl.shape[1]
    raws, vw, n = conv.shape[1], heads * DV, seqs * heads
    full = lambda shape: pl.BlockSpec(shape, lambda c: (0,) * len(shape))
    seq = lambda width: pl.BlockSpec((seqs, CHUNK, width), lambda c: (0, c, 0))
    return pl.pallas_call(
        mix_fwd_kernel,
        grid=(count,),
        in_specs=[
            pl.BlockSpec(memory_space=pltpu.SMEM),
            seq(width),
            full((4, raws)),
            full((1, heads)),
            full((1, DV)),
        ],
        out_specs=[
            seq(vw),
            seq(raws),
            seq(vw),
            seq(vw),
            pl.BlockSpec((n, None, CHUNK, CHUNK), lambda c: (0, c, 0, 0)),
            pl.BlockSpec((n, None, DK, DV), lambda c: (0, c, 0, 0)),
        ],
        out_shape=[
            jax.ShapeDtypeStruct((seqs, SEQ_LEN, vw), BF16),
            jax.ShapeDtypeStruct((seqs, SEQ_LEN, raws), F32),
            jax.ShapeDtypeStruct((seqs, SEQ_LEN, vw), F32),
            jax.ShapeDtypeStruct((seqs, SEQ_LEN, vw), BF16),
            jax.ShapeDtypeStruct((n, count, CHUNK, CHUNK), BF16),
            jax.ShapeDtypeStruct((n, count, DK, DV), BF16),
        ],
        scratch_shapes=[
            pltpu.VMEM((seqs, CHUNK + 8, raws), F32),
            pltpu.VMEM((n, DK, DV), F32),
        ],
        compiler_params=pltpu.CompilerParams(
            dimension_semantics=("arbitrary",), vmem_limit_bytes=48 * 1024 * 1024
        ),
        name="mixer_forward",
    )(lengths, proj, conv, dl, gain)


def mixer_bwd(lengths, proj, conv, dl, gain, gm, pre, o, u, t, s):
    count = SEQ_LEN // CHUNK
    seqs, _, width = proj.shape
    heads = dl.shape[1]
    raws, vw, n = conv.shape[1], heads * DV, seqs * heads
    full = lambda shape: pl.BlockSpec(shape, lambda c: (0,) * len(shape))
    seq = lambda width: pl.BlockSpec((seqs, CHUNK, width), lambda c: (0, count - 1 - c, 0))
    return pl.pallas_call(
        mix_bwd_kernel,
        grid=(count,),
        in_specs=[
            pl.BlockSpec(memory_space=pltpu.SMEM),
            seq(width),
            full((4, raws)),
            full((1, heads)),
            full((1, DV)),
            seq(vw),
            seq(raws),
            seq(vw),
            seq(vw),
            pl.BlockSpec((n, None, CHUNK, CHUNK), lambda c: (0, count - 1 - c, 0, 0)),
            pl.BlockSpec((n, None, DK, DV), lambda c: (0, count - 1 - c, 0, 0)),
        ],
        out_specs=[seq(width), full((4, 8, raws)), full((1, heads)), full((8, DV))],
        out_shape=[
            jax.ShapeDtypeStruct((seqs, SEQ_LEN, width), BF16),
            jax.ShapeDtypeStruct((4, 8, raws), F32),
            jax.ShapeDtypeStruct((1, heads), F32),
            jax.ShapeDtypeStruct((8, DV), F32),
        ],
        scratch_shapes=[
            pltpu.VMEM((seqs, CHUNK + 8, raws), F32),
            pltpu.VMEM((n, DK, DV), F32),
        ],
        compiler_params=pltpu.CompilerParams(
            dimension_semantics=("arbitrary",), vmem_limit_bytes=48 * 1024 * 1024
        ),
        name="mixer_backward",
    )(lengths, proj, conv, dl, gain, gm, pre, o, u, t, s)


def inner_rows(left, right):
    return lax.dot_general(
        left, right, (((0,), (0,)), ((), ())), preferred_element_type=jnp.float32
    )


def outer_cols(left, right):
    return lax.dot_general(
        left, right, (((1,), (1,)), ((), ())), preferred_element_type=jnp.float32
    )


def root_scale(values, gain):
    return values * lax.rsqrt(jnp.mean(values * values, axis=-1, keepdims=True) + 1e-05) * gain


def scatter(values):
    return lax.psum_scatter(
        values.astype(jnp.bfloat16), "head", scatter_dimension=0, tiled=True
    ).astype(jnp.float32)


def gather(values):
    return lax.all_gather(values.astype(jnp.bfloat16), "head", axis=0, tiled=True)


def total(values):
    return lax.psum(values.astype(jnp.bfloat16), "item").astype(jnp.float32)


def local(
    layer_input,
    lengths,
    norm_gain,
    w_query,
    w_key,
    w_value,
    w_outgate,
    w_decay,
    w_write,
    conv_query,
    conv_key,
    conv_value,
    decay_log,
    out_gain,
    w_out,
    ffn_gain,
    w_gate,
    w_up,
    w_down,
    cotangent,
):
    inputs = layer_input.astype(F32)
    normed, norm_pull = jax.vjp(root_scale, inputs, norm_gain.astype(F32))
    group = gather(normed)
    w_all = jnp.concatenate([w_query, w_key, w_value, w_outgate, w_decay, w_write], axis=1)
    conv = jnp.concatenate([conv_query, conv_key, conv_value], axis=1).astype(F32)
    dl = decay_log.reshape(1, -1)
    og = out_gain.astype(F32).reshape(1, DV)
    projected = jnp.dot(group, w_all, preferred_element_type=F32)
    proj = projected.reshape(-1, SEQ_LEN, projected.shape[1])
    mixed, *kept = mixer_fwd(lengths, proj, conv, dl, og)
    mixed = mixed.reshape(group.shape[0], -1)
    attended = scatter(jnp.dot(mixed, w_out, preferred_element_type=F32))
    resid = inputs + attended
    normed_two, ffn_pull = jax.vjp(root_scale, resid, ffn_gain.astype(F32))
    group_two = gather(normed_two)
    units = w_gate.shape[1]
    w_pair = jnp.concatenate([w_gate, w_up], axis=1)
    paired = jnp.dot(group_two, w_pair, preferred_element_type=F32)
    gate = paired[:, :units]
    up = paired[:, units:]
    sigma = jax.nn.sigmoid(gate)
    silu_gate = gate * sigma
    hidden = (silu_gate * up).astype(BF16)
    output = (resid + scatter(jnp.dot(hidden, w_down, preferred_element_type=F32))).astype(BF16)
    grad_rows = gather(cotangent)
    grad_down = inner_rows(hidden, grad_rows)
    grad_hidden = outer_cols(grad_rows, w_down)
    grad_gate = grad_hidden * up * sigma * (1.0 + gate * (1.0 - sigma))
    grad_up = grad_hidden * silu_gate
    grad_pair = jnp.concatenate([grad_gate.astype(BF16), grad_up.astype(BF16)], axis=1)
    grad_w_pair = inner_rows(group_two, grad_pair)
    grad_normed_two = scatter(outer_cols(grad_pair, w_pair))
    grad_resid_part, grad_ffn_gain = ffn_pull(grad_normed_two)
    grad_resid = cotangent.astype(F32) + grad_resid_part
    grad_group = gather(grad_resid)
    grad_w_out = inner_rows(mixed, grad_group)
    grad_mixed = outer_cols(grad_group, w_out).reshape(proj.shape[0], SEQ_LEN, -1)
    grad_proj, gconv, gdl, ggain = mixer_bwd(lengths, proj, conv, dl, og, grad_mixed, *kept)
    grad_proj = grad_proj.reshape(projected.shape)
    gconv = jnp.sum(gconv, axis=1)
    grad_w_all = inner_rows(group, grad_proj)
    grad_normed = scatter(outer_cols(grad_proj, w_all))
    grad_input_part, grad_norm_gain = norm_pull(grad_normed)
    input_grad = grad_resid + grad_input_part
    whole = total(grad_w_all)
    conv_grad = total(gconv)
    pair_grad = total(grad_w_pair)
    gains = lax.psum((grad_norm_gain, jnp.sum(ggain, axis=0), grad_ffn_gain), ("item", "head"))
    edges = [0]
    for weight in (w_query, w_key, w_value, w_outgate, w_decay, w_write):
        edges.append(edges[-1] + weight.shape[1])
    parts = [whole[:, edges[i] : edges[i + 1]] for i in range(6)]
    return (
        output,
        input_grad,
        gains[0],
        *parts,
        conv_grad[:, : edges[1]],
        conv_grad[:, edges[1] : edges[2]],
        conv_grad[:, edges[2] :],
        total(gdl[0]),
        gains[1],
        total(grad_w_out),
        gains[2],
        pair_grad[:, :units],
        pair_grad[:, units:],
        total(grad_down),
    )


def solution(mesh):
    rows = P(("item", "head"), None)
    cols = P(None, "head")
    deep = P("head", None)
    return jax.shard_map(
        local,
        mesh=mesh,
        in_specs=(rows, P("item"), P(), *[cols] * 9, P("head"), P(), deep, P(), cols, cols, deep, rows),
        out_specs=(rows, rows, P(), *[cols] * 9, P("head"), P(), deep, P(), cols, cols, deep),
        check_vma=False,
    )
```

```python
import functools

import jax
import jax.numpy as jnp
from jax import lax
from jax.experimental import pallas as pl
from jax.experimental.pallas import tpu as pltpu
from jax.sharding import PartitionSpec as P

DK = 128
DV = 256
SEQ_LEN = 1024
CHUNK = 128
F32 = jnp.float32
BF16 = jnp.bfloat16


def mm(left, right, ta=False, tb=False):
    return lax.dot_general(
        left.astype(BF16),
        right.astype(BF16),
        (((0 if ta else 1,), (1 if tb else 0,)), ((), ())),
        preferred_element_type=F32,
    )


def split(value):
    high = value.astype(BF16)
    return high, (value - high.astype(F32)).astype(BF16)


def mm3(left, right):
    lh, ll = left
    rh, rl = right
    return mm(lh, rh) + (mm(lh, rl) + mm(ll, rh))


def sigmoid(x):
    return 1.0 / (1.0 + jnp.exp(-x))


def grids():
    rows = lax.broadcasted_iota(jnp.int32, (CHUNK, CHUNK), 0)
    cols = lax.broadcasted_iota(jnp.int32, (CHUNK, CHUNK), 1)
    return rows, cols


def to_row(col, eye):
    return jnp.sum(jnp.where(eye, col, 0.0), axis=0, keepdims=True)


def inverses(mats, rows, cols):
    eye = jnp.where(rows == cols, 1.0, 0.0)
    near = rows // 16 == cols // 16
    n1 = [jnp.where(near, -a, 0.0) for a in mats]
    n1s = [split(n) for n in n1]
    n2 = [mm3(n, n) for n in n1s]
    n2s = [split(n) for n in n2]
    n3 = [mm3(a, b) for a, b in zip(n1s, n2s)]
    n4s = [split(mm3(n, n)) for n in n2s]
    p1 = [eye + a + b + c for a, b, c in zip(n1, n2, n3)]
    p2 = [p + mm3(split(p), n) for p, n in zip(p1, n4s)]
    n8s = [split(mm3(n, n)) for n in n4s]
    x = [p + mm3(split(p), n) for p, n in zip(p2, n8s)]
    size = 16
    while size < CHUNK:
        pair = (rows // (2 * size) == cols // (2 * size)) & (rows // size != cols // size)
        xs = [split(v) for v in x]
        b = [split(jnp.where(pair, a, 0.0)) for a in mats]
        bx = [split(mm3(u, v)) for u, v in zip(b, xs)]
        x = [v - mm3(vs, w) for v, vs, w in zip(x, xs, bx)]
        size *= 2
    return x


def lead(ref):
    return ref[...].astype(F32)


def decays(ld, eye, causal):
    row = to_row(ld, eye)
    g = jnp.sum(jnp.where(causal, row, 0.0), axis=1, keepdims=True)
    grow = to_row(g, eye)
    d = jnp.where(causal, jnp.exp(jnp.where(causal, g - grow, 0.0)), 0.0)
    last = g[CHUNK - 1 : CHUNK, :]
    return d, jnp.exp(g), jnp.exp(last - g), jnp.exp(last)


def live_mask(len_ref, s, c):
    spot = lax.broadcasted_iota(jnp.int32, (CHUNK, 1), 0) + c * CHUNK
    return jnp.where(spot < len_ref[s], 1.0, 0.0)


def softplus(x):
    return jnp.maximum(x, 0.0) + jnp.log1p(jnp.exp(-jnp.abs(x)))


def mix_fwd_kernel(
    len_ref, q_ref, k_ref, v_ref, g_ref, dw_ref, conv_ref, dl_ref, gain_ref,
    mixed_ref, pre_ref, o_ref, u_ref, t_ref, s_ref, buf, state,
):
    c = pl.program_id(0)
    seqs, _, raws = buf.shape
    heads = dl_ref.shape[1]
    qw = heads * DK
    pieces = ((q_ref, 0, qw), (k_ref, qw, 2 * qw), (v_ref, 2 * qw, raws))

    @pl.when(c == 0)
    def _():
        buf[:, 0:8, :] = jnp.zeros((seqs, 8, raws), F32)
        state[...] = jnp.zeros_like(state)

    rows, cols = grids()
    eye = rows == cols
    causal = rows >= cols
    lower = rows > cols
    rate = jnp.exp(dl_ref[...])
    st = []
    for s in range(seqs):
        for ref, a, b in pieces:
            buf[s, 8 : 8 + CHUNK, a:b] = ref[s]
        pre = conv_ref[0:1, :] * buf[s, 5 : 5 + CHUNK, :]
        for j in range(1, 4):
            pre = pre + conv_ref[j : j + 1, :] * buf[s, 5 + j : 5 + j + CHUNK, :]
        pre_ref[s] = pre
        buf[s, 0:8, :] = buf[s, CHUNK : CHUNK + 8, :]
        act = pre * sigmoid(pre)
        mask = live_mask(len_ref, s, c)
        x = dw_ref[s]
        ld2 = -rate * softplus(x[:, :heads]) * mask
        be2 = sigmoid(x[:, heads:]) * mask
        for h in range(heads):
            q = act[:, h * DK : (h + 1) * DK]
            k = act[:, qw + h * DK : qw + (h + 1) * DK]
            v = act[:, 2 * qw + h * DV : 2 * qw + (h + 1) * DV]
            q = q * (lax.rsqrt(jnp.sum(q * q, axis=1, keepdims=True) + 1e-06) * DK ** (-0.5))
            k = k * lax.rsqrt(jnp.sum(k * k, axis=1, keepdims=True) + 1e-06)
            be = be2[:, h : h + 1]
            d, ga, e, el = decays(ld2[:, h : h + 1], eye, causal)
            qb = q.astype(BF16)
            kb = k.astype(BF16)
            qk = jnp.concatenate([qb, kb], axis=0)
            both = mm(qk, kb, tb=True)
            w = d * both[:CHUNK]
            a = jnp.where(lower, d * both[CHUNK:], 0.0) * be
            st.append((s, h, mask, v, be, ga, e, el, qk, kb, w, a))
    inv = inverses([z[-1] for z in st], rows, cols)
    for i, (s, h, mask, v, be, ga, e, el, qk, kb, w, a) in enumerate(st):
        t = inv[i].astype(BF16)
        old = state[i]
        oldb = old.astype(BF16)
        s_ref[i] = oldb
        t_ref[i] = t
        qks = mm(qk, oldb)
        r = be * (v - ga * qks[CHUNK:])
        u = mm(t, r)
        ub = u.astype(BF16)
        u_ref[s, :, h * DV : (h + 1) * DV] = ub
        o = ga * qks[:CHUNK] + mm(w, ub)
        state[i] = el * old + mm(kb, e * u, ta=True)
        o = o * mask
        o_ref[s, :, h * DV : (h + 1) * DV] = o
        rg = g_ref[s, :, h * DV : (h + 1) * DV]
        n = o * lax.rsqrt(jnp.mean(o * o, axis=1, keepdims=True) + 1e-05) * gain_ref[...]
        mixed_ref[s, :, h * DV : (h + 1) * DV] = (n * (rg * sigmoid(rg))).astype(BF16)


def mix_bwd_kernel(
    len_ref, q_ref, k_ref, v_ref, g_ref, dw_ref, conv_ref, dl_ref, gain_ref,
    gm_ref, pre_ref, o_ref, u_ref, t_ref, s_ref,
    gq_ref, gk_ref, gv_ref, gg_ref, gdw_ref, gconv_ref, gdl_ref, ggain_ref, buf, dstate,
):
    step = pl.program_id(0)
    c = pl.num_programs(0) - 1 - step
    seqs, _, raws = buf.shape
    heads = dl_ref.shape[1]
    qw = heads * DK
    pieces = ((q_ref, 0, qw), (k_ref, qw, 2 * qw), (v_ref, 2 * qw, raws))

    @pl.when(step == 0)
    def _():
        buf[:, CHUNK : CHUNK + 8, :] = jnp.zeros((seqs, 8, raws), F32)
        dstate[...] = jnp.zeros_like(dstate)
        gconv_ref[...] = jnp.zeros_like(gconv_ref)
        gdl_ref[...] = jnp.zeros_like(gdl_ref)
        ggain_ref[...] = jnp.zeros_like(ggain_ref)

    rows, cols = grids()
    eye = rows == cols
    causal = rows >= cols
    lower = rows > cols
    later = rows <= cols
    rate = jnp.exp(dl_ref[...])
    gain = gain_ref[...]
    for s in range(seqs):
        mask = live_mask(len_ref, s, c)
        x = dw_ref[s]
        soft = -rate * mask
        ld2 = soft * softplus(x[:, :heads])
        sg = sigmoid(x)
        be2 = sg[:, heads:] * mask
        dlds = []
        dbes = []
        for h in range(heads):
            i = heads * s + h
            vs = slice(h * DV, (h + 1) * DV)
            gm = gm_ref[s, :, vs]
            o = o_ref[s, :, vs]
            rg = g_ref[s, :, h * DV : (h + 1) * DV]
            sr = sigmoid(rg)
            r = lax.rsqrt(jnp.mean(o * o, axis=1, keepdims=True) + 1e-05)
            un = o * r
            gsg = gm * sr
            gg_ref[s, :, h * DV : (h + 1) * DV] = (
                gsg * (un * gain) * (1.0 + rg * (1.0 - sr))
            ).astype(BF16)
            dn = gsg * rg
            dnu = dn * un
            ggain_ref[...] += jnp.sum(dnu.reshape(CHUNK // 8, 8, DV), axis=0)
            do = (r * mask) * (dn * gain - un * jnp.mean(dnu * gain, axis=1, keepdims=True))
            pq = pre_ref[s, :, h * DK : (h + 1) * DK]
            pk = pre_ref[s, :, qw + h * DK : qw + (h + 1) * DK]
            pv = pre_ref[s, :, 2 * qw + h * DV : 2 * qw + (h + 1) * DV]
            sq = sigmoid(pq)
            sk = sigmoid(pk)
            sv = sigmoid(pv)
            q = pq * sq
            k = pk * sk
            v = pv * sv
            rq = lax.rsqrt(jnp.sum(q * q, axis=1, keepdims=True) + 1e-06)
            rk = lax.rsqrt(jnp.sum(k * k, axis=1, keepdims=True) + 1e-06)
            q = q * rq
            k = k * rk
            scale = DK ** (-0.5)
            be = be2[:, h : h + 1]
            d, ga, e, el = decays(ld2[:, h : h + 1], eye, causal)
            qb = (q * scale).astype(BF16)
            kb = k.astype(BF16)
            qk = jnp.concatenate([qb, kb], axis=0)
            both = mm(qk, kb, tb=True)
            w = d * both[:CHUNK]
            ab = jnp.where(lower, d * both[CHUNK:], 0.0)
            a = ab * be
            t = t_ref[i]
            st = s_ref[i]
            u = u_ref[s, :, vs]
            dh = dstate[i]
            dhb = dh.astype(BF16)
            qks = mm(qk, st)
            dob = do.astype(BF16)
            kdh = e * mm(kb, dhb)
            ubar = mm(w, dob, ta=True) + kdh
            rbar = mm(t, ubar, ta=True)
            rb = rbar.astype(BF16)
            uu = mm(jnp.concatenate([dob, rb], axis=0), u, tb=True)
            wbar = jnp.where(causal, uu[:CHUNK], 0.0)
            abar = -jnp.where(lower, uu[CHUNK:], 0.0)
            gks = ga * qks[CHUNK:]
            dv = be * rbar
            y = -ga * dv
            z = ga * do
            zy = jnp.concatenate([z.astype(BF16), y.astype(BF16)], axis=0)
            zys = mm(zy, st, tb=True)
            p = (wbar * d).astype(BF16)
            m = abar * d * be
            eu = e * u.astype(F32)
            dq = zys[:CHUNK] + mm(p, kb)
            dk = (
                zys[CHUNK:]
                + mm(p, qb, ta=True)
                + mm(m, kb)
                + mm(m, kb, ta=True)
                + mm(eu, dhb, tb=True)
            )
            dstate[i] = el * dh + mm(qk, zy, ta=True)
            ee = wbar * w + abar * a
            f = jnp.sum(u.astype(F32) * kdh, axis=1, keepdims=True)
            dbe = jnp.sum(rbar * (v - gks), axis=1, keepdims=True) + jnp.sum(
                abar * ab, axis=1, keepdims=True
            )
            dgc = (
                jnp.sum(ee, axis=1, keepdims=True)
                + jnp.sum(z * qks[:CHUNK] - dv * gks, axis=1, keepdims=True)
                - f
            )
            dgr = to_row(dgc, eye) - jnp.sum(ee, axis=0, keepdims=True)
            total = jnp.sum(f, axis=0, keepdims=True) + el * jnp.sum(
                jnp.sum(st.astype(F32) * dh, axis=1, keepdims=True), axis=0, keepdims=True
            )
            dld = jnp.sum(jnp.where(later, dgr, 0.0), axis=1, keepdims=True) + total
            dlds.append(dld)
            dbes.append(dbe)
            dq = dq * scale
            dqa = rq * (dq - q * jnp.sum(q * dq, axis=1, keepdims=True))
            dka = rk * (dk - k * jnp.sum(k * dk, axis=1, keepdims=True))
            buf[s, 0:CHUNK, h * DK : (h + 1) * DK] = dqa * sq * (1.0 + pq * (1.0 - sq))
            buf[s, 0:CHUNK, qw + h * DK : qw + (h + 1) * DK] = dka * sk * (1.0 + pk * (1.0 - sk))
            buf[s, 0:CHUNK, 2 * qw + h * DV : 2 * qw + (h + 1) * DV] = dv * sv * (1.0 + pv * (1.0 - sv))
        dld2 = jnp.concatenate(dlds, axis=1) if heads > 1 else dlds[0]
        dbe2 = jnp.concatenate(dbes, axis=1) if heads > 1 else dbes[0]
        gdw_ref[s] = jnp.concatenate(
            [dld2 * soft * sg[:, :heads], dbe2 * be2 * (1.0 - sg[:, heads:])], axis=1
        ).astype(BF16)
        gdl_ref[...] += jnp.sum(dld2 * ld2, axis=0, keepdims=True)
        for (ref, a, b), out in zip(pieces, (gq_ref, gk_ref, gv_ref)):
            raw = ref[s]
            draw = None
            for j in range(4):
                shifted = buf[s, 3 - j : 3 - j + CHUNK, a:b]
                gconv_ref[j, :, a:b] += jnp.sum(
                    (raw * shifted).reshape(CHUNK // 8, 8, b - a), axis=0
                )
                term = conv_ref[j : j + 1, a:b] * shifted
                draw = term if draw is None else draw + term
            out[s] = draw.astype(BF16)
        buf[s, CHUNK : CHUNK + 8, :] = buf[s, 0:8, :]


def mixer_fwd(lengths, q, k, v, g, dw, conv, dl, gain):
    count = SEQ_LEN // CHUNK
    seqs = q.shape[0]
    heads = dl.shape[1]
    raws, vw, n = conv.shape[1], heads * DV, seqs * heads
    full = lambda shape: pl.BlockSpec(shape, lambda c: (0,) * len(shape))
    seq = lambda width: pl.BlockSpec((seqs, CHUNK, width), lambda c: (0, c, 0))
    return pl.pallas_call(
        mix_fwd_kernel,
        grid=(count,),
        in_specs=[
            pl.BlockSpec(memory_space=pltpu.SMEM),
            seq(q.shape[2]),
            seq(k.shape[2]),
            seq(vw),
            seq(vw),
            seq(2 * heads),
            full((4, raws)),
            full((1, heads)),
            full((1, DV)),
        ],
        out_specs=[
            seq(vw),
            seq(raws),
            seq(vw),
            seq(vw),
            pl.BlockSpec((n, None, CHUNK, CHUNK), lambda c: (0, c, 0, 0)),
            pl.BlockSpec((n, None, DK, DV), lambda c: (0, c, 0, 0)),
        ],
        out_shape=[
            jax.ShapeDtypeStruct((seqs, SEQ_LEN, vw), BF16),
            jax.ShapeDtypeStruct((seqs, SEQ_LEN, raws), F32),
            jax.ShapeDtypeStruct((seqs, SEQ_LEN, vw), F32),
            jax.ShapeDtypeStruct((seqs, SEQ_LEN, vw), BF16),
            jax.ShapeDtypeStruct((n, count, CHUNK, CHUNK), BF16),
            jax.ShapeDtypeStruct((n, count, DK, DV), BF16),
        ],
        scratch_shapes=[
            pltpu.VMEM((seqs, CHUNK + 8, raws), F32),
            pltpu.VMEM((n, DK, DV), F32),
        ],
        compiler_params=pltpu.CompilerParams(
            dimension_semantics=("arbitrary",), vmem_limit_bytes=48 * 1024 * 1024
        ),
        name="mixer_forward",
    )(lengths, q, k, v, g, dw, conv, dl, gain)


def mixer_bwd(lengths, q, k, v, g, dw, conv, dl, gain, gm, pre, o, u, t, s):
    count = SEQ_LEN // CHUNK
    seqs = q.shape[0]
    heads = dl.shape[1]
    raws, vw, n = conv.shape[1], heads * DV, seqs * heads
    full = lambda shape: pl.BlockSpec(shape, lambda c: (0,) * len(shape))
    seq = lambda width: pl.BlockSpec((seqs, CHUNK, width), lambda c: (0, count - 1 - c, 0))
    return pl.pallas_call(
        mix_bwd_kernel,
        grid=(count,),
        in_specs=[
            pl.BlockSpec(memory_space=pltpu.SMEM),
            seq(q.shape[2]),
            seq(k.shape[2]),
            seq(vw),
            seq(vw),
            seq(2 * heads),
            full((4, raws)),
            full((1, heads)),
            full((1, DV)),
            seq(vw),
            seq(raws),
            seq(vw),
            seq(vw),
            pl.BlockSpec((n, None, CHUNK, CHUNK), lambda c: (0, count - 1 - c, 0, 0)),
            pl.BlockSpec((n, None, DK, DV), lambda c: (0, count - 1 - c, 0, 0)),
        ],
        out_specs=[
            seq(q.shape[2]),
            seq(k.shape[2]),
            seq(vw),
            seq(vw),
            seq(2 * heads),
            full((4, 8, raws)), full((1, heads)),
            full((8, DV)),
        ],
        out_shape=[
            jax.ShapeDtypeStruct(q.shape, BF16),
            jax.ShapeDtypeStruct(k.shape, BF16),
            jax.ShapeDtypeStruct(v.shape, BF16),
            jax.ShapeDtypeStruct(g.shape, BF16),
            jax.ShapeDtypeStruct(dw.shape, BF16),
            jax.ShapeDtypeStruct((4, 8, raws), F32),
            jax.ShapeDtypeStruct((1, heads), F32),
            jax.ShapeDtypeStruct((8, DV), F32),
        ],
        scratch_shapes=[
            pltpu.VMEM((seqs, CHUNK + 8, raws), F32),
            pltpu.VMEM((n, DK, DV), F32),
        ],
        compiler_params=pltpu.CompilerParams(
            dimension_semantics=("arbitrary",), vmem_limit_bytes=48 * 1024 * 1024
        ),
        name="mixer_backward",
    )(lengths, q, k, v, g, dw, conv, dl, gain, gm, pre, o, u, t, s)


MESH = pl.DeviceIdType.MESH


class Place:
    def __init__(self, blocks):
        head = lax.axis_index("head")
        self.n = blocks // 2
        self.me = head
        self.z = head // 2
        self.c = head % 2
        self.mate = 2 * self.z + 1 - self.c
        self.right = head + 2
        self.left = head - 2
        self.has_right = self.z < self.n - 1
        self.has_left = self.z > 0

    def greet(self):
        barrier = pltpu.get_barrier_semaphore()

        def hello(device):
            pl.semaphore_signal(barrier, inc=1, device_id={"head": device}, device_id_type=MESH)

        hello(self.mate)
        pl.when(self.has_right)(lambda: hello(self.right))
        pl.when(self.has_left)(lambda: hello(self.left))
        n = self.n
        pl.semaphore_wait(barrier, 1 + (self.z + n - 1) // n + (2 * n - 2 - self.z) // n)


def remote(src, dst, send, recv, device):
    return pltpu.make_async_remote_copy(
        src_ref=src,
        dst_ref=dst,
        send_sem=send,
        recv_sem=recv,
        device_id={"head": device},
        device_id_type=MESH,
    )


class Scatter:
    def __init__(self, place, own, stage, cross, line, xs, xr, ls, lr):
        self.p = place
        self.own, self.stage, self.cross, self.line = own, stage, cross, line
        self.xs, self.xr, self.ls, self.lr = xs, xr, ls, lr

    def swap(self, q):
        return remote(
            self.stage.at[q % 2], self.cross.at[q], self.xs.at[q], self.xr.at[q], self.p.mate
        )

    def hop(self, q, slot, device):
        ref = self.line.at[q, slot]
        return remote(ref, ref, self.ls.at[q, slot], self.lr.at[q, slot], device)

    def share(self, q, t):
        return self.own[q % 2, t].astype(F32) + self.cross[q, t].astype(F32)

    def pass_on(self, q, t, slot, first, device):
        @pl.when(first)
        def _():
            self.line[q, slot] = self.share(q, t).astype(BF16)

        @pl.when(jnp.logical_not(first))
        def _():
            self.hop(q, slot, device).wait_recv()
            self.line[q, slot] = (self.share(q, t) + self.line[q, slot].astype(F32)).astype(BF16)

        self.hop(q, slot, device).start()

    def right_at(self, s):
        return self.p.n - 1 - s + self.p.z

    def left_at(self, s):
        n = self.p.n
        t = s + 1 - n + self.p.z
        return t, (t + n) % (n + 1)

    def step(self, q, s):
        p = self.p

        @pl.when(p.z <= s)
        def _():
            t = self.right_at(s)
            self.pass_on(q, t, t, p.z == 0, p.right)

        @pl.when(p.n - 1 - p.z <= s)
        def _():
            t, slot = self.left_at(s)
            self.pass_on(q, t, slot, p.z == p.n - 1, p.left)

    def result(self, q, total):
        p = self.p
        total[...] = self.share(q, p.z)

        @pl.when(p.has_left)
        def _():
            self.hop(q, p.z, p.right).wait_recv()
            total[...] += self.line[q, p.z].astype(F32)

        @pl.when(p.has_right)
        def _():
            slot = (p.z + p.n) % (p.n + 1)
            self.hop(q, slot, p.left).wait_recv()
            total[...] += self.line[q, slot].astype(F32)

    def drain(self, q):
        p = self.p
        for s in range(p.n - 1):

            @pl.when(p.z <= s)
            def _():
                self.hop(q, self.right_at(s), p.right).wait_send()

            @pl.when(p.n - 1 - p.z <= s)
            def _():
                self.hop(q, self.left_at(s)[1], p.left).wait_send()


class Gather:
    def __init__(self, place, held, ss, rr):
        self.p, self.held, self.ss, self.rr = place, held, ss, rr

    def copy(self, q, kind, z):
        p = self.p
        block = 2 * z + p.c
        ref = self.held.at[q, block]
        device = (p.right, p.left, p.mate)[kind]
        return remote(ref, ref, self.ss.at[q, kind, z], self.rr.at[q, block], device)

    def step(self, q, s):
        p = self.p
        if s == 0:
            pl.when(p.has_right)(lambda: self.copy(q, 0, p.z).start())
            pl.when(p.has_left)(lambda: self.copy(q, 1, p.z).start())
            self.copy(q, 2, p.z).start()
            return

        @pl.when(p.z >= s)
        def _():
            z = p.z - s
            self.copy(q, 0, z).wait_recv()
            pl.when(p.has_right)(lambda: self.copy(q, 0, z).start())
            self.copy(q, 2, z).start()

        @pl.when(p.z + s <= p.n - 1)
        def _():
            z = p.z + s
            self.copy(q, 1, z).wait_recv()
            pl.when(p.has_left)(lambda: self.copy(q, 1, z).start())
            self.copy(q, 2, z).start()

    def finish(self, q):
        p = self.p
        for z in range(p.n):
            block = 2 * z + 1 - p.c
            ref = self.held.at[q, block]
            remote(ref, ref, self.ss.at[q, 2, z], self.rr.at[q, block], p.mate).wait_recv()

    def drain(self, q):
        p = self.p
        for z in range(p.n):
            self.copy(q, 2, z).wait_send()

            @pl.when(jnp.logical_and(p.has_right, p.z >= z))
            def _():
                self.copy(q, 0, z).wait_send()

            @pl.when(jnp.logical_and(p.has_left, p.z <= z))
            def _():
                self.copy(q, 1, z).wait_send()


def lane_tiles(width, size=256):
    return [(at, min(at + size, width)) for at in range(0, width, size)]


def put_share(place, own, stage, q, values, a, b):
    _, n, rows, _ = own.shape
    parts = values.reshape(n, 2, rows, b - a)

    @pl.when(place.c == 0)
    def _():
        own[q % 2, :, :, a:b] = parts[:, 0]
        stage[q % 2, :, :, a:b] = parts[:, 1].astype(BF16)

    @pl.when(place.c == 1)
    def _():
        own[q % 2, :, :, a:b] = parts[:, 1]
        stage[q % 2, :, :, a:b] = parts[:, 0].astype(BF16)


def ring_scratch(chunks, blocks, rows, depth):
    n = blocks // 2
    dma = pltpu.SemaphoreType.DMA
    return [
        pltpu.VMEM((2, n, rows, depth), F32),
        pltpu.VMEM((2, n, rows, depth), BF16),
        pltpu.VMEM((chunks, n, rows, depth), BF16),
        pltpu.VMEM((chunks, n + 1, rows, depth), BF16),
        dma((chunks,)),
        dma((chunks,)),
        dma((chunks, n + 1)),
        dma((chunks, n + 1)),
    ]


def gather_scratch(chunks, blocks, rows, depth):
    dma = pltpu.SemaphoreType.DMA
    return [
        pltpu.VMEM((chunks, blocks, rows, depth), BF16),
        dma((chunks, 3, blocks // 2)),
        dma((chunks, blocks)),
    ]


def lockstep(chunks, n, scatter, gather, partial, middle, consume):
    partial(0)
    scatter.swap(0).start()

    def turn(r, _):
        summing = r < chunks
        passing = jnp.logical_and(r >= 1, r <= chunks)

        @pl.when(passing)
        def _():
            gather.step(r - 1, 0)

        @pl.when(summing)
        def _():
            scatter.swap(r).wait_recv()
            scatter.step(r, 0)

        @pl.when(r + 1 < chunks)
        def _():
            @pl.when(r >= 1)
            def _():
                scatter.swap(r - 1).wait_send()

            partial(r + 1)
            scatter.swap(r + 1).start()

        for s in range(1, n):

            @pl.when(passing)
            def _():
                gather.step(r - 1, s)

            if s < n - 1:

                @pl.when(summing)
                def _():
                    scatter.step(r, s)

            if s <= 2:

                @pl.when(r >= 2)
                def _():
                    consume(r - 2, s - 1)

        @pl.when(summing)
        def _():
            middle(r)

        @pl.when(passing)
        def _():
            gather.finish(r - 1)

        return 0

    lax.fori_loop(0, chunks + 2, turn, 0)
    for q in range(max(chunks - 2, 0), chunks):
        scatter.swap(q).wait_send()

    def drain(q, _):
        scatter.drain(q)
        gather.drain(q)
        return 0

    lax.fori_loop(0, chunks, drain, 0)


def ffn_kernel(
    mixed_ref, w_out_ref, input_ref, gain_ref, w_gate_hbm, w_up_hbm, w_down_hbm, cot_hbm,
    resid_ref, group_hbm, hidden_hbm, dgate_hbm, dup_hbm, down_hbm,
    own, stage, cross, line, xs, xr, ls, lr, held, gs, gr,
    w_gate, w_up, w_down, cot, hid, dg, du, down, total, wsem, csem, osem,
):
    chunks, blocks, rows, depth = held.shape
    units = w_gate.shape[0]
    p = Place(blocks)
    scatter = Scatter(p, own, stage, cross, line, xs, xr, ls, lr)
    gather = Gather(p, held, gs, gr)
    loads = [
        pltpu.make_async_copy(src, dst, wsem.at[i])
        for i, (src, dst) in enumerate(
            ((w_gate_hbm, w_gate), (w_up_hbm, w_up), (w_down_hbm, w_down))
        )
    ]
    for load in loads:
        load.start()
    cot_load = lambda q: pltpu.make_async_copy(cot_hbm.at[:, q], cot.at[q % 2], csem.at[q % 2])
    cot_load(0).start()
    p.greet()

    def partial(q):
        x = mixed_ref[:, q].reshape(blocks * rows, -1)
        for a, b in lane_tiles(depth, 512):
            put_share(
                p, own, stage, q, jnp.dot(x, w_out_ref[:, a:b], preferred_element_type=F32), a, b
            )

    def middle(q):
        scatter.result(q, total)
        here = pl.ds(pl.multiple_of(q * rows, rows), rows)
        resid = input_ref[here, :].astype(F32) + total[...]
        resid_ref[here, :] = resid
        normed = resid * lax.rsqrt(jnp.mean(resid * resid, axis=1, keepdims=True) + 1e-05)
        held[q, p.me] = (normed * gain_ref[...]).astype(BF16)

    half = blocks // 2

    def saves(q):
        slot = q % 2
        return [
            pltpu.make_async_copy(src.at[slot], dst.at[:, q], osem.at[slot, i])
            for i, (src, dst) in enumerate(((hid, hidden_hbm), (dg, dgate_hbm), (du, dup_hbm)))
        ] + [pltpu.make_async_copy(held.at[q], group_hbm.at[:, q], osem.at[slot, 3])]

    def down_save(q, i):
        return pltpu.make_async_copy(
            down.at[i], down_hbm.at[pl.ds(i * half, half), q], osem.at[i, 4]
        )

    def consume(q, i):
        slot = q % 2
        if i == 0:

            @pl.when(q == 0)
            def _():
                for load in loads:
                    load.wait()

            cot_load(q).wait()

            @pl.when(q + 1 < chunks)
            def _():
                cot_load(q + 1).start()

            @pl.when(q >= 2)
            def _():
                for save in saves(q - 2):
                    save.wait()

        at = slice(i * half, (i + 1) * half)
        x = held[q, at].reshape(half * rows, depth)
        g = cot[slot, at].reshape(half * rows, depth)
        for a, b in lane_tiles(units):
            gate = mm(x, w_gate[a:b, :], tb=True)
            up = mm(x, w_up[a:b, :], tb=True)
            gh = mm(g, w_down[a:b, :], tb=True)
            sg = sigmoid(gate)
            act = gate * sg
            shape = (half, rows, b - a)
            hid[slot, at, :, a:b] = (act * up).astype(BF16).reshape(shape)
            dg[slot, at, :, a:b] = (
                (gh * up * sg * (1.0 + gate * (1.0 - sg))).astype(BF16).reshape(shape)
            )
            du[slot, at, :, a:b] = (gh * act).astype(BF16).reshape(shape)

        @pl.when(q >= 1)
        def _():
            down_save(q - 1, i).wait()

        h = hid[slot, at].reshape(half * rows, units)
        for a, b in lane_tiles(depth, 512):
            down[i, :, :, a:b] = (
                jnp.dot(h, w_down[:, a:b], preferred_element_type=F32)
                .astype(BF16)
                .reshape(half, rows, b - a)
            )
        down_save(q, i).start()
        if i == 1:
            for save in saves(q):
                save.start()

    lockstep(chunks, p.n, scatter, gather, partial, middle, consume)
    for i in range(2):
        down_save(chunks - 1, i).wait()
    for q in range(max(chunks - 2, 0), chunks):
        for save in saves(q):
            save.wait()


def chunk_rows(blocks, owned):
    return min(owned, max(16, 4096 // (blocks * blocks)))


ANY = pl.BlockSpec(memory_space=pl.ANY)
WHOLE = pl.BlockSpec(memory_space=pltpu.VMEM)


def ffn(mixed, w_out, inputs, gain, w_gate, w_up, w_down, cot):
    owned, depth = inputs.shape
    blocks = mixed.shape[0] // owned
    rows = chunk_rows(blocks, owned)
    chunks = owned // rows
    units = w_gate.shape[0]
    cut = lambda width: jax.ShapeDtypeStruct((blocks, chunks, rows, width), BF16)
    dma = pltpu.SemaphoreType.DMA
    return pl.pallas_call(
        ffn_kernel,
        in_specs=[WHOLE] * 4 + [ANY] * 4,
        out_specs=[WHOLE] + [ANY] * 5,
        out_shape=[
            jax.ShapeDtypeStruct((owned, depth), F32),
            cut(depth),
            cut(units),
            cut(units),
            cut(units),
            cut(depth),
        ],
        scratch_shapes=ring_scratch(chunks, blocks, rows, depth)
        + gather_scratch(chunks, blocks, rows, depth)
        + [
            pltpu.VMEM(w_gate.shape, BF16),
            pltpu.VMEM(w_up.shape, BF16),
            pltpu.VMEM(w_down.shape, BF16),
            pltpu.VMEM((2, blocks, rows, depth), BF16),
            pltpu.VMEM((2, blocks, rows, units), BF16),
            pltpu.VMEM((2, blocks, rows, units), BF16),
            pltpu.VMEM((2, blocks, rows, units), BF16),
            pltpu.VMEM((2, blocks // 2, rows, depth), BF16),
            pltpu.VMEM((rows, depth), F32),
            dma((3,)),
            dma((2,)),
            dma((2, 5)),
        ],
        compiler_params=pltpu.CompilerParams(
            collective_id=1, has_side_effects=True, vmem_limit_bytes=60 * 1024 * 1024
        ),
        name="ffn_rounds",
    )(
        mixed.reshape(blocks, chunks, rows, -1),
        w_out,
        inputs,
        gain,
        w_gate,
        w_up,
        w_down,
        cot.reshape(blocks, chunks, rows, depth),
    )


def back_kernel(
    dgate_ref, dup_ref, w_gate_ref, w_up_ref, resid_ref, gain_ref, cot_ref, w_out_ref,
    gres_ref, ggain_ref, group_hbm, gm_hbm,
    own, stage, cross, line, xs, xr, ls, lr, held, gs, gr, gm, total, osem,
):
    chunks, blocks, rows, depth = held.shape
    p = Place(blocks)
    scatter = Scatter(p, own, stage, cross, line, xs, xr, ls, lr)
    gather = Gather(p, held, gs, gr)
    p.greet()
    ggain_ref[...] = jnp.zeros_like(ggain_ref)

    def partial(q):
        g = dgate_ref[:, q].reshape(blocks * rows, -1)
        u = dup_ref[:, q].reshape(blocks * rows, -1)
        for a, b in lane_tiles(depth, 512):
            put_share(
                p,
                own,
                stage,
                q,
                mm(g, w_gate_ref[:, a:b]) + mm(u, w_up_ref[:, a:b]),
                a,
                b,
            )

    def middle(q):
        scatter.result(q, total)
        here = pl.ds(pl.multiple_of(q * rows, rows), rows)
        resid = resid_ref[here, :]
        n = lax.rsqrt(jnp.mean(resid * resid, axis=1, keepdims=True) + 1e-05)
        u = resid * n
        grad = total[...]
        ggain_ref[...] += jnp.sum((grad * u).reshape(rows // 8, 8, depth), axis=0)
        e = grad * gain_ref[...]
        gres = cot_ref[here, :].astype(F32) + n * (e - u * jnp.mean(e * u, axis=1, keepdims=True))
        gres_ref[here, :] = gres
        held[q, p.me] = gres.astype(BF16)

    half = blocks // 2

    def saves(q, i):
        at = pl.ds(i * half, half)
        return [
            pltpu.make_async_copy(gm.at[i], gm_hbm.at[at, q], osem.at[i, 0]),
            pltpu.make_async_copy(held.at[q, at], group_hbm.at[at, q], osem.at[i, 1]),
        ]

    def consume(q, i):
        @pl.when(q >= 1)
        def _():
            for save in saves(q - 1, i):
                save.wait()

        x = held[q, i * half : (i + 1) * half].reshape(half * rows, depth)
        gm[i] = mm(x, w_out_ref[...], tb=True).reshape(half, rows, -1)
        for save in saves(q, i):
            save.start()

    lockstep(chunks, p.n, scatter, gather, partial, middle, consume)
    for i in range(2):
        for save in saves(chunks - 1, i):
            save.wait()


def back(dgate, dup, w_gate, w_up, resid, gain, cot, w_out):
    blocks, chunks, rows, _ = dgate.shape
    owned, depth = resid.shape
    width = w_out.shape[0]
    dma = pltpu.SemaphoreType.DMA
    return pl.pallas_call(
        back_kernel,
        in_specs=[WHOLE] * 8,
        out_specs=[WHOLE, WHOLE, ANY, ANY],
        out_shape=[
            jax.ShapeDtypeStruct((owned, depth), F32),
            jax.ShapeDtypeStruct((8, depth), F32),
            jax.ShapeDtypeStruct((blocks, chunks, rows, depth), BF16),
            jax.ShapeDtypeStruct((blocks, chunks, rows, width), F32),
        ],
        scratch_shapes=ring_scratch(chunks, blocks, rows, depth)
        + gather_scratch(chunks, blocks, rows, depth)
        + [
            pltpu.VMEM((2, blocks // 2, rows, width), F32),
            pltpu.VMEM((rows, depth), F32),
            dma((2, 2)),
        ],
        compiler_params=pltpu.CompilerParams(
            collective_id=2, has_side_effects=True, vmem_limit_bytes=60 * 1024 * 1024
        ),
        name="back_rounds",
    )(dgate, dup, w_gate, w_up, resid, gain, cot, w_out)


class Peers:
    def __init__(self, axis, count, held, ss, rr):
        self.axis, self.count, self.held, self.ss, self.rr = axis, count, held, ss, rr
        self.me = lax.axis_index(axis)

    def other(self, k):
        return (self.me + k) % self.count

    def copy(self, slot, k):
        ref = self.held.at[slot]
        return pltpu.make_async_remote_copy(
            src_ref=ref,
            dst_ref=ref,
            send_sem=self.ss.at[k],
            recv_sem=self.rr.at[slot],
            device_id={self.axis: self.other(k)},
            device_id_type=MESH,
        )

    def greet(self):
        barrier = pltpu.get_barrier_semaphore()
        for k in range(1, self.count):
            pl.semaphore_signal(
                barrier, inc=1, device_id={self.axis: self.other(k)}, device_id_type=MESH
            )

    def send(self):
        for k in range(1, self.count):
            self.copy(self.me, k).start()

    def total(self):
        for k in range(1, self.count):
            self.copy(self.other(k), k).wait_recv()
        out = self.held[0]
        for slot in range(1, self.count):
            out = out + self.held[slot]
        return out

    def drain(self):
        for k in range(1, self.count):
            self.copy(self.me, k).wait_send()


def tail_kernel(
    gq_ref, gk_ref, gv_ref, gg_ref, gdw_ref, wq_ref, wk_ref, wv_ref, wg_ref, wdw_ref,
    input_ref, gain_ref, gres_ref, resid_ref, fgain_ref, ogain_ref, conv_ref, dl_ref, wide_ref, down_hbm,
    output_ref, igrad_ref, small_ref,
    own, stage, cross, line, xs, xr, ls, lr, own2, cross2, line2, xs2, xr2, ls2, lr2, osem,
    total, ngain, held1, held2, s1, r1, s2, r2,
):
    chunks, n, rows, depth = cross.shape
    blocks = 2 * n
    p = Place(blocks)
    first = Scatter(p, own, stage, cross, line, xs, xr, ls, lr)
    second = Scatter(p, own2, None, cross2, line2, xs2, xr2, ls2, lr2)
    heads = Peers("head", held1.shape[0], held1, s1, r1)
    items = Peers("item", held2.shape[0], held2, s2, r2)
    heads.greet()
    items.greet()
    pl.semaphore_wait(pltpu.get_barrier_semaphore(), heads.count + items.count - 2)
    ngain[...] = jnp.zeros_like(ngain)
    width1 = held1.shape[2]
    half = conv_ref.shape[2] // 2
    held1[heads.me] = jnp.zeros(held1.shape[1:], F32)
    held2[items.me] = jnp.zeros(held2.shape[1:], F32)

    def swap2(q):
        return remote(
            down_hbm.at[:, 1 - p.c, q], cross2.at[q], xs2.at[q], xr2.at[q], p.mate
        )

    def own_load(q):
        return pltpu.make_async_copy(down_hbm.at[:, p.c, q], own2.at[q % 2], osem.at[q % 2])

    def partial(q):
        pairs = [
            (ref[:, q].reshape(blocks * rows, -1), w)
            for ref, w in ((gq_ref, wq_ref), (gk_ref, wk_ref), (gv_ref, wv_ref), (gg_ref, wg_ref))
        ]
        dw = gdw_ref[:, q].reshape(blocks * rows, -1)
        for a, b in lane_tiles(depth, 512):
            value = mm(dw, wdw_ref[:, a:b])
            for x, w in pairs:
                value = value + mm(x, w[a:b, :], tb=True)
            put_share(p, own, stage, q, value, a, b)

    for q in range(chunks):
        swap2(q).start()
    own_load(0).start()
    partial(0)
    first.swap(0).start()

    def turn(r, _):
        own_load(r).wait()

        @pl.when(r + 1 < chunks)
        def _():
            own_load(r + 1).start()

        swap2(r).wait_recv()
        second.step(r, 0)
        first.swap(r).wait_recv()
        first.step(r, 0)

        @pl.when(r + 1 < chunks)
        def _():
            @pl.when(r >= 1)
            def _():
                first.swap(r - 1).wait_send()

            partial(r + 1)
            first.swap(r + 1).start()

        for s in range(1, n - 1):
            second.step(r, s)
            first.step(r, s)
        here = pl.ds(pl.multiple_of(r * rows, rows), rows)
        second.result(r, total)
        output_ref[here, :] = (resid_ref[here, :] + total[...]).astype(BF16)
        first.result(r, total)
        x = input_ref[here, :].astype(F32)
        scale = lax.rsqrt(jnp.mean(x * x, axis=1, keepdims=True) + 1e-05)
        u = x * scale
        grad = total[...]
        ngain[...] += jnp.sum((grad * u).reshape(rows // 8, 8, depth), axis=0)
        e = grad * gain_ref[...]
        igrad_ref[here, :] = gres_ref[here, :] + scale * (
            e - u * jnp.mean(e * u, axis=1, keepdims=True)
        )
        return 0

    lax.fori_loop(0, chunks, turn, 0)
    part = depth // 8
    for at, ref in ((0, ngain), (part, fgain_ref)):
        row = jnp.sum(ref[...], axis=0, keepdims=True)
        for i in range(8):
            held1[heads.me, i : i + 1, at : at + part] = row[:, i * part : (i + 1) * part]
    row = jnp.sum(ogain_ref[...], axis=0, keepdims=True)
    for i in range(2):
        held1[heads.me, i : i + 1, 2 * part : 2 * part + 128] = row[:, i * 128 : (i + 1) * 128]
    heads.send()
    for j in range(4):
        row = jnp.sum(conv_ref[j], axis=0, keepdims=True)
        for i in range(2):
            held2[items.me, 4 * i + j : 4 * i + j + 1, width1 : width1 + half] = row[
                :, i * half : (i + 1) * half
            ]
    at = width1 + half + 128
    held2[items.me, 0:1, width1 + half : at] = dl_ref[...]
    held2[items.me, :, at:] = wide_ref[...]
    held2[items.me, :, 0:width1] = heads.total()
    items.send()

    def drain(q, _):
        first.drain(q)
        second.drain(q)
        swap2(q).wait_send()
        return 0

    lax.fori_loop(0, chunks, drain, 0)
    for q in range(max(chunks - 2, 0), chunks):
        first.swap(q).wait_send()
    small_ref[...] = items.total()
    heads.drain()
    items.drain()


def tail(grads, weights, inputs, gain, gres, resid, fgain, ogain, gconv, gdl, wide, down, items):
    blocks, chunks, rows, depth = down.shape
    owned = inputs.shape[0]
    n = blocks // 2
    cut = lambda value: value.reshape(blocks, chunks, rows, -1)
    width1 = depth // 4 + 128
    width2 = width1 + gconv.shape[2] // 2 + 128 + wide.size // 8
    gdl = jnp.pad(gdl, ((0, 0), (0, 128 - gdl.shape[1])))
    dma = pltpu.SemaphoreType.DMA
    one = ring_scratch(chunks, blocks, rows, depth)
    output, igrad, small = pl.pallas_call(
        tail_kernel,
        in_specs=[WHOLE] * 19 + [ANY],
        out_specs=[WHOLE] * 3,
        out_shape=[
            jax.ShapeDtypeStruct((owned, depth), BF16),
            jax.ShapeDtypeStruct((owned, depth), F32),
            jax.ShapeDtypeStruct((8, width2), F32),
        ],
        scratch_shapes=one
        + [one[1]]
        + one[2:]
        + [
            dma((2,)),
            pltpu.VMEM((rows, depth), F32),
            pltpu.VMEM((8, depth), F32),
            pltpu.VMEM((blocks, 8, width1), F32),
            pltpu.VMEM((items, 8, width2), F32),
            dma((blocks,)),
            dma((blocks,)),
            dma((items,)),
            dma((items,)),
        ],
        compiler_params=pltpu.CompilerParams(
            collective_id=3, has_side_effects=True, vmem_limit_bytes=60 * 1024 * 1024
        ),
        name="tail_rounds",
    )(
        *[cut(value) for value in grads],
        *weights,
        inputs,
        gain,
        gres,
        resid,
        fgain,
        ogain,
        gconv,
        gdl,
        wide.reshape(8, -1),
        down.reshape(n, 2, chunks, rows, depth),
    )
    part = depth // 8
    half = gconv.shape[2] // 2
    conv = small[:, width1 : width1 + half]
    return (
        output,
        igrad,
        small[:, :part].reshape(-1),
        small[:, part : 2 * part].reshape(-1),
        small[:2, 2 * part : 2 * part + 128].reshape(-1),
        jnp.concatenate([conv[:4], conv[4:]], axis=1),
        small[0, width1 + half : width1 + half + 128],
        small[:, width1 + half + 128 :].reshape(wide.shape),
    )


def inner_rows(left, right):
    return lax.dot_general(
        left, right, (((0,), (0,)), ((), ())), preferred_element_type=jnp.float32
    )


def gather(values):
    return lax.all_gather(values.astype(jnp.bfloat16), "head", axis=0, tiled=True)


def total(values):
    return lax.psum([value.astype(jnp.bfloat16) for value in values], "item")


def after(values, *earlier):
    return lax.optimization_barrier((values, earlier))[0]


def local(
    items,
    layer_input,
    lengths,
    norm_gain,
    w_query,
    w_key,
    w_value,
    w_outgate,
    w_decay,
    w_write,
    conv_query,
    conv_key,
    conv_value,
    decay_log,
    out_gain,
    w_out,
    ffn_gain,
    w_gate,
    w_up,
    w_down,
    cotangent,
):
    inputs = layer_input.astype(F32)
    ng = norm_gain.astype(F32).reshape(1, -1)
    fg = ffn_gain.astype(F32).reshape(1, -1)
    og = out_gain.astype(F32).reshape(1, DV)
    conv = jnp.concatenate([conv_query, conv_key, conv_value], axis=1).astype(F32)
    dl = decay_log.reshape(1, -1)
    w_dw = jnp.concatenate([w_decay.T, w_write.T], axis=0)
    gate_t, up_t = w_gate.T, w_up.T
    normed = inputs * lax.rsqrt(jnp.mean(inputs * inputs, axis=-1, keepdims=True) + 1e-05) * ng
    group = gather(normed)
    tokens, depth = group.shape
    flat = lambda value: value.reshape(tokens, -1)
    grad_rows = gather(after(cotangent, group))
    by_seq = lambda value: value.reshape(-1, SEQ_LEN, value.shape[-1])
    project = lambda weight: by_seq(jnp.dot(group, weight, preferred_element_type=F32))
    raw = [project(weight) for weight in (w_query, w_key, w_value, w_outgate, w_dw.T)]
    mixed, *kept = mixer_fwd(lengths, *raw, conv, dl, og)
    mixed, grad_rows = lax.optimization_barrier((flat(mixed), grad_rows))
    resid, group_two, hidden, dgate, dup, down = ffn(
        mixed, w_out, layer_input, fg, gate_t, up_t, w_down, grad_rows
    )
    group_two, hidden = flat(group_two), flat(hidden)
    ffn_sums = total(
        (
            inner_rows(hidden, grad_rows),
            inner_rows(flat(dgate), group_two),
            inner_rows(flat(dup), group_two),
        )
    )
    grad_resid, fgain, grad_group, grad_mixed = back(
        dgate, dup, gate_t, up_t, resid, fg, cotangent, w_out
    )
    grad_w_out = inner_rows(mixed, flat(grad_group))
    *grads, gconv, gdl, ogain = mixer_bwd(
        lengths, *raw, conv, dl, og, by_seq(flat(grad_mixed)), *kept
    )
    grads = [flat(value) for value in grads]
    wide = [inner_rows(group, value) for value in grads[:4]]
    thin = inner_rows(grads[4], group)
    mix_sums = total(after([grad_w_out] + wide, ffn_sums))
    grads = after(grads, wide)
    output, input_grad, ngain, fgain, ogain, conv_grad, dl_grad, thin = tail(
        grads,
        (w_query, w_key, w_value, w_outgate, w_dw),
        layer_input,
        ng,
        grad_resid,
        resid,
        fgain,
        ogain,
        gconv,
        gdl,
        thin,
        down,
        items,
    )
    sums = [value.astype(F32) for value in mix_sums]
    heads = dl.shape[1]
    qw = w_query.shape[1]
    return (
        output,
        input_grad,
        ngain,
        *sums[1:],
        thin[:heads].T,
        thin[heads:].T,
        conv_grad[:, :qw],
        conv_grad[:, qw : 2 * qw],
        conv_grad[:, 2 * qw :],
        dl_grad[:heads],
        ogain,
        sums[0],
        fgain,
        ffn_sums[1].T.astype(F32),
        ffn_sums[2].T.astype(F32),
        ffn_sums[0].astype(F32),
    )


def solution(mesh):
    rows = P(("item", "head"), None)
    cols = P(None, "head")
    deep = P("head", None)
    return jax.shard_map(
        functools.partial(local, mesh.shape["item"]),
        mesh=mesh,
        in_specs=(rows, P("item"), P(), *[cols] * 9, P("head"), P(), deep, P(), cols, cols, deep, rows),
        out_specs=(rows, rows, P(), *[cols] * 9, P("head"), P(), deep, P(), cols, cols, deep),
        check_vma=False,
    )
```

```python
import functools

import jax
import jax.numpy as jnp
from jax import lax
from jax.experimental import pallas as pl
from jax.experimental.pallas import tpu as pltpu
from jax.sharding import PartitionSpec as P

DK = 128
DV = 256
SEQ_LEN = 1024
CHUNK = 128
F32 = jnp.float32
BF16 = jnp.bfloat16


def mm(left, right, ta=False, tb=False):
    return lax.dot_general(
        left.astype(BF16),
        right.astype(BF16),
        (((0 if ta else 1,), (1 if tb else 0,)), ((), ())),
        preferred_element_type=F32,
    )


def split(value):
    high = value.astype(BF16)
    return high, (value - high.astype(F32)).astype(BF16)


def mm3(left, right):
    lh, ll = left
    rh, rl = right
    return mm(lh, rh) + (mm(lh, rl) + mm(ll, rh))


def sigmoid(x):
    return 1.0 / (1.0 + jnp.exp(-x))


def grids():
    rows = lax.broadcasted_iota(jnp.int32, (CHUNK, CHUNK), 0)
    cols = lax.broadcasted_iota(jnp.int32, (CHUNK, CHUNK), 1)
    return rows, cols


def to_row(col, eye):
    return jnp.sum(jnp.where(eye, col, 0.0), axis=0, keepdims=True)


def inverses(mats, rows, cols):
    eye = jnp.where(rows == cols, 1.0, 0.0)
    near = rows // 16 == cols // 16
    n1 = [jnp.where(near, -a, 0.0) for a in mats]
    n1s = [split(n) for n in n1]
    n2 = [mm3(n, n) for n in n1s]
    n2s = [split(n) for n in n2]
    n3 = [mm3(a, b) for a, b in zip(n1s, n2s)]
    n4s = [split(mm3(n, n)) for n in n2s]
    p1 = [eye + a + b + c for a, b, c in zip(n1, n2, n3)]
    p2 = [p + mm3(split(p), n) for p, n in zip(p1, n4s)]
    n8s = [split(mm3(n, n)) for n in n4s]
    x = [p + mm3(split(p), n) for p, n in zip(p2, n8s)]
    size = 16
    while size < CHUNK:
        pair = (rows // (2 * size) == cols // (2 * size)) & (rows // size != cols // size)
        xs = [split(v) for v in x]
        b = [split(jnp.where(pair, a, 0.0)) for a in mats]
        bx = [split(mm3(u, v)) for u, v in zip(b, xs)]
        x = [v - mm3(vs, w) for v, vs, w in zip(x, xs, bx)]
        size *= 2
    return x


def lead(ref):
    return ref[...].astype(F32)


def decays(ld, eye, causal):
    row = to_row(ld, eye)
    g = jnp.sum(jnp.where(causal, row, 0.0), axis=1, keepdims=True)
    grow = to_row(g, eye)
    d = jnp.where(causal, jnp.exp(jnp.where(causal, g - grow, 0.0)), 0.0)
    last = g[CHUNK - 1 : CHUNK, :]
    return d, jnp.exp(g), jnp.exp(last - g), jnp.exp(last)


def live_mask(len_ref, s, c):
    spot = lax.broadcasted_iota(jnp.int32, (CHUNK, 1), 0) + c * CHUNK
    return jnp.where(spot < len_ref[s], 1.0, 0.0)


def softplus(x):
    return jnp.maximum(x, 0.0) + jnp.log1p(jnp.exp(-jnp.abs(x)))


def mix_fwd_kernel(
    len_ref, q_ref, k_ref, v_ref, g_ref, dw_ref, conv_ref, dl_ref, gain_ref,
    mixed_ref, pre_ref, o_ref, u_ref, t_ref, s_ref, buf, state,
):
    c = pl.program_id(0)
    seqs, _, raws = buf.shape
    heads = dl_ref.shape[1]
    qw = heads * DK
    pieces = ((q_ref, 0, qw), (k_ref, qw, 2 * qw), (v_ref, 2 * qw, raws))

    @pl.when(c == 0)
    def _():
        buf[:, 0:8, :] = jnp.zeros((seqs, 8, raws), F32)
        state[...] = jnp.zeros_like(state)

    rows, cols = grids()
    eye = rows == cols
    causal = rows >= cols
    lower = rows > cols
    rate = jnp.exp(dl_ref[...])
    st = []
    for s in range(seqs):
        for ref, a, b in pieces:
            buf[s, 8 : 8 + CHUNK, a:b] = ref[s]
        pre = conv_ref[0:1, :] * buf[s, 5 : 5 + CHUNK, :]
        for j in range(1, 4):
            pre = pre + conv_ref[j : j + 1, :] * buf[s, 5 + j : 5 + j + CHUNK, :]
        pre_ref[s] = pre
        buf[s, 0:8, :] = buf[s, CHUNK : CHUNK + 8, :]
        act = pre * sigmoid(pre)
        mask = live_mask(len_ref, s, c)
        x = dw_ref[s]
        ld2 = -rate * softplus(x[:, :heads]) * mask
        be2 = sigmoid(x[:, heads:]) * mask
        for h in range(heads):
            q = act[:, h * DK : (h + 1) * DK]
            k = act[:, qw + h * DK : qw + (h + 1) * DK]
            v = act[:, 2 * qw + h * DV : 2 * qw + (h + 1) * DV]
            q = q * (lax.rsqrt(jnp.sum(q * q, axis=1, keepdims=True) + 1e-06) * DK ** (-0.5))
            k = k * lax.rsqrt(jnp.sum(k * k, axis=1, keepdims=True) + 1e-06)
            be = be2[:, h : h + 1]
            d, ga, e, el = decays(ld2[:, h : h + 1], eye, causal)
            qb = q.astype(BF16)
            kb = k.astype(BF16)
            qk = jnp.concatenate([qb, kb], axis=0)
            both = mm(qk, kb, tb=True)
            w = d * both[:CHUNK]
            a = jnp.where(lower, d * both[CHUNK:], 0.0) * be
            st.append((s, h, mask, v, be, ga, e, el, qk, kb, w, a))
    inv = inverses([z[-1] for z in st], rows, cols)
    for i, (s, h, mask, v, be, ga, e, el, qk, kb, w, a) in enumerate(st):
        t = inv[i].astype(BF16)
        old = state[i]
        oldb = old.astype(BF16)
        s_ref[i] = oldb
        t_ref[i] = t
        qks = mm(qk, oldb)
        r = be * (v - ga * qks[CHUNK:])
        u = mm(t, r)
        ub = u.astype(BF16)
        u_ref[s, :, h * DV : (h + 1) * DV] = ub
        o = ga * qks[:CHUNK] + mm(w, ub)
        state[i] = el * old + mm(kb, e * u, ta=True)
        o = o * mask
        o_ref[s, :, h * DV : (h + 1) * DV] = o
        rg = g_ref[s, :, h * DV : (h + 1) * DV]
        n = o * lax.rsqrt(jnp.mean(o * o, axis=1, keepdims=True) + 1e-05) * gain_ref[...]
        mixed_ref[s, :, h * DV : (h + 1) * DV] = (n * (rg * sigmoid(rg))).astype(BF16)


def mix_bwd_kernel(
    len_ref, q_ref, k_ref, v_ref, g_ref, dw_ref, conv_ref, dl_ref, gain_ref,
    gm_ref, pre_ref, o_ref, u_ref, t_ref, s_ref, group_ref, resid_ref, down_hbm,
    gq_ref, gk_ref, gv_ref, gg_ref, gdw_ref, gconv_ref, gdl_ref, ggain_ref,
    wq_ref, wk_ref, wv_ref, wg_ref, thin_ref, output_ref, buf, dstate, wq, wk, wv, wg,
    own, cross, line, xs, xr, ls, lr, osem, total,
):
    step = pl.program_id(0)
    c = pl.num_programs(0) - 1 - step
    place = Place(2 * cross.shape[1])
    summing = Late(place, down_hbm, 0, own, cross, line, xs, xr, ls, lr, osem)

    @pl.when(step == 0)
    def _():
        place.greet()
        summing.start()


    def add_output(q):
        rows = total.shape[0]
        here = pl.ds(pl.multiple_of(q * rows, rows), rows)
        summing.scatter.result(q, total)
        output_ref[here, :] = (resid_ref[here, :] + total[...]).astype(BF16)

    each = -(-(own.shape[0] + place.n - 1) // (SEQ_LEN // CHUNK - 1))

    @pl.when(step >= 1)
    def _():
        for i in range(each):
            summing.tick((step - 1) * each + i, add_output)

    seqs, _, raws = buf.shape
    heads = dl_ref.shape[1]
    qw = heads * DK
    pieces = ((q_ref, 0, qw), (k_ref, qw, 2 * qw), (v_ref, 2 * qw, raws))

    @pl.when(step == 0)
    def _():
        buf[:, CHUNK : CHUNK + 8, :] = jnp.zeros((seqs, 8, raws), F32)
        dstate[...] = jnp.zeros_like(dstate)
        gconv_ref[...] = jnp.zeros_like(gconv_ref)
        gdl_ref[...] = jnp.zeros_like(gdl_ref)
        ggain_ref[...] = jnp.zeros_like(ggain_ref)
        for ref in (wq, wk, wv, wg, thin_ref):
            ref[...] = jnp.zeros_like(ref)

    rows, cols = grids()
    eye = rows == cols
    causal = rows >= cols
    lower = rows > cols
    later = rows <= cols
    rate = jnp.exp(dl_ref[...])
    gain = gain_ref[...]
    for s in range(seqs):
        mask = live_mask(len_ref, s, c)
        x = dw_ref[s]
        soft = -rate * mask
        ld2 = soft * softplus(x[:, :heads])
        sg = sigmoid(x)
        be2 = sg[:, heads:] * mask
        dlds = []
        dbes = []
        for h in range(heads):
            i = heads * s + h
            vs = slice(h * DV, (h + 1) * DV)
            gm = gm_ref[s, :, vs]
            o = o_ref[s, :, vs]
            rg = g_ref[s, :, h * DV : (h + 1) * DV]
            sr = sigmoid(rg)
            r = lax.rsqrt(jnp.mean(o * o, axis=1, keepdims=True) + 1e-05)
            un = o * r
            gsg = gm * sr
            gg_ref[s, :, h * DV : (h + 1) * DV] = (
                gsg * (un * gain) * (1.0 + rg * (1.0 - sr))
            ).astype(BF16)
            dn = gsg * rg
            dnu = dn * un
            ggain_ref[...] += jnp.sum(dnu.reshape(CHUNK // 8, 8, DV), axis=0)
            do = (r * mask) * (dn * gain - un * jnp.mean(dnu * gain, axis=1, keepdims=True))
            pq = pre_ref[s, :, h * DK : (h + 1) * DK]
            pk = pre_ref[s, :, qw + h * DK : qw + (h + 1) * DK]
            pv = pre_ref[s, :, 2 * qw + h * DV : 2 * qw + (h + 1) * DV]
            sq = sigmoid(pq)
            sk = sigmoid(pk)
            sv = sigmoid(pv)
            q = pq * sq
            k = pk * sk
            v = pv * sv
            rq = lax.rsqrt(jnp.sum(q * q, axis=1, keepdims=True) + 1e-06)
            rk = lax.rsqrt(jnp.sum(k * k, axis=1, keepdims=True) + 1e-06)
            q = q * rq
            k = k * rk
            scale = DK ** (-0.5)
            be = be2[:, h : h + 1]
            d, ga, e, el = decays(ld2[:, h : h + 1], eye, causal)
            qb = (q * scale).astype(BF16)
            kb = k.astype(BF16)
            qk = jnp.concatenate([qb, kb], axis=0)
            both = mm(qk, kb, tb=True)
            w = d * both[:CHUNK]
            ab = jnp.where(lower, d * both[CHUNK:], 0.0)
            a = ab * be
            t = t_ref[i]
            st = s_ref[i]
            u = u_ref[s, :, vs]
            dh = dstate[i]
            dhb = dh.astype(BF16)
            qks = mm(qk, st)
            dob = do.astype(BF16)
            kdh = e * mm(kb, dhb)
            ubar = mm(w, dob, ta=True) + kdh
            rbar = mm(t, ubar, ta=True)
            rb = rbar.astype(BF16)
            uu = mm(jnp.concatenate([dob, rb], axis=0), u, tb=True)
            wbar = jnp.where(causal, uu[:CHUNK], 0.0)
            abar = -jnp.where(lower, uu[CHUNK:], 0.0)
            gks = ga * qks[CHUNK:]
            dv = be * rbar
            y = -ga * dv
            z = ga * do
            zy = jnp.concatenate([z.astype(BF16), y.astype(BF16)], axis=0)
            zys = mm(zy, st, tb=True)
            p = (wbar * d).astype(BF16)
            m = abar * d * be
            eu = e * u.astype(F32)
            dq = zys[:CHUNK] + mm(p, kb)
            dk = (
                zys[CHUNK:]
                + mm(p, qb, ta=True)
                + mm(m, kb)
                + mm(m, kb, ta=True)
                + mm(eu, dhb, tb=True)
            )
            dstate[i] = el * dh + mm(qk, zy, ta=True)
            ee = wbar * w + abar * a
            f = jnp.sum(u.astype(F32) * kdh, axis=1, keepdims=True)
            dbe = jnp.sum(rbar * (v - gks), axis=1, keepdims=True) + jnp.sum(
                abar * ab, axis=1, keepdims=True
            )
            dgc = (
                jnp.sum(ee, axis=1, keepdims=True)
                + jnp.sum(z * qks[:CHUNK] - dv * gks, axis=1, keepdims=True)
                - f
            )
            dgr = to_row(dgc, eye) - jnp.sum(ee, axis=0, keepdims=True)
            total = jnp.sum(f, axis=0, keepdims=True) + el * jnp.sum(
                jnp.sum(st.astype(F32) * dh, axis=1, keepdims=True), axis=0, keepdims=True
            )
            dld = jnp.sum(jnp.where(later, dgr, 0.0), axis=1, keepdims=True) + total
            dlds.append(dld)
            dbes.append(dbe)
            dq = dq * scale
            dqa = rq * (dq - q * jnp.sum(q * dq, axis=1, keepdims=True))
            dka = rk * (dk - k * jnp.sum(k * dk, axis=1, keepdims=True))
            buf[s, 0:CHUNK, h * DK : (h + 1) * DK] = dqa * sq * (1.0 + pq * (1.0 - sq))
            buf[s, 0:CHUNK, qw + h * DK : qw + (h + 1) * DK] = dka * sk * (1.0 + pk * (1.0 - sk))
            buf[s, 0:CHUNK, 2 * qw + h * DV : 2 * qw + (h + 1) * DV] = dv * sv * (1.0 + pv * (1.0 - sv))
        dld2 = jnp.concatenate(dlds, axis=1) if heads > 1 else dlds[0]
        dbe2 = jnp.concatenate(dbes, axis=1) if heads > 1 else dbes[0]
        gdw_ref[s] = jnp.concatenate(
            [dld2 * soft * sg[:, :heads], dbe2 * be2 * (1.0 - sg[:, heads:])], axis=1
        ).astype(BF16)
        gdl_ref[...] += jnp.sum(dld2 * ld2, axis=0, keepdims=True)
        for (ref, a, b), out in zip(pieces, (gq_ref, gk_ref, gv_ref)):
            raw = ref[s]
            draw = None
            for j in range(4):
                shifted = buf[s, 3 - j : 3 - j + CHUNK, a:b]
                gconv_ref[j, :, a:b] += jnp.sum(
                    (raw * shifted).reshape(CHUNK // 8, 8, b - a), axis=0
                )
                term = conv_ref[j : j + 1, a:b] * shifted
                draw = term if draw is None else draw + term
            out[s] = draw.astype(BF16)
        buf[s, CHUNK : CHUNK + 8, :] = buf[s, 0:8, :]
    x = group_ref[...].reshape(seqs * CHUNK, -1)
    wides = ((wq, gq_ref, wq_ref), (wk, gk_ref, wk_ref), (wv, gv_ref, wv_ref), (wg, gg_ref, wg_ref))
    for acc, ref, _ in wides:
        grad = ref[...].reshape(seqs * CHUNK, -1)
        for a in range(0, x.shape[1], 512):
            acc[a : a + 512, :] += mm(x[:, a : a + 512], grad, ta=True)
    thin_ref[...] += mm(gdw_ref[...].reshape(seqs * CHUNK, -1), x, ta=True)

    @pl.when(c == 0)
    def _():
        for acc, _, out in wides:
            out[...] = acc[...].astype(BF16)
        summing.drain()


def mixer_fwd(lengths, q, k, v, g, dw, conv, dl, gain):
    count = SEQ_LEN // CHUNK
    seqs = q.shape[0]
    heads = dl.shape[1]
    raws, vw, n = conv.shape[1], heads * DV, seqs * heads
    full = lambda shape: pl.BlockSpec(shape, lambda c: (0,) * len(shape))
    seq = lambda width: pl.BlockSpec((seqs, CHUNK, width), lambda c: (0, c, 0))
    return pl.pallas_call(
        mix_fwd_kernel,
        grid=(count,),
        in_specs=[
            pl.BlockSpec(memory_space=pltpu.SMEM),
            seq(q.shape[2]),
            seq(k.shape[2]),
            seq(vw),
            seq(vw),
            seq(2 * heads),
            full((4, raws)),
            full((1, heads)),
            full((1, DV)),
        ],
        out_specs=[
            seq(vw),
            seq(raws),
            seq(vw),
            seq(vw),
            pl.BlockSpec((n, None, CHUNK, CHUNK), lambda c: (0, c, 0, 0)),
            pl.BlockSpec((n, None, DK, DV), lambda c: (0, c, 0, 0)),
        ],
        out_shape=[
            jax.ShapeDtypeStruct((seqs, SEQ_LEN, vw), BF16),
            jax.ShapeDtypeStruct((seqs, SEQ_LEN, raws), F32),
            jax.ShapeDtypeStruct((seqs, SEQ_LEN, vw), F32),
            jax.ShapeDtypeStruct((seqs, SEQ_LEN, vw), BF16),
            jax.ShapeDtypeStruct((n, count, CHUNK, CHUNK), BF16),
            jax.ShapeDtypeStruct((n, count, DK, DV), BF16),
        ],
        scratch_shapes=[
            pltpu.VMEM((seqs, CHUNK + 8, raws), F32),
            pltpu.VMEM((n, DK, DV), F32),
        ],
        compiler_params=pltpu.CompilerParams(
            dimension_semantics=("arbitrary",), vmem_limit_bytes=48 * 1024 * 1024
        ),
        name="mixer_forward",
    )(lengths, q, k, v, g, dw, conv, dl, gain)


def mixer_bwd(lengths, q, k, v, g, dw, conv, dl, gain, gm, pre, o, u, t, s, group, resid, down):
    count = SEQ_LEN // CHUNK
    seqs = q.shape[0]
    heads = dl.shape[1]
    raws, vw, n = conv.shape[1], heads * DV, seqs * heads
    depth = group.shape[2]
    blocks, chunks, rows, _ = down.shape
    early = chunks // 2
    wide = [(depth, value.shape[2]) for value in (q, k, v, g)] + [(dw.shape[2], depth)]
    full = lambda shape: pl.BlockSpec(shape, lambda c: (0,) * len(shape))
    seq = lambda width: pl.BlockSpec((seqs, CHUNK, width), lambda c: (0, count - 1 - c, 0))
    return pl.pallas_call(
        mix_bwd_kernel,
        grid=(count,),
        in_specs=[
            pl.BlockSpec(memory_space=pltpu.SMEM),
            seq(q.shape[2]),
            seq(k.shape[2]),
            seq(vw),
            seq(vw),
            seq(2 * heads),
            full((4, raws)),
            full((1, heads)),
            full((1, DV)),
            seq(vw),
            seq(raws),
            seq(vw),
            seq(vw),
            pl.BlockSpec((n, None, CHUNK, CHUNK), lambda c: (0, count - 1 - c, 0, 0)),
            pl.BlockSpec((n, None, DK, DV), lambda c: (0, count - 1 - c, 0, 0)),
            seq(group.shape[2]),
            full((early * rows, depth)),
            pl.BlockSpec(memory_space=pl.ANY),
        ],
        out_specs=[
            seq(q.shape[2]),
            seq(k.shape[2]),
            seq(vw),
            seq(vw),
            seq(2 * heads),
            full((4, 8, raws)), full((1, heads)),
            full((8, DV)),
            *[full(shape) for shape in wide],
            full((early * rows, depth)),
        ],
        out_shape=[
            jax.ShapeDtypeStruct(q.shape, BF16),
            jax.ShapeDtypeStruct(k.shape, BF16),
            jax.ShapeDtypeStruct(v.shape, BF16),
            jax.ShapeDtypeStruct(g.shape, BF16),
            jax.ShapeDtypeStruct(dw.shape, BF16),
            jax.ShapeDtypeStruct((4, 8, raws), F32),
            jax.ShapeDtypeStruct((1, heads), F32),
            jax.ShapeDtypeStruct((8, DV), F32),
            *[jax.ShapeDtypeStruct(shape, BF16) for shape in wide[:4]],
            jax.ShapeDtypeStruct(wide[4], F32),
            jax.ShapeDtypeStruct((early * rows, depth), BF16),
        ],
        scratch_shapes=[
            pltpu.VMEM((seqs, CHUNK + 8, raws), F32),
            pltpu.VMEM((n, DK, DV), F32),
            *[pltpu.VMEM(shape, F32) for shape in wide[:4]],
            *late_scratch(early, early, blocks, rows, depth),
            pltpu.VMEM((rows, depth), F32),
        ],
        compiler_params=pltpu.CompilerParams(
            dimension_semantics=("arbitrary",),
            vmem_limit_bytes=62 * 1024 * 1024,
            collective_id=5,
            has_side_effects=True,
        ),
        name="mixer_backward",
    )(
        lengths,
        q,
        k,
        v,
        g,
        dw,
        conv,
        dl,
        gain,
        gm,
        pre,
        o,
        u,
        t,
        s,
        group,
        resid,
        down.reshape(blocks // 2, 2, chunks, rows, depth),
    )


MESH = pl.DeviceIdType.MESH


class Place:
    def __init__(self, blocks):
        head = lax.axis_index("head")
        self.n = blocks // 2
        self.me = head
        self.z = head // 2
        self.c = head % 2
        self.mate = 2 * self.z + 1 - self.c
        self.right = head + 2
        self.left = head - 2
        self.has_right = self.z < self.n - 1
        self.has_left = self.z > 0

    def greet(self, items=1):
        barrier = pltpu.get_barrier_semaphore()
        item = lax.axis_index("item")
        for k in range(1, items):
            pl.semaphore_signal(
                barrier, inc=1, device_id={"item": (item + k) % items}, device_id_type=MESH
            )

        def hello(device):
            pl.semaphore_signal(barrier, inc=1, device_id={"head": device}, device_id_type=MESH)

        hello(self.mate)
        pl.when(self.has_right)(lambda: hello(self.right))
        pl.when(self.has_left)(lambda: hello(self.left))
        n = self.n
        pl.semaphore_wait(barrier, items + (self.z + n - 1) // n + (2 * n - 2 - self.z) // n)


def remote(src, dst, send, recv, device):
    return pltpu.make_async_remote_copy(
        src_ref=src,
        dst_ref=dst,
        send_sem=send,
        recv_sem=recv,
        device_id={"head": device},
        device_id_type=MESH,
    )


class Scatter:
    def __init__(self, place, own, stage, cross, line, xs, xr, ls, lr):
        self.p = place
        self.own, self.stage, self.cross, self.line = own, stage, cross, line
        self.xs, self.xr, self.ls, self.lr = xs, xr, ls, lr

    def swap(self, q):
        return remote(
            self.stage.at[q % 2], self.cross.at[q], self.xs.at[q], self.xr.at[q], self.p.mate
        )

    def hop(self, q, slot, device):
        ref = self.line.at[q, slot]
        return remote(ref, ref, self.ls.at[q, slot], self.lr.at[q, slot], device)

    def share(self, q, t):
        return self.own[q % self.own.shape[0], t].astype(F32) + self.cross[q, t].astype(F32)

    def pass_on(self, q, t, slot, first, device):
        @pl.when(first)
        def _():
            self.line[q, slot] = self.share(q, t).astype(BF16)

        @pl.when(jnp.logical_not(first))
        def _():
            self.hop(q, slot, device).wait_recv()
            self.line[q, slot] = (self.share(q, t) + self.line[q, slot].astype(F32)).astype(BF16)

        self.hop(q, slot, device).start()

    def right_at(self, s):
        return self.p.n - 1 - s + self.p.z

    def left_at(self, s):
        n = self.p.n
        t = s + 1 - n + self.p.z
        return t, (t + n) % (n + 1)

    def step(self, q, s):
        p = self.p

        @pl.when(p.z <= s)
        def _():
            t = self.right_at(s)
            self.pass_on(q, t, t, p.z == 0, p.right)

        @pl.when(p.n - 1 - p.z <= s)
        def _():
            t, slot = self.left_at(s)
            self.pass_on(q, t, slot, p.z == p.n - 1, p.left)

    def result(self, q, total):
        p = self.p
        total[...] = self.share(q, p.z)

        @pl.when(p.has_left)
        def _():
            self.hop(q, p.z, p.right).wait_recv()
            total[...] += self.line[q, p.z].astype(F32)

        @pl.when(p.has_right)
        def _():
            slot = (p.z + p.n) % (p.n + 1)
            self.hop(q, slot, p.left).wait_recv()
            total[...] += self.line[q, slot].astype(F32)

    def drain(self, q):
        p = self.p
        for s in range(p.n - 1):

            @pl.when(p.z <= s)
            def _():
                self.hop(q, self.right_at(s), p.right).wait_send()

            @pl.when(p.n - 1 - p.z <= s)
            def _():
                self.hop(q, self.left_at(s)[1], p.left).wait_send()


class Late:
    def __init__(self, place, src, first, own, cross, line, xs, xr, ls, lr, osem):
        self.p, self.src, self.first = place, src, first
        self.count = cross.shape[0]
        self.own, self.cross, self.osem = own, cross, osem
        self.xs, self.xr = xs, xr
        self.scatter = Scatter(place, own, None, cross, line, xs, xr, ls, lr)

    def swap(self, q):
        return remote(
            self.src.at[:, 1 - self.p.c, self.first + q],
            self.cross.at[q],
            self.xs.at[q],
            self.xr.at[q],
            self.p.mate,
        )

    def load(self, q):
        slot = q % self.own.shape[0]
        return pltpu.make_async_copy(
            self.src.at[:, self.p.c, self.first + q], self.own.at[slot], self.osem.at[slot]
        )

    def start(self):
        for q in range(self.count):
            self.swap(q).start()
        for q in range(self.own.shape[0]):
            self.load(q).start()

    def enter(self, q):
        self.load(q).wait()
        self.swap(q).wait_recv()
        self.scatter.step(q, 0)

    def tick(self, w, result):
        n = self.p.n

        @pl.when(within(w - n + 1, self.count))
        def _():
            result(w - n + 1)

        for s in range(n - 2, 0, -1):

            @pl.when(within(w - s, self.count))
            def _():
                self.scatter.step(w - s, s)

        @pl.when(w < self.count)
        def _():
            self.enter(w)

    def drain(self):
        def body(q, _):
            self.scatter.drain(q)
            self.swap(q).wait_send()
            return 0

        lax.fori_loop(0, self.count, body, 0)


def late_scratch(count, slots, blocks, rows, depth):
    n = blocks // 2
    dma = pltpu.SemaphoreType.DMA
    return [
        pltpu.VMEM((slots, n, rows, depth), BF16),
        pltpu.VMEM((count, n, rows, depth), BF16),
        pltpu.VMEM((count, n + 1, rows, depth), BF16),
        dma((count,)),
        dma((count,)),
        dma((count, n + 1)),
        dma((count, n + 1)),
        dma((slots,)),
    ]


class Gather:
    def __init__(self, place, held, ss, rr):
        self.p, self.held, self.ss, self.rr = place, held, ss, rr

    def copy(self, q, kind, z):
        p = self.p
        block = 2 * z + p.c
        ref = self.held.at[q, block]
        device = (p.right, p.left, p.mate)[kind]
        return remote(ref, ref, self.ss.at[q, kind, z], self.rr.at[q, block], device)

    def step(self, q, s):
        p = self.p
        if s == 0:
            pl.when(p.has_right)(lambda: self.copy(q, 0, p.z).start())
            pl.when(p.has_left)(lambda: self.copy(q, 1, p.z).start())
            self.copy(q, 2, p.z).start()
            return

        @pl.when(p.z >= s)
        def _():
            z = p.z - s
            self.copy(q, 0, z).wait_recv()
            pl.when(p.has_right)(lambda: self.copy(q, 0, z).start())
            self.copy(q, 2, z).start()

        @pl.when(p.z + s <= p.n - 1)
        def _():
            z = p.z + s
            self.copy(q, 1, z).wait_recv()
            pl.when(p.has_left)(lambda: self.copy(q, 1, z).start())
            self.copy(q, 2, z).start()

    def finish(self, q):
        p = self.p
        for z in range(p.n):
            block = 2 * z + 1 - p.c
            ref = self.held.at[q, block]
            remote(ref, ref, self.ss.at[q, 2, z], self.rr.at[q, block], p.mate).wait_recv()

    def drain(self, q):
        p = self.p
        for z in range(p.n):
            self.copy(q, 2, z).wait_send()

            @pl.when(jnp.logical_and(p.has_right, p.z >= z))
            def _():
                self.copy(q, 0, z).wait_send()

            @pl.when(jnp.logical_and(p.has_left, p.z <= z))
            def _():
                self.copy(q, 1, z).wait_send()


def lane_tiles(width, size=256):
    return [(at, min(at + size, width)) for at in range(0, width, size)]


def put_share(place, own, stage, q, values, a, b):
    slots, n, rows, _ = own.shape
    parts = values.astype(BF16).reshape(n, 2, rows, b - a)

    @pl.when(place.c == 0)
    def _():
        own[q % slots, :, :, a:b] = parts[:, 0]
        stage[q % 2, :, :, a:b] = parts[:, 1]

    @pl.when(place.c == 1)
    def _():
        own[q % slots, :, :, a:b] = parts[:, 1]
        stage[q % 2, :, :, a:b] = parts[:, 0]


def ring_scratch(chunks, blocks, rows, depth):
    n = blocks // 2
    dma = pltpu.SemaphoreType.DMA
    return [
        pltpu.VMEM((min(chunks, n), n, rows, depth), BF16),
        pltpu.VMEM((2, n, rows, depth), BF16),
        pltpu.VMEM((chunks, n, rows, depth), BF16),
        pltpu.VMEM((chunks, n + 1, rows, depth), BF16),
        dma((chunks,)),
        dma((chunks,)),
        dma((chunks, n + 1)),
        dma((chunks, n + 1)),
    ]


def gather_scratch(chunks, blocks, rows, depth):
    dma = pltpu.SemaphoreType.DMA
    return [
        pltpu.VMEM((chunks, blocks, rows, depth), BF16),
        dma((chunks, 3, blocks // 2)),
        dma((chunks, blocks)),
    ]


def within(q, chunks):
    return jnp.logical_and(q >= 0, q < chunks)


def ticks(chunks, n, scatter, gather, partial, middle, consume, also=None):
    partial(0)
    scatter.swap(0).start()

    def tick(w, _):
        v = w - n + 1

        @pl.when(within(v, chunks))
        def _():
            middle(v)
            gather.step(v, 0)

        for s in range(n - 2, 0, -1):

            @pl.when(within(w - s, chunks))
            def _():
                scatter.step(w - s, s)

        @pl.when(w < chunks)
        def _():
            scatter.swap(w).wait_recv()
            scatter.step(w, 0)

        for s in range(n - 1, 0, -1):

            @pl.when(within(v - s, chunks))
            def _():
                gather.step(v - s, s)

        if also is not None:
            also(w)

        @pl.when(w + 1 < chunks)
        def _():
            @pl.when(w >= 1)
            def _():
                scatter.swap(w - 1).wait_send()

            partial(w + 1)
            scatter.swap(w + 1).start()

        @pl.when(v >= n - 1)
        def _():
            gather.finish(v - n + 1)
            consume(v - n + 1)

        return 0

    lax.fori_loop(0, chunks + 2 * n - 2, tick, 0)
    for q in range(max(chunks - 2, 0), chunks):
        scatter.swap(q).wait_send()

    def drain(q, _):
        scatter.drain(q)
        gather.drain(q)
        return 0

    lax.fori_loop(0, chunks, drain, 0)


def ffn_kernel(
    mixed_ref, w_out_ref, input_ref, gain_ref, w_gate_hbm, w_up_hbm, w_down_hbm, cot_ref, cot_hbm,
    resid_ref, group_hbm, dgate_hbm, dup_hbm, down_hbm, gdown_hbm,
    own, stage, cross, line, xs, xr, ls, lr, held, gs, gr,
    held2, gs2, gr2,
    w_gate, w_up, w_down, cot, hid, dg, du, down, gdown, total, wsem, csem, osem, dsem,
):
    chunks, blocks, rows, depth = held.shape
    units = w_gate.shape[0]
    p = Place(blocks)
    scatter = Scatter(p, own, stage, cross, line, xs, xr, ls, lr)
    gather = Gather(p, held, gs, gr)
    loads = [
        pltpu.make_async_copy(src, dst, wsem.at[i])
        for i, (src, dst) in enumerate(
            ((w_gate_hbm, w_gate), (w_up_hbm, w_up), (w_down_hbm, w_down))
        )
    ]
    for load in loads:
        load.start()
    cot_load = lambda q: pltpu.make_async_copy(cot_hbm.at[:, q], cot.at[q % 2], csem.at[q % 2])
    cot_load(0).start()
    early = cot_hbm.shape[1]
    p.greet()
    later = Gather(p, held2, gs2, gr2)

    def also(w):
        for s in range(p.n - 1, -1, -1):

            @pl.when(within(w - s, chunks - early))
            def _():
                if s == 0:
                    here = pl.ds(pl.multiple_of((early + w) * rows, rows), rows)
                    held2[w, p.me] = cot_ref[here, :]
                later.step(w - s, s)
                if s == p.n - 1:
                    later.finish(w - s)

    def partial(q):
        x = mixed_ref[:, q].reshape(blocks * rows, -1)
        for a, b in lane_tiles(depth, 512):
            put_share(
                p, own, stage, q, jnp.dot(x, w_out_ref[:, a:b], preferred_element_type=F32), a, b
            )

    def middle(q):
        scatter.result(q, total)
        here = pl.ds(pl.multiple_of(q * rows, rows), rows)
        resid = input_ref[here, :].astype(F32) + total[...]
        resid_ref[here, :] = resid
        normed = resid * lax.rsqrt(jnp.mean(resid * resid, axis=1, keepdims=True) + 1e-05)
        held[q, p.me] = (normed * gain_ref[...]).astype(BF16)

    def saves(q):
        slot = q % 2
        return [
            pltpu.make_async_copy(src.at[slot], dst.at[:, q], osem.at[slot, i])
            for i, (src, dst) in enumerate(((dg, dgate_hbm), (du, dup_hbm), (down, down_hbm)))
        ] + [pltpu.make_async_copy(held.at[q], group_hbm.at[:, q], osem.at[slot, 3])]

    def consume(q):
        slot = q % 2

        @pl.when(q == 0)
        def _():
            for load in loads:
                load.wait()
            gdown[...] = jnp.zeros_like(gdown)

        @pl.when(q < early)
        def _():
            cot_load(q).wait()

        @pl.when(q >= early)
        def _():
            cot[slot] = held2[q - early]

        @pl.when(q + 1 < early)
        def _():
            cot_load(q + 1).start()

        @pl.when(q >= 2)
        def _():
            for save in saves(q - 2):
                save.wait()

        x = held[q].reshape(blocks * rows, depth)
        g = cot[slot].reshape(blocks * rows, depth)
        for a, b in lane_tiles(units):
            gate = mm(x, w_gate[a:b, :], tb=True)
            up = mm(x, w_up[a:b, :], tb=True)
            gh = mm(g, w_down[a:b, :], tb=True)
            sg = sigmoid(gate)
            act = gate * sg
            shape = (blocks, rows, b - a)
            hid[:, a:b] = (act * up).astype(BF16)
            dg[slot, :, :, a:b] = (
                (gh * up * sg * (1.0 + gate * (1.0 - sg))).astype(BF16).reshape(shape)
            )
            du[slot, :, :, a:b] = (gh * act).astype(BF16).reshape(shape)
        h = hid[...]
        for a, b in lane_tiles(depth, 512):
            gdown[:, a:b] += mm(h, g[:, a:b], ta=True)
            down[slot, :, :, a:b] = (
                jnp.dot(h, w_down[:, a:b], preferred_element_type=F32)
                .astype(BF16)
                .reshape(blocks, rows, b - a)
            )
        for save in saves(q):
            save.start()

    ticks(chunks, p.n, scatter, gather, partial, middle, consume, also)
    w_down[...] = gdown[...].astype(BF16)
    gdown_save = pltpu.make_async_copy(w_down, gdown_hbm, dsem)
    gdown_save.start()
    lax.fori_loop(0, chunks - early, lambda q, _: later.drain(q), None)
    gdown_save.wait()
    for q in range(max(chunks - 2, 0), chunks):
        for save in saves(q):
            save.wait()


def chunk_rows(blocks, owned):
    return min(owned, max(16, 2048 // (blocks * blocks)))


def early_chunks(chunks, blocks):
    return chunks - 32 * chunks // (blocks * blocks)


ANY = pl.BlockSpec(memory_space=pl.ANY)
WHOLE = pl.BlockSpec(memory_space=pltpu.VMEM)


def ffn(mixed, w_out, inputs, gain, w_gate, w_up, w_down, cot, early):
    owned, depth = inputs.shape
    blocks = mixed.shape[0] // owned
    rows = chunk_rows(blocks, owned)
    chunks = owned // rows
    units = w_gate.shape[0]
    cut = lambda width: jax.ShapeDtypeStruct((blocks, chunks, rows, width), BF16)
    dma = pltpu.SemaphoreType.DMA
    return pl.pallas_call(
        ffn_kernel,
        in_specs=[WHOLE] * 4 + [ANY] * 3 + [WHOLE, ANY],
        out_specs=[WHOLE] + [ANY] * 5,
        out_shape=[
            jax.ShapeDtypeStruct((owned, depth), F32),
            cut(depth),
            cut(units),
            cut(units),
            cut(depth),
            jax.ShapeDtypeStruct((units, depth), BF16),
        ],
        scratch_shapes=ring_scratch(chunks, blocks, rows, depth)
        + gather_scratch(chunks, blocks, rows, depth)
        + gather_scratch(chunks - early_chunks(chunks, blocks), blocks, rows, depth)
        + [
            pltpu.VMEM(w_gate.shape, BF16),
            pltpu.VMEM(w_up.shape, BF16),
            pltpu.VMEM(w_down.shape, BF16),
            pltpu.VMEM((2, blocks, rows, depth), BF16),
            pltpu.VMEM((blocks * rows, units), BF16),
            pltpu.VMEM((2, blocks, rows, units), BF16),
            pltpu.VMEM((2, blocks, rows, units), BF16),
            pltpu.VMEM((2, blocks, rows, depth), BF16),
            pltpu.VMEM((units, depth), F32),
            pltpu.VMEM((rows, depth), F32),
            dma((3,)),
            dma((2,)),
            dma((2, 4)),
            dma,
        ],
        compiler_params=pltpu.CompilerParams(
            collective_id=1, has_side_effects=True, vmem_limit_bytes=63 * 1024 * 1024
        ),
        name="ffn_rounds",
    )(
        mixed.reshape(blocks, chunks, rows, -1),
        w_out,
        inputs,
        gain,
        w_gate,
        w_up,
        w_down,
        cot,
        early.reshape(blocks, -1, rows, depth),
    )


def back_kernel(
    dgate_ref, dup_ref, w_gate_ref, w_up_ref, resid_ref, gain_ref, cot_ref, w_out_ref, mixed_ref,
    gres_ref, ggain_ref, gout_ref, gm_hbm,
    own, stage, cross, line, xs, xr, ls, lr, held, gs, gr, gm, total, gout, osem,
):
    chunks, blocks, rows, depth = held.shape
    p = Place(blocks)
    scatter = Scatter(p, own, stage, cross, line, xs, xr, ls, lr)
    gather = Gather(p, held, gs, gr)
    p.greet()
    ggain_ref[...] = jnp.zeros_like(ggain_ref)

    def partial(q):
        g = dgate_ref[:, q].reshape(blocks * rows, -1)
        u = dup_ref[:, q].reshape(blocks * rows, -1)
        for a, b in lane_tiles(depth, 512):
            put_share(
                p,
                own,
                stage,
                q,
                mm(g, w_gate_ref[:, a:b]) + mm(u, w_up_ref[:, a:b]),
                a,
                b,
            )

    def middle(q):
        scatter.result(q, total)
        here = pl.ds(pl.multiple_of(q * rows, rows), rows)
        resid = resid_ref[here, :]
        n = lax.rsqrt(jnp.mean(resid * resid, axis=1, keepdims=True) + 1e-05)
        u = resid * n
        grad = total[...]
        ggain_ref[...] += jnp.sum((grad * u).reshape(rows // 8, 8, depth), axis=0)
        e = grad * gain_ref[...]
        gres = cot_ref[here, :].astype(F32) + n * (e - u * jnp.mean(e * u, axis=1, keepdims=True))
        gres_ref[here, :] = gres
        held[q, p.me] = gres.astype(BF16)

    def save(q):
        return pltpu.make_async_copy(gm.at[q % 2], gm_hbm.at[:, q], osem.at[q % 2])

    def consume(q):
        @pl.when(q >= 2)
        def _():
            save(q - 2).wait()

        @pl.when(q == 0)
        def _():
            gout[...] = jnp.zeros_like(gout)

        x = held[q].reshape(blocks * rows, depth)
        gm[q % 2] = mm(x, w_out_ref[...], tb=True).reshape(blocks, rows, -1)
        save(q).start()
        m = mixed_ref[:, q].reshape(blocks * rows, -1)
        for a, b in lane_tiles(depth, 512):
            gout[:, a:b] += mm(m, x[:, a:b], ta=True)

    ticks(chunks, p.n, scatter, gather, partial, middle, consume)
    for q in range(max(chunks - 2, 0), chunks):
        save(q).wait()
    gout_ref[...] = gout[...].astype(BF16)


def back(dgate, dup, w_gate, w_up, resid, gain, cot, w_out, mixed):
    blocks, chunks, rows, _ = dgate.shape
    owned, depth = resid.shape
    width = w_out.shape[0]
    dma = pltpu.SemaphoreType.DMA
    return pl.pallas_call(
        back_kernel,
        in_specs=[WHOLE] * 9,
        out_specs=[WHOLE, WHOLE, WHOLE, ANY],
        out_shape=[
            jax.ShapeDtypeStruct((owned, depth), F32),
            jax.ShapeDtypeStruct((8, depth), F32),
            jax.ShapeDtypeStruct((width, depth), BF16),
            jax.ShapeDtypeStruct((blocks, chunks, rows, width), F32),
        ],
        scratch_shapes=ring_scratch(chunks, blocks, rows, depth)
        + gather_scratch(chunks, blocks, rows, depth)
        + [
            pltpu.VMEM((2, blocks, rows, width), F32),
            pltpu.VMEM((rows, depth), F32),
            pltpu.VMEM((width, depth), F32),
            dma((2,)),
        ],
        compiler_params=pltpu.CompilerParams(
            collective_id=2, has_side_effects=True, vmem_limit_bytes=62 * 1024 * 1024
        ),
        name="back_rounds",
    )(
        dgate,
        dup,
        w_gate,
        w_up,
        resid,
        gain,
        cot,
        w_out,
        mixed.reshape(blocks, chunks, rows, width),
    )


def add_rows(out, left, right, count):
    size = 64 if count % 64 == 0 else 16

    def body(i, _):
        rows = lambda at: pl.ds(pl.multiple_of(at + i * size, 16), size)
        value = left[0][rows(left[1]), :].astype(F32) + right[0][rows(right[1]), :].astype(F32)
        out[0][rows(out[1]), :] = value.astype(out[0].dtype)
        return 0

    lax.fori_loop(0, count // size, body, 0)


class Reduce:
    def __init__(self, count, src, parts, done, out, ss, rr, load, save):
        self.src, self.parts, self.done, self.out = src, parts, done, out
        self.ss, self.rr, self.load_sem, self.save_sem = ss, rr, load, save
        self.bits = count.bit_length() - 1
        item = lax.axis_index("item")
        total = src.shape[0]
        self.plan = []
        for half in range(2):
            start = half * (total // 2)
            size = total // 2
            steps = []
            for k in range(self.bits):
                unit = 2 ** (k if half == 0 else self.bits - 1 - k)
                bit = (item // unit) % 2
                size //= 2
                keep = start + bit * size
                give = start + (1 - bit) * size
                steps.append((size, keep, give, bit * size, (1 - bit) * size, item + unit - 2 * unit * bit))
                start = keep
            self.plan.append(steps)

    def rows(self, ref, at, size):
        return ref.at[pl.ds(pl.multiple_of(at, 16), size)]

    def load(self, half):
        size, keep = self.plan[half][0][:2]
        return pltpu.make_async_copy(
            self.rows(self.src, keep, size), self.rows(self.done, keep, size), self.load_sem.at[half]
        )

    def down(self, half, k):
        size, _, give, _, local, partner = self.plan[half][k]
        source = self.rows(self.src, give, size) if k == 0 else self.rows(self.parts[k - 1].at[half], local, size)
        return pltpu.make_async_remote_copy(
            src_ref=source,
            dst_ref=self.parts[k].at[half],
            send_sem=self.ss.at[half, k],
            recv_sem=self.rr.at[half, k],
            device_id={"item": partner},
            device_id_type=MESH,
        )

    def up(self, half, k, back=False):
        size, keep, give, _, _, partner = self.plan[half][k]
        ref = self.rows(self.done, give if back else keep, size)
        return pltpu.make_async_remote_copy(
            src_ref=ref,
            dst_ref=ref,
            send_sem=self.ss.at[half, self.bits + k],
            recv_sem=self.rr.at[half, self.bits + k],
            device_id={"item": partner},
            device_id_type=MESH,
        )

    def start(self):
        for half in range(2):
            self.load(half).start()
            self.down(half, 0).start()

    def halve(self, k):
        for half in range(2):
            size, keep, _, local, _, _ = self.plan[half][k]
            if k == 0:
                self.load(half).wait()
                mine = (self.done, keep)
            else:
                mine = (self.parts[k - 1].at[half], local)
            self.down(half, k).wait_recv()
            part = (self.parts[k].at[half], 0)
            if k + 1 < self.bits:
                add_rows(part, mine, part, size)
                self.down(half, k + 1).start()
            else:
                add_rows((self.done, keep), mine, part, size)
                self.up(half, k).start()

    def double(self, k):
        for half in range(2):
            self.up(half, k, True).wait_recv()
            self.up(half, k - 1).start()

    def save(self):
        return pltpu.make_async_copy(self.done, self.out, self.save_sem)

    def finish(self):
        for half in range(2):
            self.up(half, 0, True).wait_recv()
        self.save().start()

    def drain(self):
        for half in range(2):
            for k in range(self.bits):
                self.down(half, k).wait_send()
                self.up(half, k).wait_send()
        self.save().wait()

    def handlers(self):
        return (
            [functools.partial(self.halve, k) for k in range(self.bits)]
            + [functools.partial(self.double, k) for k in range(self.bits - 1, 0, -1)]
            + [self.finish]
        )


def reduce_scratch(count, total, width):
    dma = pltpu.SemaphoreType.DMA
    bits = count.bit_length() - 1
    return [
        pltpu.VMEM((total, width), BF16),
        *[pltpu.VMEM((2, total // 2 ** (k + 2), width), BF16) for k in range(bits)],
        dma((2, 2 * bits)),
        dma((2, 2 * bits)),
        dma((2,)),
        dma,
    ]


class Peers:
    def __init__(self, axis, count, held, ss, rr):
        self.axis, self.count, self.held, self.ss, self.rr = axis, count, held, ss, rr
        self.me = lax.axis_index(axis)

    def other(self, k):
        return (self.me + k) % self.count

    def copy(self, slot, k):
        ref = self.held.at[slot]
        return pltpu.make_async_remote_copy(
            src_ref=ref,
            dst_ref=ref,
            send_sem=self.ss.at[k],
            recv_sem=self.rr.at[slot],
            device_id={self.axis: self.other(k)},
            device_id_type=MESH,
        )

    def greet(self):
        barrier = pltpu.get_barrier_semaphore()
        for k in range(1, self.count):
            pl.semaphore_signal(
                barrier, inc=1, device_id={self.axis: self.other(k)}, device_id_type=MESH
            )

    def send(self):
        for k in range(1, self.count):
            self.copy(self.me, k).start()

    def total(self):
        for k in range(1, self.count):
            self.copy(self.other(k), k).wait_recv()
        out = self.held[0]
        for slot in range(1, self.count):
            out = out + self.held[slot]
        return out

    def drain(self):
        for k in range(1, self.count):
            self.copy(self.me, k).wait_send()


def tail_kernel(
    gq_ref, gk_ref, gv_ref, gg_ref, gdw_ref, wq_ref, wk_ref, wv_ref, wg_ref, wdw_ref,
    input_ref, gain_ref, gres_ref, resid_ref, fgain_ref, ogain_ref, conv_ref, dl_ref, wide_ref, down_hbm,
    so_hbm,
    output_ref, igrad_ref, small_ref, ro_hbm,
    own, stage, cross, line, xs, xr, ls, lr, own2, cross2, line2, xs2, xr2, ls2, lr2, osem,
    total, ngain, held1, held2, s1, r1, s2, r2, *sums,
):
    chunks, n, rows, depth = cross.shape
    blocks = 2 * n
    p = Place(blocks)
    first = Scatter(p, own, stage, cross, line, xs, xr, ls, lr)
    first_late = chunks - cross2.shape[0]
    second = Late(p, down_hbm, first_late, own2, cross2, line2, xs2, xr2, ls2, lr2, osem)
    heads = Peers("head", held1.shape[0], held1, s1, r1)
    items = Peers("item", held2.shape[0], held2, s2, r2)
    heads.greet()
    items.greet()
    pl.semaphore_wait(pltpu.get_barrier_semaphore(), heads.count + items.count - 2)
    ngain[...] = jnp.zeros_like(ngain)
    width1 = held1.shape[2]
    half = conv_ref.shape[2] // 2
    held1[heads.me] = jnp.zeros(held1.shape[1:], F32)
    held2[items.me] = jnp.zeros(held2.shape[1:], F32)

    bits = items.count.bit_length() - 1
    pairs = ((so_hbm, ro_hbm),)
    each = len(sums) // len(pairs)
    reduces = []
    for i, (src, out) in enumerate(pairs):
        done, *rest = sums[i * each : (i + 1) * each]
        reduces.append(Reduce(items.count, src, rest[:bits], done, out, *rest[bits:]))
    for reduce in reduces:
        reduce.start()
    second.start()
    todo = [step for group in zip(*[reduce.handlers() for reduce in reduces]) for step in group]
    def finish_late(j):
        here = pl.ds(pl.multiple_of(j * rows, rows), rows)
        second.scatter.result(j, total)
        output_ref[here, :] = (resid_ref[here, :] + total[...]).astype(BF16)

    def partial(q):
        pairs = [
            (ref[:, q].reshape(blocks * rows, -1), w)
            for ref, w in ((gq_ref, wq_ref), (gk_ref, wk_ref), (gv_ref, wv_ref), (gg_ref, wg_ref))
        ]
        dw = gdw_ref[:, q].reshape(blocks * rows, -1)
        for a, b in lane_tiles(depth, 512):
            value = mm(dw, wdw_ref[:, a:b])
            for x, w in pairs:
                value = value + mm(x, w[a:b, :], tb=True)
            put_share(p, own, stage, q, value, a, b)

    partial(0)
    first.swap(0).start()

    def end(q):
        here = pl.ds(pl.multiple_of(q * rows, rows), rows)
        first.result(q, total)
        x = input_ref[here, :].astype(F32)
        scale = lax.rsqrt(jnp.mean(x * x, axis=1, keepdims=True) + 1e-05)
        u = x * scale
        grad = total[...]
        ngain[...] += jnp.sum((grad * u).reshape(rows // 8, 8, depth), axis=0)
        e = grad * gain_ref[...]
        igrad_ref[here, :] = gres_ref[here, :] + scale * (
            e - u * jnp.mean(e * u, axis=1, keepdims=True)
        )

    def turn(w, _):
        pl.when(within(w - n + 1, chunks))(lambda: end(w - n + 1))
        for s in range(n - 2, 0, -1):
            pl.when(within(w - s, chunks))(lambda: first.step(w - s, s))

        @pl.when(w < chunks)
        def _():
            first.swap(w).wait_recv()
            first.step(w, 0)

        second.tick(w, finish_late)

        @pl.when(w + 1 < chunks)
        def _():
            @pl.when(w >= 1)
            def _():
                first.swap(w - 1).wait_send()

            partial(w + 1)
            first.swap(w + 1).start()

        for i, step in enumerate(todo):
            pl.when(w == 1 + i * 9 // len(todo))(step)

        return 0

    lax.fori_loop(0, chunks + n - 1, turn, 0)
    part = depth // 8
    for at, ref in ((0, ngain), (part, fgain_ref)):
        row = jnp.sum(ref[...], axis=0, keepdims=True)
        for i in range(8):
            held1[heads.me, i : i + 1, at : at + part] = row[:, i * part : (i + 1) * part]
    row = jnp.sum(ogain_ref[...], axis=0, keepdims=True)
    for i in range(2):
        held1[heads.me, i : i + 1, 2 * part : 2 * part + 128] = row[:, i * 128 : (i + 1) * 128]
    heads.send()
    for j in range(4):
        row = jnp.sum(conv_ref[j], axis=0, keepdims=True)
        for i in range(2):
            held2[items.me, 4 * i + j : 4 * i + j + 1, width1 : width1 + half] = row[
                :, i * half : (i + 1) * half
            ]
    at = width1 + half + 128
    held2[items.me, 0:1, width1 + half : at] = dl_ref[...]
    held2[items.me, :, at:] = wide_ref[...]
    held2[items.me, :, 0:width1] = heads.total()
    items.send()

    def drain(q, _):
        first.drain(q)
        return 0

    lax.fori_loop(0, chunks, drain, 0)
    second.drain()
    for q in range(max(chunks - 2, 0), chunks):
        first.swap(q).wait_send()
    small_ref[...] = items.total()
    for reduce in reduces:
        reduce.drain()
    heads.drain()
    items.drain()


def tail(grads, weights, inputs, gain, gres, resid, fgain, ogain, gconv, gdl, wide, down, sums, items):
    blocks, chunks, rows, depth = down.shape
    owned = inputs.shape[0]
    n = blocks // 2
    cut = lambda value: value.reshape(blocks, chunks, rows, -1)
    width1 = depth // 4 + 128
    width2 = width1 + gconv.shape[2] // 2 + 128 + wide.size // 8
    gdl = jnp.pad(gdl, ((0, 0), (0, 128 - gdl.shape[1])))
    dma = pltpu.SemaphoreType.DMA
    one = ring_scratch(chunks, blocks, rows, depth)
    late = chunks - chunks // 2
    output, igrad, small, *sums = pl.pallas_call(
        tail_kernel,
        in_specs=[WHOLE] * 19 + [ANY] * 2,
        out_specs=[WHOLE] * 3 + [ANY],
        out_shape=[
            jax.ShapeDtypeStruct((late * rows, depth), BF16),
            jax.ShapeDtypeStruct((owned, depth), F32),
            jax.ShapeDtypeStruct((8, width2), F32),
            *[jax.ShapeDtypeStruct(value.shape, BF16) for value in sums],
        ],
        scratch_shapes=one
        + late_scratch(late, min(late, n), blocks, rows, depth)
        + [
            pltpu.VMEM((rows, depth), F32),
            pltpu.VMEM((8, depth), F32),
            pltpu.VMEM((blocks, 8, width1), F32),
            pltpu.VMEM((items, 8, width2), F32),
            dma((blocks,)),
            dma((blocks,)),
            dma((items,)),
            dma((items,)),
            *[part for value in sums for part in reduce_scratch(items, *value.shape)],
        ],
        compiler_params=pltpu.CompilerParams(
            collective_id=3, has_side_effects=True, vmem_limit_bytes=63 * 1024 * 1024
        ),
        name="tail_rounds",
    )(
        *[cut(value) for value in grads],
        *weights,
        inputs,
        gain,
        gres,
        resid[owned - late * rows :],
        fgain,
        ogain,
        gconv,
        gdl,
        wide.reshape(8, -1),
        down.reshape(n, 2, chunks, rows, depth),
        *sums,
    )
    part = depth // 8
    half = gconv.shape[2] // 2
    conv = small[:, width1 : width1 + half]
    return (
        output,
        igrad,
        small[:, :part].reshape(-1),
        small[:, part : 2 * part].reshape(-1),
        small[:2, 2 * part : 2 * part + 128].reshape(-1),
        jnp.concatenate([conv[:4], conv[4:]], axis=1),
        small[0, width1 + half : width1 + half + 128],
        small[:, width1 + half + 128 :].reshape(wide.shape),
        sums,
    )


def head_kernel(
    input_ref, gain_ref, cot_hbm, wq_ref, wk_ref, wv_ref, wg_ref, wdw_ref,
    dw_ref, early_hbm, group_hbm, q_hbm, k_hbm, v_hbm, g_hbm,
    held, gs, gr, pq, pk, pv, pg, gsem, osem, esem,
):
    chunks, blocks, rows, depth = held.shape
    p = Place(blocks)
    gather = Gather(p, held, gs, gr)
    early = pltpu.make_async_copy(cot_hbm.at[0 : early_hbm.shape[0]], early_hbm, esem)
    early.start()
    p.greet()
    for q in range(chunks):
        x = input_ref[q * rows : (q + 1) * rows, :].astype(F32)
        x = x * lax.rsqrt(jnp.mean(x * x, axis=1, keepdims=True) + 1e-05)
        held[q, p.me] = (x * gain_ref[...]).astype(BF16)
        gather.step(q, 0)

    def saves(q):
        slot = q % 2
        return [
            pltpu.make_async_copy(src.at[slot], dst.at[:, q], osem.at[slot, i])
            for i, (src, dst) in enumerate(((pq, q_hbm), (pk, k_hbm), (pv, v_hbm), (pg, g_hbm)))
        ]

    def group_save(q):
        return pltpu.make_async_copy(held.at[q], group_hbm.at[:, q], gsem.at[q])

    def consume(q):
        gather.finish(q)
        group_save(q).start()

        @pl.when(q >= 2)
        def _():
            for save in saves(q - 2):
                save.wait()

        x = held[q].reshape(blocks * rows, depth)
        for out, weight in ((pq, wq_ref), (pk, wk_ref), (pv, wv_ref), (pg, wg_ref)):
            for a, b in lane_tiles(weight.shape[1]):
                out[q % 2, :, :, a:b] = jnp.dot(
                    x, weight[:, a:b], preferred_element_type=F32
                ).reshape(blocks, rows, b - a)
        dw_ref[:, q] = mm(x, wdw_ref[...], tb=True).reshape(blocks, rows, -1)
        for save in saves(q):
            save.start()

    last = p.n - 1

    def turn(w, _):
        for s in range(1, p.n):

            @pl.when(jnp.logical_and(w >= s - 1, w - s + 1 < chunks))
            def _():
                gather.step(w - s + 1, s)

        @pl.when(w >= last)
        def _():
            consume(w - last)

        return 0

    lax.fori_loop(0, chunks + last, turn, 0)
    for q in range(max(chunks - 2, 0), chunks):
        for save in saves(q):
            save.wait()
    early.wait()

    def drain(q, _):
        gather.drain(q)
        group_save(q).wait()
        return 0

    lax.fori_loop(0, chunks, drain, 0)


def head(inputs, gain, cot, weights, thin, blocks):
    owned, depth = inputs.shape
    rows = chunk_rows(blocks, owned)
    chunks = owned // rows
    cut = lambda width, kind: jax.ShapeDtypeStruct((blocks, chunks, rows, width), kind)
    dma = pltpu.SemaphoreType.DMA
    return pl.pallas_call(
        head_kernel,
        in_specs=[WHOLE] * 2 + [ANY] + [WHOLE] * 5,
        out_specs=[WHOLE] + [ANY] * 6,
        out_shape=[
            cut(thin.shape[0], F32),
            jax.ShapeDtypeStruct((early_chunks(chunks, blocks) * rows, depth), BF16),
            cut(depth, BF16),
        ]
        + [cut(weight.shape[1], F32) for weight in weights],
        scratch_shapes=gather_scratch(chunks, blocks, rows, depth)
        + [pltpu.VMEM((2, blocks, rows, weight.shape[1]), F32) for weight in weights]
        + [dma((chunks,)), dma((2, 4)), pltpu.SemaphoreType.DMA],
        compiler_params=pltpu.CompilerParams(
            collective_id=4, has_side_effects=True, vmem_limit_bytes=62 * 1024 * 1024
        ),
        name="head_rounds",
    )(inputs, gain, cot, *weights, thin)


def inner_rows(left, right):
    return lax.dot_general(
        left, right, (((0,), (0,)), ((), ())), preferred_element_type=jnp.float32
    )


def gather(values):
    return lax.all_gather(values.astype(jnp.bfloat16), "head", axis=0, tiled=True)


def scatter(values):
    return lax.psum_scatter(values, "head", scatter_dimension=0, tiled=True)


def total(values):
    return lax.psum([value.astype(jnp.bfloat16) for value in values], "item")


def after(values, *earlier):
    return lax.optimization_barrier((values, earlier))[0]


def local(
    items,
    blocks,
    layer_input,
    lengths,
    norm_gain,
    w_query,
    w_key,
    w_value,
    w_outgate,
    w_decay,
    w_write,
    conv_query,
    conv_key,
    conv_value,
    decay_log,
    out_gain,
    w_out,
    ffn_gain,
    w_gate,
    w_up,
    w_down,
    cotangent,
):
    ng = norm_gain.astype(F32).reshape(1, -1)
    fg = ffn_gain.astype(F32).reshape(1, -1)
    og = out_gain.astype(F32).reshape(1, DV)
    conv = jnp.concatenate([conv_query, conv_key, conv_value], axis=1).astype(F32)
    dl = decay_log.reshape(1, -1)
    w_dw = jnp.concatenate([w_decay.T, w_write.T], axis=0)
    gate_t, up_t = w_gate.T, w_up.T
    owned, depth = layer_input.shape
    tokens = owned * blocks
    flat = lambda value: value.reshape(tokens, -1)
    by_seq = lambda value: value.reshape(-1, SEQ_LEN, value.shape[-1])
    raw_dw, early, group, *raw = head(
        layer_input, ng, cotangent, (w_query, w_key, w_value, w_outgate), w_dw, blocks
    )
    group = flat(group)
    early = gather(early)
    raw = [by_seq(flat(value)) for value in (*raw, raw_dw)]
    mixed, *kept = mixer_fwd(lengths, *raw, conv, dl, og)
    mixed = flat(mixed)
    resid, group_two, dgate, dup, down, grad_down = ffn(
        mixed, w_out, layer_input, fg, gate_t, up_t, w_down, cotangent, early
    )
    group_two = flat(group_two)
    ffn_sums = total(
        (
            grad_down,
            inner_rows(flat(dgate), group_two),
            inner_rows(flat(dup), group_two),
        )
    )
    grad_resid, fgain, grad_w_out, grad_mixed = back(
        dgate, dup, gate_t, up_t, resid, fg, cotangent, w_out, mixed
    )
    backward = mixer_bwd(
        lengths, *raw, conv, dl, og, by_seq(flat(grad_mixed)), *kept, by_seq(group), resid, down
    )
    grads, (gconv, gdl, ogain), wide, thin = backward[:5], backward[5:8], backward[8:12], backward[12]
    first = backward[13]
    mix_sums = total(after(list(wide), ffn_sums))
    wide = [grad_w_out]
    grads = [flat(value) for value in grads]
    output, input_grad, ngain, fgain, ogain, conv_grad, dl_grad, thin, sums = tail(
        grads,
        (w_query, w_key, w_value, w_outgate, w_dw),
        layer_input,
        ng,
        grad_resid,
        resid,
        fgain,
        ogain,
        gconv,
        gdl,
        thin,
        down,
        wide,
        items,
    )
    output = jnp.concatenate([first, output])
    heads = dl.shape[1]
    qw = w_query.shape[1]
    return (
        output,
        input_grad,
        ngain,
        *[value.astype(F32) for value in mix_sums],
        thin[:heads].T,
        thin[heads:].T,
        conv_grad[:, :qw],
        conv_grad[:, qw : 2 * qw],
        conv_grad[:, 2 * qw :],
        dl_grad[:heads],
        ogain,
        sums[0].astype(F32),
        fgain,
        ffn_sums[1].T.astype(F32),
        ffn_sums[2].T.astype(F32),
        ffn_sums[0].astype(F32),
    )


def solution(mesh):
    rows = P(("item", "head"), None)
    cols = P(None, "head")
    deep = P("head", None)
    return jax.shard_map(
        functools.partial(local, mesh.shape["item"], mesh.shape["head"]),
        mesh=mesh,
        in_specs=(rows, P("item"), P(), *[cols] * 9, P("head"), P(), deep, P(), cols, cols, deep, rows),
        out_specs=(rows, rows, P(), *[cols] * 9, P("head"), P(), deep, P(), cols, cols, deep),
        check_vma=False,
    )
```

```python
import functools

import jax
import jax.numpy as jnp
from jax import lax
from jax.experimental import pallas as pl
from jax.experimental.pallas import tpu as pltpu
from jax.sharding import PartitionSpec as P

DK = 128
DV = 256
SEQ_LEN = 1024
CHUNK = 128
F32 = jnp.float32
BF16 = jnp.bfloat16


def mm(left, right, ta=False, tb=False):
    return lax.dot_general(
        left.astype(BF16),
        right.astype(BF16),
        (((0 if ta else 1,), (1 if tb else 0,)), ((), ())),
        preferred_element_type=F32,
    )


def split(value):
    high = value.astype(BF16)
    return high, (value - high.astype(F32)).astype(BF16)


def mm3(left, right):
    lh, ll = left
    rh, rl = right
    return mm(lh, rh) + (mm(lh, rl) + mm(ll, rh))


def sigmoid(x):
    return 1.0 / (1.0 + jnp.exp(-x))


def grids():
    rows = lax.broadcasted_iota(jnp.int32, (CHUNK, CHUNK), 0)
    cols = lax.broadcasted_iota(jnp.int32, (CHUNK, CHUNK), 1)
    return rows, cols


def to_row(col, eye):
    return jnp.sum(jnp.where(eye, col, 0.0), axis=0, keepdims=True)


def inverses(mats, rows, cols):
    eye = jnp.where(rows == cols, 1.0, 0.0)
    near = rows // 8 == cols // 8
    n1 = [jnp.where(near, -a, 0.0) for a in mats]
    n1s = [split(n) for n in n1]
    n2 = [mm3(n, n) for n in n1s]
    n2s = [split(n) for n in n2]
    n3 = [mm3(a, b) for a, b in zip(n1s, n2s)]
    n4s = [split(mm3(n, n)) for n in n2s]
    p1 = [eye + a + b + c for a, b, c in zip(n1, n2, n3)]
    x = [p + mm3(split(p), n) for p, n in zip(p1, n4s)]
    size = 8
    while size < CHUNK:
        pair = (rows // (2 * size) == cols // (2 * size)) & (rows // size != cols // size)
        xs = [v.astype(BF16) for v in x]
        bx = [mm(jnp.where(pair, a, 0.0), v) for a, v in zip(mats, xs)]
        x = [v - mm(vs, w) for v, vs, w in zip(x, xs, bx)]
        size *= 2
    return x


def decays(ld, eye, causal):
    row = to_row(ld, eye)
    g = jnp.sum(jnp.where(causal, row, 0.0), axis=1, keepdims=True)
    grow = to_row(g, eye)
    d = jnp.where(causal, jnp.exp(jnp.where(causal, g - grow, 0.0)), 0.0)
    last = g[CHUNK - 1 : CHUNK, :]
    return d, jnp.exp(g), jnp.exp(last - g), jnp.exp(last)


def live_mask(len_ref, s, c):
    spot = lax.broadcasted_iota(jnp.int32, (CHUNK, 1), 0) + c * CHUNK
    return jnp.where(spot < len_ref[s], 1.0, 0.0)


def softplus(x):
    return jnp.maximum(x, 0.0) + jnp.log1p(jnp.exp(-jnp.abs(x)))


def mix_fwd_kernel(
    len_ref, q_ref, k_ref, v_ref, g_ref, dw_ref, conv_ref, dl_ref, gain_ref,
    mixed_ref, pre_ref, o_ref, u_ref, t_ref, s_ref, buf, state,
):
    c = pl.program_id(0)
    seqs, _, raws = buf.shape
    heads = dl_ref.shape[1]
    qw = heads * DK
    pieces = ((q_ref, 0, qw), (k_ref, qw, 2 * qw), (v_ref, 2 * qw, raws))

    @pl.when(c == 0)
    def _():
        buf[:, 0:8, :] = jnp.zeros((seqs, 8, raws), F32)
        state[...] = jnp.zeros_like(state)

    rows, cols = grids()
    eye = rows == cols
    causal = rows >= cols
    lower = rows > cols
    rate = jnp.exp(dl_ref[...])
    st = []
    for s in range(seqs):
        for ref, a, b in pieces:
            buf[s, 8 : 8 + CHUNK, a:b] = ref[s]
        pre = conv_ref[0:1, :] * buf[s, 5 : 5 + CHUNK, :]
        for j in range(1, 4):
            pre = pre + conv_ref[j : j + 1, :] * buf[s, 5 + j : 5 + j + CHUNK, :]
        pre_ref[s] = pre
        buf[s, 0:8, :] = buf[s, CHUNK : CHUNK + 8, :]
        act = pre * sigmoid(pre)
        mask = live_mask(len_ref, s, c)
        x = dw_ref[s]
        ld2 = -rate * softplus(x[:, :heads]) * mask
        be2 = sigmoid(x[:, heads:]) * mask
        for h in range(heads):
            q = act[:, h * DK : (h + 1) * DK]
            k = act[:, qw + h * DK : qw + (h + 1) * DK]
            v = act[:, 2 * qw + h * DV : 2 * qw + (h + 1) * DV]
            q = q * (lax.rsqrt(jnp.sum(q * q, axis=1, keepdims=True) + 1e-06) * DK ** (-0.5))
            k = k * lax.rsqrt(jnp.sum(k * k, axis=1, keepdims=True) + 1e-06)
            be = be2[:, h : h + 1]
            d, ga, e, el = decays(ld2[:, h : h + 1], eye, causal)
            qb = q.astype(BF16)
            kb = k.astype(BF16)
            qk = jnp.concatenate([qb, kb], axis=0)
            both = mm(qk, kb, tb=True)
            w = d * both[:CHUNK]
            a = jnp.where(lower, d * both[CHUNK:], 0.0) * be
            st.append((s, h, mask, v, be, ga, e, el, qk, kb, w, a))
    inv = inverses([z[-1] for z in st], rows, cols)
    for i, (s, h, mask, v, be, ga, e, el, qk, kb, w, a) in enumerate(st):
        t = inv[i].astype(BF16)
        old = state[i]
        oldb = old.astype(BF16)
        s_ref[i] = oldb
        t_ref[i] = t
        qks = mm(qk, oldb)
        r = be * (v - ga * qks[CHUNK:])
        u = mm(t, r)
        ub = u.astype(BF16)
        u_ref[s, :, h * DV : (h + 1) * DV] = ub
        o = ga * qks[:CHUNK] + mm(w, ub)
        state[i] = el * old + mm(kb, e * u, ta=True)
        o = o * mask
        o_ref[s, :, h * DV : (h + 1) * DV] = o
        rg = g_ref[s, :, h * DV : (h + 1) * DV]
        n = o * lax.rsqrt(jnp.mean(o * o, axis=1, keepdims=True) + 1e-05) * gain_ref[...]
        mixed_ref[s, :, h * DV : (h + 1) * DV] = (n * (rg * sigmoid(rg))).astype(BF16)


def mix_bwd_kernel(
    items, len_ref, q_ref, k_ref, v_ref, g_ref, dw_ref, conv_ref, dl_ref, gain_ref,
    gm_ref, pre_ref, o_ref, u_ref, t_ref, s_ref, group_ref, resid_ref, down_hbm, so_hbm,
    gq_ref, gk_ref, gv_ref, gg_ref, gdw_ref, gconv_ref, gdl_ref, ggain_ref,
    wq_ref, wk_ref, wv_ref, wg_ref, thin_ref, output_ref, ro_hbm, buf, dstate, weights,
    own, cross, line, xs, xr, ls, lr, osem, total, done, *sums,
):
    step = pl.program_id(0)
    c = pl.num_programs(0) - 1 - step
    place = Place(2 * cross.shape[1])
    summing = Late(place, down_hbm, 0, own, cross, line, xs, xr, ls, lr, osem)

    bits = items.bit_length() - 1
    reduce = Reduce(items, so_hbm, sums[:bits], done, ro_hbm, *sums[bits:])

    @pl.when(step == 0)
    def _():
        place.greet(items)
        reduce.start()
        summing.start()

    steps = reduce.handlers()
    for i, handler in enumerate(steps):
        at = SEQ_LEN // CHUNK - 1 if i == len(steps) - 1 else SEQ_LEN // CHUNK - 1 - len(steps) + i
        pl.when(step == at)(handler)

    def add_output(q):
        rows = total.shape[0]
        here = pl.ds(pl.multiple_of(q * rows, rows), rows)
        summing.scatter.result(q, total)
        output_ref[here, :] = (resid_ref[here, :] + total[...]).astype(BF16)

    total_ticks = cross.shape[0] + place.n - 1
    spans = SEQ_LEN // CHUNK - 1

    @pl.when(step >= 1)
    def _():
        def tick(w, _):
            summing.tick(w, add_output)
            return 0

        first = ((step - 1) * total_ticks + spans - 1) // spans
        lax.fori_loop(first, (step * total_ticks + spans - 1) // spans, tick, 0)

    seqs, _, raws = buf.shape
    heads = dl_ref.shape[1]
    qw = heads * DK
    pieces = ((q_ref, 0, qw), (k_ref, qw, 2 * qw), (v_ref, 2 * qw, raws))

    @pl.when(step == 0)
    def _():
        buf[:, CHUNK : CHUNK + 8, :] = jnp.zeros((seqs, 8, raws), F32)
        dstate[...] = jnp.zeros_like(dstate)
        gconv_ref[...] = jnp.zeros_like(gconv_ref)
        gdl_ref[...] = jnp.zeros_like(gdl_ref)
        ggain_ref[...] = jnp.zeros_like(ggain_ref)
        weights[...] = jnp.zeros_like(weights)
        thin_ref[...] = jnp.zeros_like(thin_ref)

    rows, cols = grids()
    eye = rows == cols
    causal = rows >= cols
    lower = rows > cols
    later = rows <= cols
    rate = jnp.exp(dl_ref[...])
    gain = gain_ref[...]
    for s in range(seqs):
        mask = live_mask(len_ref, s, c)
        x = dw_ref[s]
        soft = -rate * mask
        ld2 = soft * softplus(x[:, :heads])
        sg = sigmoid(x)
        be2 = sg[:, heads:] * mask
        dlds = []
        dbes = []
        for h in range(heads):
            i = heads * s + h
            vs = slice(h * DV, (h + 1) * DV)
            gm = gm_ref[s, :, vs]
            o = o_ref[s, :, vs]
            rg = g_ref[s, :, h * DV : (h + 1) * DV]
            sr = sigmoid(rg)
            r = lax.rsqrt(jnp.mean(o * o, axis=1, keepdims=True) + 1e-05)
            un = o * r
            gsg = gm * sr
            gg_ref[s, :, h * DV : (h + 1) * DV] = (
                gsg * (un * gain) * (1.0 + rg * (1.0 - sr))
            ).astype(BF16)
            dn = gsg * rg
            dnu = dn * un
            ggain_ref[...] += jnp.sum(dnu.reshape(CHUNK // 8, 8, DV), axis=0)
            do = (r * mask) * (dn * gain - un * jnp.mean(dnu * gain, axis=1, keepdims=True))
            pq = pre_ref[s, :, h * DK : (h + 1) * DK]
            pk = pre_ref[s, :, qw + h * DK : qw + (h + 1) * DK]
            pv = pre_ref[s, :, 2 * qw + h * DV : 2 * qw + (h + 1) * DV]
            sq = sigmoid(pq)
            sk = sigmoid(pk)
            sv = sigmoid(pv)
            q = pq * sq
            k = pk * sk
            v = pv * sv
            rq = lax.rsqrt(jnp.sum(q * q, axis=1, keepdims=True) + 1e-06)
            rk = lax.rsqrt(jnp.sum(k * k, axis=1, keepdims=True) + 1e-06)
            q = q * rq
            k = k * rk
            scale = DK ** (-0.5)
            be = be2[:, h : h + 1]
            d, ga, e, el = decays(ld2[:, h : h + 1], eye, causal)
            qb = (q * scale).astype(BF16)
            kb = k.astype(BF16)
            qk = jnp.concatenate([qb, kb], axis=0)
            both = mm(qk, kb, tb=True)
            w = d * both[:CHUNK]
            ab = jnp.where(lower, d * both[CHUNK:], 0.0)
            a = ab * be
            t = t_ref[i]
            st = s_ref[i]
            u = u_ref[s, :, vs]
            dh = dstate[i]
            dhb = dh.astype(BF16)
            qks = mm(qk, st)
            dob = do.astype(BF16)
            kdh = e * mm(kb, dhb)
            ubar = mm(w, dob, ta=True) + kdh
            rbar = mm(t, ubar, ta=True)
            rb = rbar.astype(BF16)
            uu = mm(jnp.concatenate([dob, rb], axis=0), u, tb=True)
            wbar = jnp.where(causal, uu[:CHUNK], 0.0)
            abar = -jnp.where(lower, uu[CHUNK:], 0.0)
            gks = ga * qks[CHUNK:]
            dv = be * rbar
            y = -ga * dv
            z = ga * do
            zy = jnp.concatenate([z.astype(BF16), y.astype(BF16)], axis=0)
            zys = mm(zy, st, tb=True)
            p = (wbar * d).astype(BF16)
            m = abar * d * be
            eu = e * u.astype(F32)
            dq = zys[:CHUNK] + mm(p, kb)
            dk = (
                zys[CHUNK:]
                + mm(p, qb, ta=True)
                + mm(m, kb)
                + mm(m, kb, ta=True)
                + mm(eu, dhb, tb=True)
            )
            dstate[i] = el * dh + mm(qk, zy, ta=True)
            ee = wbar * w + abar * a
            f = jnp.sum(u.astype(F32) * kdh, axis=1, keepdims=True)
            dbe = jnp.sum(rbar * (v - gks), axis=1, keepdims=True) + jnp.sum(
                abar * ab, axis=1, keepdims=True
            )
            dgc = (
                jnp.sum(ee, axis=1, keepdims=True)
                + jnp.sum(z * qks[:CHUNK] - dv * gks, axis=1, keepdims=True)
                - f
            )
            dgr = to_row(dgc, eye) - jnp.sum(ee, axis=0, keepdims=True)
            total = jnp.sum(f, axis=0, keepdims=True) + el * jnp.sum(
                jnp.sum(st.astype(F32) * dh, axis=1, keepdims=True), axis=0, keepdims=True
            )
            dld = jnp.sum(jnp.where(later, dgr, 0.0), axis=1, keepdims=True) + total
            dlds.append(dld)
            dbes.append(dbe)
            dq = dq * scale
            dqa = rq * (dq - q * jnp.sum(q * dq, axis=1, keepdims=True))
            dka = rk * (dk - k * jnp.sum(k * dk, axis=1, keepdims=True))
            buf[s, 0:CHUNK, h * DK : (h + 1) * DK] = dqa * sq * (1.0 + pq * (1.0 - sq))
            buf[s, 0:CHUNK, qw + h * DK : qw + (h + 1) * DK] = dka * sk * (1.0 + pk * (1.0 - sk))
            buf[s, 0:CHUNK, 2 * qw + h * DV : 2 * qw + (h + 1) * DV] = dv * sv * (1.0 + pv * (1.0 - sv))
        dld2 = jnp.concatenate(dlds, axis=1) if heads > 1 else dlds[0]
        dbe2 = jnp.concatenate(dbes, axis=1) if heads > 1 else dbes[0]
        gdw_ref[s] = jnp.concatenate(
            [dld2 * soft * sg[:, :heads], dbe2 * be2 * (1.0 - sg[:, heads:])], axis=1
        ).astype(BF16)
        gdl_ref[...] += jnp.sum(dld2 * ld2, axis=0, keepdims=True)
        for (ref, a, b), out in zip(pieces, (gq_ref, gk_ref, gv_ref)):
            raw = ref[s]
            draw = None
            for j in range(4):
                shifted = buf[s, 3 - j : 3 - j + CHUNK, a:b]
                gconv_ref[j, :, a:b] += jnp.sum(
                    (raw * shifted).reshape(CHUNK // 8, 8, b - a), axis=0
                )
                term = conv_ref[j : j + 1, a:b] * shifted
                draw = term if draw is None else draw + term
            out[s] = draw.astype(BF16)
        buf[s, CHUNK : CHUNK + 8, :] = buf[s, 0:8, :]
    x = group_ref[...].reshape(seqs * CHUNK, -1)
    flat = lambda ref: ref[...].reshape(seqs * CHUNK, -1)
    joined = jnp.concatenate([flat(ref) for ref in (gq_ref, gk_ref, gv_ref, gg_ref)], axis=1)
    for a in range(0, x.shape[1], 256):
        weights[a : a + 256, :] += mm(x[:, a : a + 256], joined, ta=True)
    thin_ref[...] += mm(gdw_ref[...].reshape(seqs * CHUNK, -1), x, ta=True)

    @pl.when(c == 0)
    def _():
        at = 0
        for out in (wq_ref, wk_ref, wv_ref, wg_ref):
            out[...] = weights[:, at : at + out.shape[1]].astype(BF16)
            at += out.shape[1]

        summing.drain()
        reduce.drain()


def mixer_fwd(lengths, q, k, v, g, dw, conv, dl, gain):
    count = SEQ_LEN // CHUNK
    seqs = q.shape[0]
    heads = dl.shape[1]
    raws, vw, n = conv.shape[1], heads * DV, seqs * heads
    full = lambda shape: pl.BlockSpec(shape, lambda c: (0,) * len(shape))
    seq = lambda width: pl.BlockSpec((seqs, CHUNK, width), lambda c: (0, c, 0))
    return pl.pallas_call(
        mix_fwd_kernel,
        grid=(count,),
        in_specs=[
            pl.BlockSpec(memory_space=pltpu.SMEM),
            seq(q.shape[2]),
            seq(k.shape[2]),
            seq(vw),
            seq(vw),
            seq(2 * heads),
            full((4, raws)),
            full((1, heads)),
            full((1, DV)),
        ],
        out_specs=[
            seq(vw),
            seq(raws),
            seq(vw),
            seq(vw),
            pl.BlockSpec((n, None, CHUNK, CHUNK), lambda c: (0, c, 0, 0)),
            pl.BlockSpec((n, None, DK, DV), lambda c: (0, c, 0, 0)),
        ],
        out_shape=[
            jax.ShapeDtypeStruct((seqs, SEQ_LEN, vw), BF16),
            jax.ShapeDtypeStruct((seqs, SEQ_LEN, raws), F32),
            jax.ShapeDtypeStruct((seqs, SEQ_LEN, vw), F32),
            jax.ShapeDtypeStruct((seqs, SEQ_LEN, vw), BF16),
            jax.ShapeDtypeStruct((n, count, CHUNK, CHUNK), BF16),
            jax.ShapeDtypeStruct((n, count, DK, DV), BF16),
        ],
        scratch_shapes=[
            pltpu.VMEM((seqs, CHUNK + 8, raws), F32),
            pltpu.VMEM((n, DK, DV), F32),
        ],
        compiler_params=pltpu.CompilerParams(
            dimension_semantics=("arbitrary",), vmem_limit_bytes=48 * 1024 * 1024
        ),
        name="mixer_forward",
    )(lengths, q, k, v, g, dw, conv, dl, gain)


def mixer_bwd(lengths, q, k, v, g, dw, conv, dl, gain, gm, pre, o, u, t, s, group, resid, down, grad_out, items):
    count = SEQ_LEN // CHUNK
    seqs = q.shape[0]
    heads = dl.shape[1]
    raws, vw, n = conv.shape[1], heads * DV, seqs * heads
    depth = group.shape[2]
    blocks, chunks, rows, _ = down.shape
    early = 3 * chunks // 4
    wide = [(depth, value.shape[2]) for value in (q, k, v, g)] + [(dw.shape[2], depth)]
    full = lambda shape: pl.BlockSpec(shape, lambda c: (0,) * len(shape))
    seq = lambda width: pl.BlockSpec((seqs, CHUNK, width), lambda c: (0, count - 1 - c, 0))
    return pl.pallas_call(
        functools.partial(mix_bwd_kernel, items),
        grid=(count,),
        in_specs=[
            pl.BlockSpec(memory_space=pltpu.SMEM),
            seq(q.shape[2]),
            seq(k.shape[2]),
            seq(vw),
            seq(vw),
            seq(2 * heads),
            full((4, raws)),
            full((1, heads)),
            full((1, DV)),
            seq(vw),
            seq(raws),
            seq(vw),
            seq(vw),
            pl.BlockSpec((n, None, CHUNK, CHUNK), lambda c: (0, count - 1 - c, 0, 0)),
            pl.BlockSpec((n, None, DK, DV), lambda c: (0, count - 1 - c, 0, 0)),
            seq(group.shape[2]),
            full((early * rows, depth)),
            pl.BlockSpec(memory_space=pl.ANY),
            pl.BlockSpec(memory_space=pl.ANY),
        ],
        out_specs=[
            seq(q.shape[2]),
            seq(k.shape[2]),
            seq(vw),
            seq(vw),
            seq(2 * heads),
            full((4, 8, raws)), full((1, heads)),
            full((8, DV)),
            *[full(shape) for shape in wide],
            full((early * rows, depth)),
            pl.BlockSpec(memory_space=pl.ANY),
        ],
        out_shape=[
            jax.ShapeDtypeStruct(q.shape, BF16),
            jax.ShapeDtypeStruct(k.shape, BF16),
            jax.ShapeDtypeStruct(v.shape, BF16),
            jax.ShapeDtypeStruct(g.shape, BF16),
            jax.ShapeDtypeStruct(dw.shape, BF16),
            jax.ShapeDtypeStruct((4, 8, raws), F32),
            jax.ShapeDtypeStruct((1, heads), F32),
            jax.ShapeDtypeStruct((8, DV), F32),
            *[jax.ShapeDtypeStruct(shape, BF16) for shape in wide[:4]],
            jax.ShapeDtypeStruct(wide[4], F32),
            jax.ShapeDtypeStruct((early * rows, depth), BF16),
            jax.ShapeDtypeStruct(grad_out.shape, BF16),
        ],
        scratch_shapes=[
            pltpu.VMEM((seqs, CHUNK + 8, raws), F32),
            pltpu.VMEM((n, DK, DV), F32),
            pltpu.VMEM((depth, sum(shape[1] for shape in wide[:4])), F32),
            *late_scratch(early, min(early, blocks // 2), blocks, rows, depth),
            pltpu.VMEM((rows, depth), F32),
            *reduce_scratch(items, *grad_out.shape),
        ],
        compiler_params=pltpu.CompilerParams(
            dimension_semantics=("arbitrary",),
            vmem_limit_bytes=62 * 1024 * 1024,
            collective_id=5,
            has_side_effects=True,
        ),
        name="mixer_backward",
    )(
        lengths,
        q,
        k,
        v,
        g,
        dw,
        conv,
        dl,
        gain,
        gm,
        pre,
        o,
        u,
        t,
        s,
        group,
        resid,
        down.reshape(blocks // 2, 2, chunks, rows, depth),
        grad_out,
    )


MESH = pl.DeviceIdType.MESH


class Place:
    def __init__(self, blocks):
        head = lax.axis_index("head")
        self.n = blocks // 2
        self.me = head
        self.z = head // 2
        self.c = head % 2
        self.mate = 2 * self.z + 1 - self.c
        self.right = head + 2
        self.left = head - 2
        self.has_right = self.z < self.n - 1
        self.has_left = self.z > 0

    def greet(self, items=1):
        barrier = pltpu.get_barrier_semaphore()
        item = lax.axis_index("item")
        for k in range(1, items):
            pl.semaphore_signal(
                barrier, inc=1, device_id={"item": (item + k) % items}, device_id_type=MESH
            )

        def hello(device):
            pl.semaphore_signal(barrier, inc=1, device_id={"head": device}, device_id_type=MESH)

        hello(self.mate)
        pl.when(self.has_right)(lambda: hello(self.right))
        pl.when(self.has_left)(lambda: hello(self.left))
        n = self.n
        pl.semaphore_wait(barrier, items + (self.z + n - 1) // n + (2 * n - 2 - self.z) // n)


def remote(src, dst, send, recv, device):
    return pltpu.make_async_remote_copy(
        src_ref=src,
        dst_ref=dst,
        send_sem=send,
        recv_sem=recv,
        device_id={"head": device},
        device_id_type=MESH,
    )


class Scatter:
    def __init__(self, place, own, stage, cross, line, xs, xr, ls, lr):
        self.p = place
        self.own, self.stage, self.cross, self.line = own, stage, cross, line
        self.xs, self.xr, self.ls, self.lr = xs, xr, ls, lr

    def swap(self, q):
        return remote(
            self.stage, self.cross.at[q], self.xs.at[q], self.xr.at[q], self.p.mate
        )

    def hop(self, q, slot, device):
        ref = self.line.at[q, slot]
        return remote(ref, ref, self.ls.at[q, slot], self.lr.at[q, slot], device)

    def share(self, q, t):
        return self.own[q % self.own.shape[0], t].astype(F32) + self.cross[q, t].astype(F32)

    def pass_on(self, q, t, slot, first, device):
        @pl.when(first)
        def _():
            self.line[q, slot] = self.share(q, t).astype(BF16)

        @pl.when(jnp.logical_not(first))
        def _():
            self.hop(q, slot, device).wait_recv()
            self.line[q, slot] = (self.share(q, t) + self.line[q, slot].astype(F32)).astype(BF16)

        self.hop(q, slot, device).start()

    def right_at(self, s):
        return self.p.n - 1 - s + self.p.z

    def left_at(self, s):
        n = self.p.n
        t = s + 1 - n + self.p.z
        return t, (t + n) % (n + 1)

    def step(self, q, s):
        p = self.p

        @pl.when(p.z <= s)
        def _():
            t = self.right_at(s)
            self.pass_on(q, t, t, p.z == 0, p.right)

        @pl.when(p.n - 1 - p.z <= s)
        def _():
            t, slot = self.left_at(s)
            self.pass_on(q, t, slot, p.z == p.n - 1, p.left)

    def result(self, q, total):
        p = self.p
        total[...] = self.share(q, p.z)

        @pl.when(p.has_left)
        def _():
            self.hop(q, p.z, p.right).wait_recv()
            total[...] += self.line[q, p.z].astype(F32)

        @pl.when(p.has_right)
        def _():
            slot = (p.z + p.n) % (p.n + 1)
            self.hop(q, slot, p.left).wait_recv()
            total[...] += self.line[q, slot].astype(F32)

    def drain(self, q):
        p = self.p
        for s in range(p.n - 1):

            @pl.when(p.z <= s)
            def _():
                self.hop(q, self.right_at(s), p.right).wait_send()

            @pl.when(p.n - 1 - p.z <= s)
            def _():
                self.hop(q, self.left_at(s)[1], p.left).wait_send()


class Late:
    def __init__(self, place, src, first, own, cross, line, xs, xr, ls, lr, osem):
        self.p, self.src, self.first = place, src, first
        self.count = cross.shape[0]
        self.own, self.cross, self.osem = own, cross, osem
        self.xs, self.xr = xs, xr
        self.scatter = Scatter(place, own, None, cross, line, xs, xr, ls, lr)

    def swap(self, q):
        return remote(
            self.src.at[:, 1 - self.p.c, self.first + q],
            self.cross.at[q],
            self.xs.at[q],
            self.xr.at[q],
            self.p.mate,
        )

    def load(self, q):
        slot = q % self.own.shape[0]
        return pltpu.make_async_copy(
            self.src.at[:, self.p.c, self.first + q], self.own.at[slot], self.osem.at[slot]
        )

    def start(self):
        for q in range(self.count):
            self.swap(q).start()
        for q in range(self.own.shape[0]):
            self.load(q).start()

    def enter(self, q):
        self.load(q).wait()
        self.swap(q).wait_recv()
        self.scatter.step(q, 0)

    def tick(self, w, result):
        n = self.p.n

        @pl.when(within(w - n + 1, self.count))
        def _():
            result(w - n + 1)
            slots = self.own.shape[0]

            @pl.when(w - n + 1 + slots < self.count)
            def _():
                self.load(w - n + 1 + slots).start()

        for s in range(n - 2, 0, -1):

            @pl.when(within(w - s, self.count))
            def _():
                self.scatter.step(w - s, s)

        @pl.when(w < self.count)
        def _():
            self.enter(w)

    def drain(self):
        def body(q, _):
            self.scatter.drain(q)
            self.swap(q).wait_send()
            return 0

        lax.fori_loop(0, self.count, body, 0)


def late_scratch(count, slots, blocks, rows, depth):
    n = blocks // 2
    dma = pltpu.SemaphoreType.DMA
    return [
        pltpu.VMEM((slots, n, rows, depth), BF16),
        pltpu.VMEM((count, n, rows, depth), BF16),
        pltpu.VMEM((count, n + 1, rows, depth), BF16),
        dma((count,)),
        dma((count,)),
        dma((count, n + 1)),
        dma((count, n + 1)),
        dma((slots,)),
    ]


class Gather:
    def __init__(self, place, held, ss, rr):
        self.p, self.held, self.ss, self.rr = place, held, ss, rr

    def copy(self, q, kind, z):
        p = self.p
        block = 2 * z + p.c
        ref = self.held.at[q, block]
        device = (p.right, p.left, p.mate)[kind]
        return remote(ref, ref, self.ss.at[q, kind, z], self.rr.at[q, block], device)

    def step(self, q, s):
        p = self.p
        if s == 0:
            pl.when(p.has_right)(lambda: self.copy(q, 0, p.z).start())
            pl.when(p.has_left)(lambda: self.copy(q, 1, p.z).start())
            self.copy(q, 2, p.z).start()
            return

        @pl.when(p.z >= s)
        def _():
            z = p.z - s
            self.copy(q, 0, z).wait_recv()
            pl.when(p.has_right)(lambda: self.copy(q, 0, z).start())
            self.copy(q, 2, z).start()

        @pl.when(p.z + s <= p.n - 1)
        def _():
            z = p.z + s
            self.copy(q, 1, z).wait_recv()
            pl.when(p.has_left)(lambda: self.copy(q, 1, z).start())
            self.copy(q, 2, z).start()

    def finish(self, q):
        p = self.p
        for z in range(p.n):
            block = 2 * z + 1 - p.c
            ref = self.held.at[q, block]
            remote(ref, ref, self.ss.at[q, 2, z], self.rr.at[q, block], p.mate).wait_recv()

    def drain(self, q):
        p = self.p
        for z in range(p.n):
            self.copy(q, 2, z).wait_send()

            @pl.when(jnp.logical_and(p.has_right, p.z >= z))
            def _():
                self.copy(q, 0, z).wait_send()

            @pl.when(jnp.logical_and(p.has_left, p.z <= z))
            def _():
                self.copy(q, 1, z).wait_send()


def lane_tiles(width, size=256):
    return [(at, min(at + size, width)) for at in range(0, width, size)]


def put_share(place, own, stage, q, values, a, b):
    slots, n, rows, _ = own.shape
    parts = values.astype(BF16).reshape(n, 2, rows, b - a)

    @pl.when(place.c == 0)
    def _():
        own[q % slots, :, :, a:b] = parts[:, 0]
        stage[:, :, a:b] = parts[:, 1]

    @pl.when(place.c == 1)
    def _():
        own[q % slots, :, :, a:b] = parts[:, 1]
        stage[:, :, a:b] = parts[:, 0]


def ring_scratch(chunks, blocks, rows, depth):
    n = blocks // 2
    dma = pltpu.SemaphoreType.DMA
    return [
        pltpu.VMEM((min(chunks, n), n, rows, depth), BF16),
        pltpu.VMEM((n, rows, depth), BF16),
        pltpu.VMEM((chunks, n, rows, depth), BF16),
        pltpu.VMEM((chunks, n + 1, rows, depth), BF16),
        dma((chunks,)),
        dma((chunks,)),
        dma((chunks, n + 1)),
        dma((chunks, n + 1)),
    ]


def gather_scratch(chunks, blocks, rows, depth):
    dma = pltpu.SemaphoreType.DMA
    return [
        pltpu.VMEM((chunks, blocks, rows, depth), BF16),
        dma((chunks, 3, blocks // 2)),
        dma((chunks, blocks)),
    ]


def within(q, chunks):
    return jnp.logical_and(q >= 0, q < chunks)


def ticks(chunks, n, scatter, gather, partial, middle, consume, also=None):
    partial(0)
    scatter.swap(0).start()

    def tick(w, _):
        v = w - n + 1

        @pl.when(within(v, chunks))
        def _():
            middle(v)
            gather.step(v, 0)

        for s in range(n - 2, 0, -1):

            @pl.when(within(w - s, chunks))
            def _():
                scatter.step(w - s, s)

        @pl.when(w < chunks)
        def _():
            scatter.swap(w).wait_recv()
            scatter.step(w, 0)

        for s in range(n - 1, 0, -1):

            @pl.when(within(v - s, chunks))
            def _():
                gather.step(v - s, s)

        if also is not None:
            also(w)

        @pl.when(w + 1 < chunks)
        def _():
            scatter.swap(w).wait_send()
            partial(w + 1)
            scatter.swap(w + 1).start()

        @pl.when(v >= n - 1)
        def _():
            gather.finish(v - n + 1)
            consume(v - n + 1)

        return 0

    lax.fori_loop(0, chunks + 2 * n - 2, tick, 0)
    scatter.swap(chunks - 1).wait_send()

    def drain(q, _):
        scatter.drain(q)
        gather.drain(q)
        return 0

    lax.fori_loop(0, chunks, drain, 0)


def ffn_kernel(
    fuse, mixed_hbm, w_out_ref, input_hbm, gain_ref, w_gate_hbm, w_up_hbm, w_down_hbm, late_hbm,
    cot_hbm, resid_hbm, dgate_hbm, dup_hbm, down_hbm, gdown_hbm, *refs,
):
    outs, refs = refs[: 1 + fuse], refs[1 + fuse :]
    own, stage, cross, line, xs, xr, ls, lr, held, gs, gr, held2, gs2, gr2, *refs = refs
    w_gate, w_up, w_down, cot, hid, dg, du, down, gdown, total, mix, inp, res, *refs = refs
    wsem, csem, osem, dsem, msem, hsem, isem, rsem, *wide = refs
    chunks, blocks, rows, depth = held.shape
    units = w_gate.shape[0]
    p = Place(blocks)
    scatter = Scatter(p, own, stage, cross, line, xs, xr, ls, lr)
    gather = Gather(p, held, gs, gr)
    loads = [
        pltpu.make_async_copy(src, dst, wsem.at[i])
        for i, (src, dst) in enumerate(
            ((w_gate_hbm, w_gate), (w_up_hbm, w_up), (w_down_hbm, w_down))
        )
    ]
    for load in loads:
        load.start()
    cot_load = lambda q: pltpu.make_async_copy(cot_hbm.at[:, q], cot.at[q % 2], csem.at[q % 2])
    cot_load(0).start()
    early = cot_hbm.shape[1]
    mix_load = lambda q: pltpu.make_async_copy(mixed_hbm.at[:, q], mix, msem)
    mix_load(0).start()

    def own_rows(q):
        return pl.ds(pl.multiple_of(q * rows, rows), rows)

    in_load = lambda q: pltpu.make_async_copy(
        input_hbm.at[own_rows(q)], inp, isem
    )
    res_save = lambda q: pltpu.make_async_copy(
        res.at[q % 2], resid_hbm.at[own_rows(q)], rsem.at[q % 2]
    )
    in_load(0).start()

    def late_load(j):
        here = pl.ds(pl.multiple_of((early + j) * rows, rows), rows)
        return pltpu.make_async_copy(late_hbm.at[here], held2.at[j, p.me], hsem.at[j])

    for j in range(chunks - early):
        late_load(j).start()
    p.greet()
    later = Gather(p, held2, gs2, gr2)

    def also(w):
        for s in range(p.n - 1, -1, -1):

            @pl.when(within(w - s, chunks - early))
            def _():
                if s == 0:
                    late_load(w).wait()
                later.step(w - s, s)
                if s == p.n - 1:
                    later.finish(w - s)

    def partial(q):
        mix_load(q).wait()
        x = mix[...].reshape(blocks * rows, -1)
        for a, b in lane_tiles(depth, 512):
            put_share(
                p, own, stage, q, jnp.dot(x, w_out_ref[:, a:b], preferred_element_type=F32), a, b
            )

        @pl.when(q + 1 < chunks)
        def _():
            mix_load(q + 1).start()

    def middle(q):
        scatter.result(q, total)
        in_load(q).wait()
        @pl.when(q >= 2)
        def _():
            res_save(q - 2).wait()

        resid = inp[...].astype(F32) + total[...]
        res[q % 2] = resid
        res_save(q).start()

        @pl.when(q + 1 < chunks)
        def _():
            in_load(q + 1).start()

        normed = resid * lax.rsqrt(jnp.mean(resid * resid, axis=1, keepdims=True) + 1e-05)
        held[q, p.me] = (normed * gain_ref[...]).astype(BF16)

    def saves(q):
        slot = q % 2
        return [
            pltpu.make_async_copy(src.at[slot], dst.at[:, q], osem.at[slot, i])
            for i, (src, dst) in enumerate(((dg, dgate_hbm), (du, dup_hbm)))
        ] + [
            pltpu.make_async_copy(held.at[q], out.at[:, q], osem.at[slot, 3])
            for out in outs
            if not fuse
        ]

    def down_save(q):
        return pltpu.make_async_copy(down, down_hbm.at[:, q], osem.at[0, 2])

    def consume(q):
        slot = q % 2

        @pl.when(q == 0)
        def _():
            for load in loads:
                load.wait()
            for ref in (gdown, *wide):
                ref[...] = jnp.zeros_like(ref)

        @pl.when(q < early)
        def _():
            cot_load(q).wait()

        @pl.when(q >= early)
        def _():
            cot[slot] = held2[q - early]

        @pl.when(q >= 2)
        def _():
            for save in saves(q - 2):
                save.wait()

        x = held[q].reshape(blocks * rows, depth)
        g = cot[slot].reshape(blocks * rows, depth)
        for a, b in lane_tiles(units):
            gate = mm(x, w_gate[a:b, :], tb=True)
            up = mm(x, w_up[a:b, :], tb=True)
            gh = mm(g, w_down[a:b, :], tb=True)
            sg = sigmoid(gate)
            act = gate * sg
            shape = (blocks, rows, b - a)
            hid[slot, :, a:b] = (act * up).astype(BF16)
            dg[slot, :, :, a:b] = (
                (gh * up * sg * (1.0 + gate * (1.0 - sg))).astype(BF16).reshape(shape)
            )
            du[slot, :, :, a:b] = (gh * act).astype(BF16).reshape(shape)
        h = hid[slot]

        @pl.when(q >= 1)
        def _():
            down_save(q - 1).wait()

        for a, b in lane_tiles(depth, 512):
            down[:, :, a:b] = (
                jnp.dot(h, w_down[:, a:b], preferred_element_type=F32)
                .astype(BF16)
                .reshape(blocks, rows, b - a)
            )
        down_save(q).start()
        for save in saves(q):
            save.start()

        @pl.when(slot == 1)
        def _():
            both = 2 * blocks * rows
            x = held[pl.ds(q - 1, 2)].reshape(both, depth)
            g = cot[...].reshape(both, depth)
            for acc, left, right in zip((gdown, *wide), (hid, dg, du), (g, x, x)):
                left = left[...].reshape(both, units)
                for a, b in lane_tiles(depth, 256):
                    acc[:, a:b] += mm(left, right[:, a:b], ta=True)

        @pl.when(q + 1 < early)
        def _():
            cot_load(q + 1).start()

    ticks(chunks, p.n, scatter, gather, partial, middle, consume, also)
    ends = []
    pairs = ((gdown, w_down, gdown_hbm), *zip(wide, (w_gate, w_up), outs))
    for i, (acc, low, out) in enumerate(pairs):
        low[...] = acc[...].astype(BF16)
        ends.append(pltpu.make_async_copy(low, out, dsem.at[i]))
        ends[-1].start()
    lax.fori_loop(0, chunks - early, lambda q, _: later.drain(q), None)
    for end in ends:
        end.wait()
    down_save(chunks - 1).wait()
    for q in range(max(chunks - 2, 0), chunks):
        res_save(q).wait()
    for q in range(max(chunks - 2, 0), chunks):
        for save in saves(q):
            save.wait()


def chunk_rows(blocks, owned):
    return min(owned, max(16, 2048 // (blocks * blocks)))


def early_chunks(chunks, blocks):
    return chunks - 32 * chunks // (blocks * blocks)


ANY = pl.BlockSpec(memory_space=pl.ANY)
WHOLE = pl.BlockSpec(memory_space=pltpu.VMEM)


def ffn(mixed, w_out, inputs, gain, w_gate, w_up, w_down, cot, early):
    owned, depth = inputs.shape
    blocks = mixed.shape[0] // owned
    rows = chunk_rows(blocks, owned)
    chunks = owned // rows
    units = w_gate.shape[0]
    fuse = blocks <= 8
    cut = lambda width: jax.ShapeDtypeStruct((blocks, chunks, rows, width), BF16)
    dma = pltpu.SemaphoreType.DMA
    return pl.pallas_call(
        functools.partial(ffn_kernel, fuse),
        in_specs=[ANY, WHOLE, ANY, WHOLE] + [ANY] * 5,
        out_specs=[ANY] * (6 + fuse),
        out_shape=[
            jax.ShapeDtypeStruct((owned, depth), F32),
            cut(units),
            cut(units),
            cut(depth),
            jax.ShapeDtypeStruct((units, depth), BF16),
            *([jax.ShapeDtypeStruct((units, depth), BF16)] * 2 if fuse else [cut(depth)]),
        ],
        scratch_shapes=ring_scratch(chunks, blocks, rows, depth)
        + gather_scratch(chunks, blocks, rows, depth)
        + gather_scratch(chunks - early_chunks(chunks, blocks), blocks, rows, depth)
        + [
            pltpu.VMEM(w_gate.shape, BF16),
            pltpu.VMEM(w_up.shape, BF16),
            pltpu.VMEM(w_down.shape, BF16),
            pltpu.VMEM((2, blocks, rows, depth), BF16),
            pltpu.VMEM((2, blocks * rows, units), BF16),
            pltpu.VMEM((2, blocks, rows, units), BF16),
            pltpu.VMEM((2, blocks, rows, units), BF16),
            pltpu.VMEM((blocks, rows, depth), BF16),
            pltpu.VMEM((units, depth), F32),
            pltpu.VMEM((rows, depth), F32),
            pltpu.VMEM((blocks, rows, mixed.shape[1]), BF16),
            pltpu.VMEM((rows, depth), BF16),
            pltpu.VMEM((2, rows, depth), F32),
            dma((3,)),
            dma((2,)),
            dma((2, 4)),
            dma((3,)),
            dma,
            dma((chunks - early_chunks(chunks, blocks),)),
            dma,
            dma((2,)),
            *[pltpu.VMEM((units, depth), F32)] * (2 * fuse),
        ],
        compiler_params=pltpu.CompilerParams(
            collective_id=1, has_side_effects=True, vmem_limit_bytes=127 * 512 * 1024
        ),
        name="ffn_rounds",
    )(
        mixed.reshape(blocks, chunks, rows, -1),
        w_out,
        inputs,
        gain,
        w_gate,
        w_up,
        w_down,
        cot,
        early.reshape(blocks, -1, rows, depth),
    )


def back_kernel(
    items, dgate_hbm, dup_hbm, w_gate_ref, w_up_ref, resid_hbm, gain_ref, cot_hbm, w_out_hbm, mixed_hbm, sd_hbm,
    gres_ref, ggain_ref, gout_ref, gm_hbm, rd_hbm,
    own, stage, cross, line, xs, xr, ls, lr, held, gs, gr, gm, total, gout, osem,
    dgate_ref, dup_ref, resid_ref, cot_ref, w_out_ref, mixed_ref, asem, bsem, done, *sums,
):
    chunks, blocks, rows, depth = held.shape
    p = Place(blocks)
    scatter = Scatter(p, own, stage, cross, line, xs, xr, ls, lr)
    gather = Gather(p, held, gs, gr)
    def shares(q):
        return [
            pltpu.make_async_copy(src.at[:, q], dst.at[:, q], asem.at[q, i])
            for i, (src, dst) in enumerate(((dgate_hbm, dgate_ref), (dup_hbm, dup_ref)))
        ]

    for load in shares(0):
        load.start()
    rest = [
        pltpu.make_async_copy(src, dst, bsem.at[i])
        for i, (src, dst) in enumerate(
            (
                (resid_hbm, resid_ref),
                (cot_hbm, cot_ref),
                (w_out_hbm, w_out_ref),
                (mixed_hbm, mixed_ref),
            )
        )
    ]
    p.greet(items)
    bits = items.bit_length() - 1
    reduce = Reduce(items, sd_hbm, sums[:bits], done, rd_hbm, *sums[bits:], axis=1)
    reduce.start()
    ggain_ref[...] = jnp.zeros_like(ggain_ref)

    def partial(q):
        for load in shares(q):
            load.wait()

        @pl.when(q == 0)
        def _():
            for i in range(1, chunks):
                for load in shares(i):
                    load.start()
            for load in rest:
                load.start()

        g = dgate_ref[:, q].reshape(blocks * rows, -1)
        u = dup_ref[:, q].reshape(blocks * rows, -1)
        for a, b in lane_tiles(depth, 512):
            put_share(
                p,
                own,
                stage,
                q,
                mm(g, w_gate_ref[:, a:b]) + mm(u, w_up_ref[:, a:b]),
                a,
                b,
            )

    def middle(q):
        @pl.when(q == 0)
        def _():
            for load in rest:
                load.wait()

        scatter.result(q, total)
        here = pl.ds(pl.multiple_of(q * rows, rows), rows)
        resid = resid_ref[here, :]
        n = lax.rsqrt(jnp.mean(resid * resid, axis=1, keepdims=True) + 1e-05)
        u = resid * n
        grad = total[...]
        ggain_ref[...] += jnp.sum((grad * u).reshape(rows // 8, 8, depth), axis=0)
        e = grad * gain_ref[...]
        gres = cot_ref[here, :].astype(F32) + n * (e - u * jnp.mean(e * u, axis=1, keepdims=True))
        gres_ref[here, :] = gres
        held[q, p.me] = gres.astype(BF16)

    def save(q):
        return pltpu.make_async_copy(gm.at[q % 2], gm_hbm.at[:, q], osem.at[q % 2])

    def consume(q):
        @pl.when(q >= 2)
        def _():
            save(q - 2).wait()

        @pl.when(q == 0)
        def _():
            gout[...] = jnp.zeros_like(gout)

        x = held[q].reshape(blocks * rows, depth)
        gm[q % 2] = mm(x, w_out_ref[...], tb=True).reshape(blocks, rows, -1)
        save(q).start()
        m = mixed_ref[:, q].reshape(blocks * rows, -1)
        for a, b in lane_tiles(depth, 1024):
            gout[:, a:b] += mm(m, x[:, a:b], ta=True)

    steps = reduce.handlers()

    def also(w):
        for i, step in enumerate(steps):
            at = 4 * len(steps) - 4 if i == len(steps) - 1 else 4 + 2 * i
            pl.when(w == at)(step)

    ticks(chunks, p.n, scatter, gather, partial, middle, consume, also)
    reduce.drain()
    for q in range(max(chunks - 2, 0), chunks):
        save(q).wait()
    gout_ref[...] = gout[...].astype(BF16)


def back(dgate, dup, w_gate, w_up, resid, gain, cot, w_out, mixed, grad_down, items):
    blocks, chunks, rows, _ = dgate.shape
    owned, depth = resid.shape
    width = w_out.shape[0]
    dma = pltpu.SemaphoreType.DMA
    return pl.pallas_call(
        functools.partial(back_kernel, items),
        in_specs=[ANY] * 2 + [WHOLE] * 2 + [ANY, WHOLE] + [ANY] * 4,
        out_specs=[WHOLE, WHOLE, WHOLE, ANY, ANY],
        out_shape=[
            jax.ShapeDtypeStruct((owned, depth), F32),
            jax.ShapeDtypeStruct((8, depth), F32),
            jax.ShapeDtypeStruct((width, depth), BF16),
            jax.ShapeDtypeStruct((blocks, chunks, rows, width), F32),
            jax.ShapeDtypeStruct(grad_down.shape, BF16),
        ],
        scratch_shapes=ring_scratch(chunks, blocks, rows, depth)
        + gather_scratch(chunks, blocks, rows, depth)
        + [
            pltpu.VMEM((2, blocks, rows, width), F32),
            pltpu.VMEM((rows, depth), F32),
            pltpu.VMEM((width, depth), F32),
            dma((2,)),
            pltpu.VMEM(dgate.shape, BF16),
            pltpu.VMEM(dup.shape, BF16),
            pltpu.VMEM(resid.shape, F32),
            pltpu.VMEM(cot.shape, BF16),
            pltpu.VMEM(w_out.shape, BF16),
            pltpu.VMEM((blocks, chunks, rows, width), BF16),
            dma((chunks, 2)),
            dma((4,)),
            *reduce_scratch(items, *grad_down.shape, axis=1),
        ],
        compiler_params=pltpu.CompilerParams(
            collective_id=2, has_side_effects=True, vmem_limit_bytes=63 * 1024 * 1024
        ),
        name="back_rounds",
    )(
        dgate,
        dup,
        w_gate,
        w_up,
        resid,
        gain,
        cot,
        w_out,
        mixed.reshape(blocks, chunks, rows, width),
        grad_down,
    )


def add_rows(out, left, right, count):
    size = 64 if count % 64 == 0 else 16

    def body(i, _):
        rows = lambda at: pl.ds(pl.multiple_of(at + i * size, 16), size)
        value = left[0][rows(left[1]), :].astype(F32) + right[0][rows(right[1]), :].astype(F32)
        out[0][rows(out[1]), :] = value.astype(out[0].dtype)
        return 0

    lax.fori_loop(0, count // size, body, 0)


def add_columns(out, left, right, count):
    size = 32
    total = out[0].shape[0]

    def body(i, _):
        rows = pl.ds(pl.multiple_of(i * size, size), size)
        cols = lambda at: pl.ds(pl.multiple_of(at, 128), count)
        value = left[0][rows, cols(left[1])].astype(F32) + right[0][rows, cols(right[1])].astype(F32)
        out[0][rows, cols(out[1])] = value.astype(out[0].dtype)
        return 0

    lax.fori_loop(0, total // size, body, 0)


class Reduce:
    def __init__(self, count, src, parts, done, out, ss, rr, load, save, axis=0):
        self.axis = axis
        self.add = (add_rows, add_columns)[axis]
        self.src, self.parts, self.done, self.out = src, parts, done, out
        self.ss, self.rr, self.load_sem, self.save_sem = ss, rr, load, save
        self.bits = count.bit_length() - 1
        item = lax.axis_index("item")
        total = src.shape[axis]
        self.plan = []
        for half in range(2):
            start = half * (total // 2)
            size = total // 2
            steps = []
            for k in range(self.bits):
                unit = 2 ** (k if half == 0 else self.bits - 1 - k)
                bit = (item // unit) % 2
                size //= 2
                keep = start + bit * size
                give = start + (1 - bit) * size
                steps.append((size, keep, give, bit * size, (1 - bit) * size, item + unit - 2 * unit * bit))
                start = keep
            self.plan.append(steps)

    def rows(self, ref, at, size):
        if self.axis:
            return ref.at[:, pl.ds(pl.multiple_of(at, 128), size)]
        return ref.at[pl.ds(pl.multiple_of(at, 16), size)]

    def load(self, half):
        size, keep = self.plan[half][0][:2]
        return pltpu.make_async_copy(
            self.rows(self.src, keep, size), self.rows(self.done, keep, size), self.load_sem.at[half]
        )

    def down(self, half, k):
        size, _, give, _, local, partner = self.plan[half][k]
        source = self.rows(self.src, give, size) if k == 0 else self.rows(self.parts[k - 1].at[half], local, size)
        return pltpu.make_async_remote_copy(
            src_ref=source,
            dst_ref=self.parts[k].at[half],
            send_sem=self.ss.at[half, k],
            recv_sem=self.rr.at[half, k],
            device_id={"item": partner},
            device_id_type=MESH,
        )

    def up(self, half, k, back=False):
        size, keep, give, _, _, partner = self.plan[half][k]
        ref = self.rows(self.done, give if back else keep, size)
        return pltpu.make_async_remote_copy(
            src_ref=ref,
            dst_ref=ref,
            send_sem=self.ss.at[half, self.bits + k],
            recv_sem=self.rr.at[half, self.bits + k],
            device_id={"item": partner},
            device_id_type=MESH,
        )

    def start(self):
        for half in range(2):
            self.load(half).start()
            self.down(half, 0).start()

    def halve(self, k):
        for half in range(2):
            size, keep, _, local, _, _ = self.plan[half][k]
            if k == 0:
                self.load(half).wait()
                mine = (self.done, keep)
            else:
                mine = (self.parts[k - 1].at[half], local)
            self.down(half, k).wait_recv()
            part = (self.parts[k].at[half], 0)
            if k + 1 < self.bits:
                self.add(part, mine, part, size)
                self.down(half, k + 1).start()
            else:
                self.add((self.done, keep), mine, part, size)
                self.up(half, k).start()

    def double(self, k):
        for half in range(2):
            self.up(half, k, True).wait_recv()
            self.up(half, k - 1).start()

    def save(self):
        return pltpu.make_async_copy(self.done, self.out, self.save_sem)

    def finish(self):
        for half in range(2):
            self.up(half, 0, True).wait_recv()
        self.save().start()

    def drain(self):
        for half in range(2):
            for k in range(self.bits):
                self.down(half, k).wait_send()
                self.up(half, k).wait_send()
        self.save().wait()

    def handlers(self):
        return (
            [functools.partial(self.halve, k) for k in range(self.bits)]
            + [functools.partial(self.double, k) for k in range(self.bits - 1, 0, -1)]
            + [self.finish]
        )


def reduce_scratch(count, total, width, axis=0):
    dma = pltpu.SemaphoreType.DMA
    bits = count.bit_length() - 1
    return [
        pltpu.VMEM((total, width), BF16),
        *[
            pltpu.VMEM(
                (2, total, width // 2 ** (k + 2)) if axis else (2, total // 2 ** (k + 2), width), BF16
            )
            for k in range(bits)
        ],
        dma((2, 2 * bits)),
        dma((2, 2 * bits)),
        dma((2,)),
        dma,
    ]


class Peers:
    def __init__(self, axis, count, held, ss, rr):
        self.axis, self.count, self.held, self.ss, self.rr = axis, count, held, ss, rr
        self.me = lax.axis_index(axis)

    def other(self, k):
        return (self.me + k) % self.count

    def copy(self, slot, k):
        ref = self.held.at[slot]
        return pltpu.make_async_remote_copy(
            src_ref=ref,
            dst_ref=ref,
            send_sem=self.ss.at[k],
            recv_sem=self.rr.at[slot],
            device_id={self.axis: self.other(k)},
            device_id_type=MESH,
        )

    def greet(self):
        barrier = pltpu.get_barrier_semaphore()
        for k in range(1, self.count):
            pl.semaphore_signal(
                barrier, inc=1, device_id={self.axis: self.other(k)}, device_id_type=MESH
            )

    def send(self):
        for k in range(1, self.count):
            self.copy(self.me, k).start()

    def total(self):
        for k in range(1, self.count):
            self.copy(self.other(k), k).wait_recv()
        out = self.held[0]
        for slot in range(1, self.count):
            out = out + self.held[slot]
        return out

    def drain(self):
        for k in range(1, self.count):
            self.copy(self.me, k).wait_send()


def tail_kernel(
    gq_hbm, gk_hbm, gv_hbm, gg_hbm, gdw_hbm, wq_ref, wk_ref, wv_ref, wg_ref, wdw_ref,
    input_hbm, gain_ref, gres_hbm, resid_hbm, fgain_ref, ogain_ref, conv_ref, dl_ref, wide_ref, down_hbm,
    output_ref, igrad_ref, small_ref,
    own, stage, cross, line, xs, xr, ls, lr, own2, cross2, line2, xs2, xr2, ls2, lr2, osem,
    total, ngain, held1, held2, s1, r1, s2, r2,
    gq_ref, gk_ref, gv_ref, gg_ref, gdw_ref, input_ref, gres_ref, resid_ref, asem, bsem,
):
    chunks, n, rows, depth = cross.shape
    blocks = 2 * n
    p = Place(blocks)
    first = Scatter(p, own, stage, cross, line, xs, xr, ls, lr)
    first_late = chunks - cross2.shape[0]
    second = Late(p, down_hbm, first_late, own2, cross2, line2, xs2, xr2, ls2, lr2, osem)
    sources = (
        (gq_hbm, gq_ref), (gk_hbm, gk_ref), (gv_hbm, gv_ref), (gg_hbm, gg_ref), (gdw_hbm, gdw_ref)
    )

    def shares(q):
        return [
            pltpu.make_async_copy(src.at[:, q], dst.at[:, q], asem.at[q, i])
            for i, (src, dst) in enumerate(sources)
        ]

    for load in shares(0):
        load.start()
    rest = [
        pltpu.make_async_copy(src, dst, bsem.at[i])
        for i, (src, dst) in enumerate(
            ((input_hbm, input_ref), (gres_hbm, gres_ref), (resid_hbm, resid_ref))
        )
    ]
    heads = Peers("head", held1.shape[0], held1, s1, r1)
    items = Peers("item", held2.shape[0], held2, s2, r2)
    heads.greet()
    items.greet()
    pl.semaphore_wait(pltpu.get_barrier_semaphore(), heads.count + items.count - 2)
    ngain[...] = jnp.zeros_like(ngain)
    width1 = held1.shape[2]
    half = conv_ref.shape[2] // 2
    held1[heads.me] = jnp.zeros(held1.shape[1:], F32)
    held2[items.me] = jnp.zeros(held2.shape[1:], F32)

    second.start()
    def finish_late(j):
        here = pl.ds(pl.multiple_of(j * rows, rows), rows)
        second.scatter.result(j, total)
        there = pl.ds(pl.multiple_of((first_late + j) * rows, rows), rows)
        output_ref[here, :] = (resid_ref[there, :] + total[...]).astype(BF16)

    def partial(q):
        for load in shares(q):
            load.wait()

        @pl.when(q == 0)
        def _():
            for i in range(1, chunks):
                for load in shares(i):
                    load.start()
            for load in rest:
                load.start()

        pairs = [
            (ref[:, q].reshape(blocks * rows, -1), w)
            for ref, w in ((gq_ref, wq_ref), (gk_ref, wk_ref), (gv_ref, wv_ref), (gg_ref, wg_ref))
        ]
        dw = gdw_ref[:, q].reshape(blocks * rows, -1)
        for a, b in lane_tiles(depth, 512):
            value = mm(dw, wdw_ref[:, a:b])
            for x, w in pairs:
                value = value + mm(x, w[a:b, :], tb=True)
            put_share(p, own, stage, q, value, a, b)

    partial(0)
    first.swap(0).start()
    for load in rest:
        load.wait()

    def end(q):
        here = pl.ds(pl.multiple_of(q * rows, rows), rows)
        first.result(q, total)
        x = input_ref[here, :].astype(F32)
        scale = lax.rsqrt(jnp.mean(x * x, axis=1, keepdims=True) + 1e-05)
        u = x * scale
        grad = total[...]
        ngain[...] += jnp.sum((grad * u).reshape(rows // 8, 8, depth), axis=0)
        e = grad * gain_ref[...]
        igrad_ref[here, :] = gres_ref[here, :] + scale * (
            e - u * jnp.mean(e * u, axis=1, keepdims=True)
        )

    def turn(w, _):
        pl.when(within(w - n + 1, chunks))(lambda: end(w - n + 1))
        for s in range(n - 2, 0, -1):
            pl.when(within(w - s, chunks))(lambda: first.step(w - s, s))

        @pl.when(w < chunks)
        def _():
            first.swap(w).wait_recv()
            first.step(w, 0)

        second.tick(w, finish_late)

        @pl.when(w + 1 < chunks)
        def _():
            first.swap(w).wait_send()
            partial(w + 1)
            first.swap(w + 1).start()

        return 0

    lax.fori_loop(0, chunks + n - 1, turn, 0)
    part = depth // 8
    for at, ref in ((0, ngain), (part, fgain_ref)):
        row = jnp.sum(ref[...], axis=0, keepdims=True)
        for i in range(8):
            held1[heads.me, i : i + 1, at : at + part] = row[:, i * part : (i + 1) * part]
    row = jnp.sum(ogain_ref[...], axis=0, keepdims=True)
    for i in range(2):
        held1[heads.me, i : i + 1, 2 * part : 2 * part + 128] = row[:, i * 128 : (i + 1) * 128]
    heads.send()
    for j in range(4):
        row = jnp.sum(conv_ref[j], axis=0, keepdims=True)
        for i in range(2):
            held2[items.me, 4 * i + j : 4 * i + j + 1, width1 : width1 + half] = row[
                :, i * half : (i + 1) * half
            ]
    at = width1 + half + 128
    held2[items.me, 0:1, width1 + half : at] = dl_ref[...]
    held2[items.me, :, at:] = wide_ref[...]
    held2[items.me, :, 0:width1] = heads.total()
    items.send()

    def drain(q, _):
        first.drain(q)
        return 0

    lax.fori_loop(0, chunks, drain, 0)
    second.drain()
    first.swap(chunks - 1).wait_send()
    small_ref[...] = items.total()
    heads.drain()
    items.drain()


def tail(grads, weights, inputs, gain, gres, resid, fgain, ogain, gconv, gdl, wide, down, items):
    blocks, chunks, rows, depth = down.shape
    owned = inputs.shape[0]
    n = blocks // 2
    cut = lambda value: value.reshape(blocks, chunks, rows, -1)
    width1 = depth // 4 + 128
    width2 = width1 + gconv.shape[2] // 2 + 128 + wide.size // 8
    gdl = jnp.pad(gdl, ((0, 0), (0, 128 - gdl.shape[1])))
    dma = pltpu.SemaphoreType.DMA
    one = ring_scratch(chunks, blocks, rows, depth)
    late = chunks - 3 * chunks // 4
    output, igrad, small = pl.pallas_call(
        tail_kernel,
        in_specs=[ANY] * 5 + [WHOLE] * 5 + [ANY, WHOLE, ANY, ANY] + [WHOLE] * 5 + [ANY],
        out_specs=[WHOLE] * 3,
        out_shape=[
            jax.ShapeDtypeStruct((late * rows, depth), BF16),
            jax.ShapeDtypeStruct((owned, depth), F32),
            jax.ShapeDtypeStruct((8, width2), F32),
        ],
        scratch_shapes=one
        + late_scratch(late, min(late, n), blocks, rows, depth)
        + [
            pltpu.VMEM((rows, depth), F32),
            pltpu.VMEM((8, depth), F32),
            pltpu.VMEM((blocks, 8, width1), F32),
            pltpu.VMEM((items, 8, width2), F32),
            dma((blocks,)),
            dma((blocks,)),
            dma((items,)),
            dma((items,)),
            *[pltpu.VMEM(cut(value).shape, BF16) for value in grads],
            pltpu.VMEM(inputs.shape, BF16),
            pltpu.VMEM(gres.shape, F32),
            pltpu.VMEM(resid.shape, F32),
            dma((chunks, 5)),
            dma((3,)),
        ],
        compiler_params=pltpu.CompilerParams(
            collective_id=3, has_side_effects=True, vmem_limit_bytes=63 * 1024 * 1024
        ),
        name="tail_rounds",
    )(
        *[cut(value) for value in grads],
        *weights,
        inputs,
        gain,
        gres,
        resid,
        fgain,
        ogain,
        gconv,
        gdl,
        wide.reshape(8, -1),
        down.reshape(n, 2, chunks, rows, depth),
    )
    part = depth // 8
    half = gconv.shape[2] // 2
    conv = small[:, width1 : width1 + half]
    return (
        output,
        igrad,
        small[:, :part].reshape(-1),
        small[:, part : 2 * part].reshape(-1),
        small[:2, 2 * part : 2 * part + 128].reshape(-1),
        jnp.concatenate([conv[:4], conv[4:]], axis=1),
        small[0, width1 + half : width1 + half + 128],
        small[:, width1 + half + 128 :].reshape(wide.shape),
    )


def head_kernel(
    input_ref, gain_ref, cot_hbm, wq_hbm, wk_hbm, wv_hbm, wg_hbm, wdw_ref,
    dw_ref, early_hbm, group_hbm, q_hbm, k_hbm, v_hbm, g_hbm,
    held, gs, gr, pq, pk, pv, pg, gsem, osem, esem, wsem, wq_ref, wk_ref, wv_ref, wg_ref,
):
    chunks, blocks, rows, depth = held.shape
    p = Place(blocks)
    gather = Gather(p, held, gs, gr)
    early = pltpu.make_async_copy(cot_hbm.at[0 : early_hbm.shape[0]], early_hbm, esem)
    early.start()
    loads = [
        pltpu.make_async_copy(src, dst, wsem.at[i])
        for i, (src, dst) in enumerate(
            ((wq_hbm, wq_ref), (wk_hbm, wk_ref), (wv_hbm, wv_ref), (wg_hbm, wg_ref))
        )
    ]
    p.greet()
    for q in range(chunks):
        x = input_ref[q * rows : (q + 1) * rows, :].astype(F32)
        x = x * lax.rsqrt(jnp.mean(x * x, axis=1, keepdims=True) + 1e-05)
        held[q, p.me] = (x * gain_ref[...]).astype(BF16)
        gather.step(q, 0)
    for load in loads:
        load.start()

    def saves(q):
        slot = q % 2
        return [
            pltpu.make_async_copy(src.at[slot], dst.at[:, q], osem.at[slot, i])
            for i, (src, dst) in enumerate(((pq, q_hbm), (pk, k_hbm), (pv, v_hbm), (pg, g_hbm)))
        ]

    def group_save(q):
        return pltpu.make_async_copy(held.at[q], group_hbm.at[:, q], gsem.at[q])

    def consume(q):
        gather.finish(q)
        group_save(q).start()

        @pl.when(q == 0)
        def _():
            for load in loads:
                load.wait()

        @pl.when(q >= 2)
        def _():
            for save in saves(q - 2):
                save.wait()

        x = held[q].reshape(blocks * rows, depth)
        for out, weight in ((pq, wq_ref), (pk, wk_ref), (pv, wv_ref), (pg, wg_ref)):
            for a, b in lane_tiles(weight.shape[1]):
                out[q % 2, :, :, a:b] = jnp.dot(
                    x, weight[:, a:b], preferred_element_type=F32
                ).reshape(blocks, rows, b - a)
        dw_ref[:, q] = mm(x, wdw_ref[...], tb=True).reshape(blocks, rows, -1)
        for save in saves(q):
            save.start()

    last = p.n - 1

    def turn(w, _):
        for s in range(1, p.n):

            @pl.when(jnp.logical_and(w >= s - 1, w - s + 1 < chunks))
            def _():
                gather.step(w - s + 1, s)

        @pl.when(w >= last)
        def _():
            consume(w - last)

        return 0

    lax.fori_loop(0, chunks + last, turn, 0)
    for q in range(max(chunks - 2, 0), chunks):
        for save in saves(q):
            save.wait()
    early.wait()

    def drain(q, _):
        gather.drain(q)
        group_save(q).wait()
        return 0

    lax.fori_loop(0, chunks, drain, 0)


def head(inputs, gain, cot, weights, thin, blocks):
    owned, depth = inputs.shape
    rows = chunk_rows(blocks, owned)
    chunks = owned // rows
    cut = lambda width, kind: jax.ShapeDtypeStruct((blocks, chunks, rows, width), kind)
    dma = pltpu.SemaphoreType.DMA
    return pl.pallas_call(
        head_kernel,
        in_specs=[WHOLE] * 2 + [ANY] * 5 + [WHOLE],
        out_specs=[WHOLE] + [ANY] * 6,
        out_shape=[
            cut(thin.shape[0], F32),
            jax.ShapeDtypeStruct((early_chunks(chunks, blocks) * rows, depth), BF16),
            cut(depth, BF16),
        ]
        + [cut(weight.shape[1], F32) for weight in weights],
        scratch_shapes=gather_scratch(chunks, blocks, rows, depth)
        + [pltpu.VMEM((2, blocks, rows, weight.shape[1]), F32) for weight in weights]
        + [dma((chunks,)), dma((2, 4)), dma, dma((4,))]
        + [pltpu.VMEM(weight.shape, BF16) for weight in weights],
        compiler_params=pltpu.CompilerParams(
            collective_id=4, has_side_effects=True, vmem_limit_bytes=62 * 1024 * 1024
        ),
        name="head_rounds",
    )(inputs, gain, cot, *weights, thin)


def widen_kernel(count, *refs):
    for source, out in zip(refs[:count], refs[count:]):
        out[...] = source[...].astype(F32)


def widen(values, parts):
    spec = [
        pl.BlockSpec((value.shape[0] // parts, value.shape[1]), lambda i: (i, 0)) for value in values
    ]
    return pl.pallas_call(
        functools.partial(widen_kernel, len(values)),
        grid=(parts,),
        in_specs=spec,
        out_specs=spec,
        out_shape=[jax.ShapeDtypeStruct(value.shape, F32) for value in values],
        compiler_params=pltpu.CompilerParams(
            dimension_semantics=("arbitrary",), vmem_limit_bytes=63 * 1024 * 1024
        ),
        name="widen",
    )(*values)


def inner_rows(left, right):
    return lax.dot_general(
        left, right, (((0,), (0,)), ((), ())), preferred_element_type=jnp.float32
    )


def gather(values):
    return lax.all_gather(values.astype(jnp.bfloat16), "head", axis=0, tiled=True)


def scatter(values):
    return lax.psum_scatter(values, "head", scatter_dimension=0, tiled=True)


def total(values):
    return lax.psum([value.astype(jnp.bfloat16) for value in values], "item")


def after(values, *earlier):
    return lax.optimization_barrier((values, earlier))[0]


def local(
    items,
    blocks,
    layer_input,
    lengths,
    norm_gain,
    w_query,
    w_key,
    w_value,
    w_outgate,
    w_decay,
    w_write,
    conv_query,
    conv_key,
    conv_value,
    decay_log,
    out_gain,
    w_out,
    ffn_gain,
    w_gate,
    w_up,
    w_down,
    cotangent,
):
    ng = norm_gain.astype(F32).reshape(1, -1)
    fg = ffn_gain.astype(F32).reshape(1, -1)
    og = out_gain.astype(F32).reshape(1, DV)
    conv = jnp.concatenate([conv_query, conv_key, conv_value], axis=1).astype(F32)
    dl = decay_log.reshape(1, -1)
    w_dw = jnp.concatenate([w_decay.T, w_write.T], axis=0)
    gate_t, up_t = w_gate.T, w_up.T
    owned, depth = layer_input.shape
    tokens = owned * blocks
    flat = lambda value: value.reshape(tokens, -1)
    by_seq = lambda value: value.reshape(-1, SEQ_LEN, value.shape[-1])
    raw_dw, early, group, *raw = head(
        layer_input, ng, cotangent, (w_query, w_key, w_value, w_outgate), w_dw, blocks
    )
    group = flat(group)
    early = gather(early)
    raw = [by_seq(flat(value)) for value in (*raw, raw_dw)]
    mixed, *kept = mixer_fwd(lengths, *raw, conv, dl, og)
    mixed = flat(mixed)
    resid, dgate, dup, down, grad_down, *rest = ffn(
        mixed, w_out, layer_input, fg, gate_t, up_t, w_down, cotangent, early
    )
    if len(rest) == 1:
        rest = [inner_rows(flat(value), flat(rest[0])) for value in (dgate, dup)]
    ffn_sums = total(rest)
    grad_resid, fgain, grad_w_out, grad_mixed, down_sum = back(
        dgate, dup, gate_t, up_t, resid, fg, cotangent, w_out, mixed, grad_down, items
    )
    backward = mixer_bwd(
        lengths, *raw, conv, dl, og, by_seq(flat(grad_mixed)), *kept, by_seq(group), resid, down,
        grad_w_out, items
    )
    grads, (gconv, gdl, ogain), wide, thin = backward[:5], backward[5:8], backward[8:12], backward[12]
    first, out_sum = backward[13:]
    mix_sums = total(after(list(wide), ffn_sums))
    grads = [flat(value) for value in grads]
    output, input_grad, ngain, fgain, ogain, conv_grad, dl_grad, thin = tail(
        grads,
        (w_query, w_key, w_value, w_outgate, w_dw),
        layer_input,
        ng,
        grad_resid,
        resid,
        fgain,
        ogain,
        gconv,
        gdl,
        thin,
        down,
        items,
    )
    output = jnp.concatenate([first, output])
    gate_sum, up_sum, down_sum, out_sum = widen(
        (*ffn_sums, down_sum, out_sum), w_down.shape[0] // 176
    )
    heads = dl.shape[1]
    qw = w_query.shape[1]
    return (
        output,
        input_grad,
        ngain,
        *widen(mix_sums, 8),
        thin[:heads].T,
        thin[heads:].T,
        conv_grad[:, :qw],
        conv_grad[:, qw : 2 * qw],
        conv_grad[:, 2 * qw :],
        dl_grad[:heads],
        ogain,
        out_sum,
        fgain,
        gate_sum.T,
        up_sum.T,
        down_sum,
    )


def solution(mesh):
    rows = P(("item", "head"), None)
    cols = P(None, "head")
    deep = P("head", None)
    return jax.shard_map(
        functools.partial(local, mesh.shape["item"], mesh.shape["head"]),
        mesh=mesh,
        in_specs=(rows, P("item"), P(), *[cols] * 9, P("head"), P(), deep, P(), cols, cols, deep, rows),
        out_specs=(rows, rows, P(), *[cols] * 9, P("head"), P(), deep, P(), cols, cols, deep),
        check_vma=False,
    )
```

```python
import functools

import jax
import jax.numpy as jnp
from jax import lax
from jax.experimental import pallas as pl
from jax.experimental.pallas import tpu as pltpu
from jax.sharding import PartitionSpec as P

DK = 128
DV = 256
SEQ_LEN = 1024
CHUNK = 128
F32 = jnp.float32
BF16 = jnp.bfloat16


def mm(left, right, ta=False, tb=False):
    return lax.dot_general(
        left.astype(BF16),
        right.astype(BF16),
        (((0 if ta else 1,), (1 if tb else 0,)), ((), ())),
        preferred_element_type=F32,
    )


def split(value):
    high = value.astype(BF16)
    return high, (value - high.astype(F32)).astype(BF16)


def mm3(left, right):
    lh, ll = left
    rh, rl = right
    return mm(lh, rh) + (mm(lh, rl) + mm(ll, rh))


def sigmoid(x):
    return 1.0 / (1.0 + jnp.exp(-x))


def grids():
    rows = lax.broadcasted_iota(jnp.int32, (CHUNK, CHUNK), 0)
    cols = lax.broadcasted_iota(jnp.int32, (CHUNK, CHUNK), 1)
    return rows, cols


def to_row(col, eye):
    return jnp.sum(jnp.where(eye, col, 0.0), axis=0, keepdims=True)


def inverses(mats, rows, cols):
    eye = jnp.where(rows == cols, 1.0, 0.0)
    near = rows // 8 == cols // 8
    n1 = [jnp.where(near, -a, 0.0) for a in mats]
    n1s = [split(n) for n in n1]
    n2 = [mm3(n, n) for n in n1s]
    n2s = [split(n) for n in n2]
    n3 = [mm3(a, b) for a, b in zip(n1s, n2s)]
    n4s = [split(mm3(n, n)) for n in n2s]
    p1 = [eye + a + b + c for a, b, c in zip(n1, n2, n3)]
    x = [p + mm3(split(p), n) for p, n in zip(p1, n4s)]
    size = 8
    while size < CHUNK:
        pair = (rows // (2 * size) == cols // (2 * size)) & (rows // size != cols // size)
        xs = [v.astype(BF16) for v in x]
        bx = [mm(jnp.where(pair, a, 0.0), v) for a, v in zip(mats, xs)]
        x = [v - mm(vs, w) for v, vs, w in zip(x, xs, bx)]
        size *= 2
    return x


def decays(ld, eye, causal):
    row = to_row(ld, eye)
    g = jnp.sum(jnp.where(causal, row, 0.0), axis=1, keepdims=True)
    grow = to_row(g, eye)
    d = jnp.where(causal, jnp.exp(jnp.where(causal, g - grow, 0.0)), 0.0)
    last = g[CHUNK - 1 : CHUNK, :]
    return d, jnp.exp(g), jnp.exp(last - g), jnp.exp(last)


def live_mask(len_ref, s, c):
    spot = lax.broadcasted_iota(jnp.int32, (CHUNK, 1), 0) + c * CHUNK
    return jnp.where(spot < len_ref[s], 1.0, 0.0)


def softplus(x):
    return jnp.maximum(x, 0.0) + jnp.log1p(jnp.exp(-jnp.abs(x)))


def mix_fwd_kernel(
    len_ref, q_ref, k_ref, v_ref, g_ref, dw_ref, conv_ref, dl_ref, gain_ref,
    mixed_ref, pre_ref, o_ref, u_ref, t_ref, s_ref, buf, state,
):
    c = pl.program_id(0)
    seqs, _, raws = buf.shape
    heads = dl_ref.shape[1]
    qw = heads * DK
    pieces = ((q_ref, 0, qw), (k_ref, qw, 2 * qw), (v_ref, 2 * qw, raws))

    @pl.when(c == 0)
    def _():
        buf[:, 0:8, :] = jnp.zeros((seqs, 8, raws), F32)
        state[...] = jnp.zeros_like(state)

    rows, cols = grids()
    eye = rows == cols
    causal = rows >= cols
    lower = rows > cols
    rate = jnp.exp(dl_ref[...])
    st = []
    for s in range(seqs):
        for ref, a, b in pieces:
            buf[s, 8 : 8 + CHUNK, a:b] = ref[s]
        pre = conv_ref[0:1, :] * buf[s, 5 : 5 + CHUNK, :]
        for j in range(1, 4):
            pre = pre + conv_ref[j : j + 1, :] * buf[s, 5 + j : 5 + j + CHUNK, :]
        pre_ref[s] = pre
        buf[s, 0:8, :] = buf[s, CHUNK : CHUNK + 8, :]
        act = pre * sigmoid(pre)
        mask = live_mask(len_ref, s, c)
        x = dw_ref[s]
        ld2 = -rate * softplus(x[:, :heads]) * mask
        be2 = sigmoid(x[:, heads:]) * mask
        for h in range(heads):
            q = act[:, h * DK : (h + 1) * DK]
            k = act[:, qw + h * DK : qw + (h + 1) * DK]
            v = act[:, 2 * qw + h * DV : 2 * qw + (h + 1) * DV]
            q = q * (lax.rsqrt(jnp.sum(q * q, axis=1, keepdims=True) + 1e-06) * DK ** (-0.5))
            k = k * lax.rsqrt(jnp.sum(k * k, axis=1, keepdims=True) + 1e-06)
            be = be2[:, h : h + 1]
            d, ga, e, el = decays(ld2[:, h : h + 1], eye, causal)
            qb = q.astype(BF16)
            kb = k.astype(BF16)
            qk = jnp.concatenate([qb, kb], axis=0)
            both = mm(qk, kb, tb=True)
            w = d * both[:CHUNK]
            a = jnp.where(lower, d * both[CHUNK:], 0.0) * be
            st.append((s, h, mask, v, be, ga, e, el, qk, kb, w, a))
    inv = inverses([z[-1] for z in st], rows, cols)
    for i, (s, h, mask, v, be, ga, e, el, qk, kb, w, a) in enumerate(st):
        t = inv[i].astype(BF16)
        old = state[i]
        oldb = old.astype(BF16)
        s_ref[i] = oldb
        t_ref[i] = t
        qks = mm(qk, oldb)
        r = be * (v - ga * qks[CHUNK:])
        u = mm(t, r)
        ub = u.astype(BF16)
        u_ref[s, :, h * DV : (h + 1) * DV] = ub
        o = ga * qks[:CHUNK] + mm(w, ub)
        state[i] = el * old + mm(kb, e * u, ta=True)
        o = o * mask
        o_ref[s, :, h * DV : (h + 1) * DV] = o
        rg = g_ref[s, :, h * DV : (h + 1) * DV]
        n = o * lax.rsqrt(jnp.mean(o * o, axis=1, keepdims=True) + 1e-05) * gain_ref[...]
        mixed_ref[s, :, h * DV : (h + 1) * DV] = (n * (rg * sigmoid(rg))).astype(BF16)


def mix_bwd_kernel(
    items, len_ref, q_ref, k_ref, v_ref, g_ref, dw_ref, conv_ref, dl_ref, gain_ref,
    gm_ref, pre_ref, o_ref, u_ref, t_ref, s_ref, group_ref, resid_ref, down_hbm, so_hbm,
    gq_ref, gk_ref, gv_ref, gg_ref, gdw_ref, gconv_ref, gdl_ref, ggain_ref,
    wq_ref, wk_ref, wv_ref, wg_ref, thin_ref, output_ref, ro_hbm, buf, dstate, weights,
    own, cross, line, xs, xr, ls, lr, osem, spare, done, *sums,
):
    step = pl.program_id(0)
    c = pl.num_programs(0) - 1 - step
    place = Place(2 * cross.shape[1])
    summing = Late(place, down_hbm, 0, own, cross, line, xs, xr, ls, lr, osem)

    bits = items.bit_length() - 1
    reduce = Reduce(items, so_hbm, sums[:bits], done, ro_hbm, *sums[bits:])

    @pl.when(step == 0)
    def _():
        place.greet(items)
        reduce.start()
        summing.start()

    steps = reduce.handlers()
    for i, handler in enumerate(steps):
        at = SEQ_LEN // CHUNK - 1 if i == len(steps) - 1 else SEQ_LEN // CHUNK - 1 - len(steps) + i
        pl.when(step == at)(handler)

    def add_output(q):
        size = spare.shape[0]
        here = pl.ds(pl.multiple_of(q * size, size), size)
        summing.scatter.result(q, spare)
        output_ref[here, :] = (resid_ref[here, :] + spare[...]).astype(BF16)

    total_ticks = cross.shape[0] + place.n - 1
    spans = 2 * (SEQ_LEN // CHUNK) - 1

    def run_ticks(place_at):
        def tick(w, _):
            summing.tick(w, add_output)
            return 0

        first = (place_at * total_ticks + spans - 1) // spans
        lax.fori_loop(first, ((place_at + 1) * total_ticks + spans - 1) // spans, tick, 0)

    pl.when(step >= 1)(lambda: run_ticks(2 * step - 1))
    seqs, _, raws = buf.shape
    heads = dl_ref.shape[1]
    qw = heads * DK
    pieces = ((q_ref, 0, qw), (k_ref, qw, 2 * qw), (v_ref, 2 * qw, raws))

    @pl.when(step == 0)
    def _():
        buf[:, CHUNK : CHUNK + 8, :] = jnp.zeros((seqs, 8, raws), F32)
        dstate[...] = jnp.zeros_like(dstate)
        gconv_ref[...] = jnp.zeros_like(gconv_ref)
        gdl_ref[...] = jnp.zeros_like(gdl_ref)
        ggain_ref[...] = jnp.zeros_like(ggain_ref)
        weights[...] = jnp.zeros_like(weights)
        thin_ref[...] = jnp.zeros_like(thin_ref)

    rows, cols = grids()
    eye = rows == cols
    causal = rows >= cols
    lower = rows > cols
    later = rows <= cols
    rate = jnp.exp(dl_ref[...])
    gain = gain_ref[...]
    for s in range(seqs):
        if s == seqs // 2:
            run_ticks(2 * step)
        mask = live_mask(len_ref, s, c)
        x = dw_ref[s]
        soft = -rate * mask
        ld2 = soft * softplus(x[:, :heads])
        sg = sigmoid(x)
        be2 = sg[:, heads:] * mask
        dlds = []
        dbes = []
        for h in range(heads):
            i = heads * s + h
            vs = slice(h * DV, (h + 1) * DV)
            gm = gm_ref[s, :, vs]
            o = o_ref[s, :, vs]
            rg = g_ref[s, :, h * DV : (h + 1) * DV]
            sr = sigmoid(rg)
            r = lax.rsqrt(jnp.mean(o * o, axis=1, keepdims=True) + 1e-05)
            un = o * r
            gsg = gm * sr
            gg_ref[s, :, h * DV : (h + 1) * DV] = (
                gsg * (un * gain) * (1.0 + rg * (1.0 - sr))
            ).astype(BF16)
            dn = gsg * rg
            dnu = dn * un
            ggain_ref[...] += jnp.sum(dnu.reshape(CHUNK // 8, 8, DV), axis=0)
            do = (r * mask) * (dn * gain - un * jnp.mean(dnu * gain, axis=1, keepdims=True))
            pq = pre_ref[s, :, h * DK : (h + 1) * DK]
            pk = pre_ref[s, :, qw + h * DK : qw + (h + 1) * DK]
            pv = pre_ref[s, :, 2 * qw + h * DV : 2 * qw + (h + 1) * DV]
            sq = sigmoid(pq)
            sk = sigmoid(pk)
            sv = sigmoid(pv)
            q = pq * sq
            k = pk * sk
            v = pv * sv
            rq = lax.rsqrt(jnp.sum(q * q, axis=1, keepdims=True) + 1e-06)
            rk = lax.rsqrt(jnp.sum(k * k, axis=1, keepdims=True) + 1e-06)
            q = q * rq
            k = k * rk
            scale = DK ** (-0.5)
            be = be2[:, h : h + 1]
            d, ga, e, el = decays(ld2[:, h : h + 1], eye, causal)
            qb = (q * scale).astype(BF16)
            kb = k.astype(BF16)
            qk = jnp.concatenate([qb, kb], axis=0)
            both = mm(qk, kb, tb=True)
            w = d * both[:CHUNK]
            ab = jnp.where(lower, d * both[CHUNK:], 0.0)
            a = ab * be
            t = t_ref[i]
            st = s_ref[i]
            u = u_ref[s, :, vs]
            dh = dstate[i]
            dhb = dh.astype(BF16)
            qks = mm(qk, st)
            dob = do.astype(BF16)
            kdh = e * mm(kb, dhb)
            ubar = mm(w, dob, ta=True) + kdh
            rbar = mm(t, ubar, ta=True)
            rb = rbar.astype(BF16)
            uu = mm(jnp.concatenate([dob, rb], axis=0), u, tb=True)
            wbar = jnp.where(causal, uu[:CHUNK], 0.0)
            abar = -jnp.where(lower, uu[CHUNK:], 0.0)
            gks = ga * qks[CHUNK:]
            dv = be * rbar
            y = -ga * dv
            z = ga * do
            zy = jnp.concatenate([z.astype(BF16), y.astype(BF16)], axis=0)
            zys = mm(zy, st, tb=True)
            p = (wbar * d).astype(BF16)
            m = abar * d * be
            eu = e * u.astype(F32)
            dq = zys[:CHUNK] + mm(p, kb)
            dk = (
                zys[CHUNK:]
                + mm(p, qb, ta=True)
                + mm(m, kb)
                + mm(m, kb, ta=True)
                + mm(eu, dhb, tb=True)
            )
            dstate[i] = el * dh + mm(qk, zy, ta=True)
            ee = wbar * w + abar * a
            f = jnp.sum(u.astype(F32) * kdh, axis=1, keepdims=True)
            dbe = jnp.sum(rbar * (v - gks), axis=1, keepdims=True) + jnp.sum(
                abar * ab, axis=1, keepdims=True
            )
            dgc = (
                jnp.sum(ee, axis=1, keepdims=True)
                + jnp.sum(z * qks[:CHUNK] - dv * gks, axis=1, keepdims=True)
                - f
            )
            dgr = to_row(dgc, eye) - jnp.sum(ee, axis=0, keepdims=True)
            total = jnp.sum(f, axis=0, keepdims=True) + el * jnp.sum(
                jnp.sum(st.astype(F32) * dh, axis=1, keepdims=True), axis=0, keepdims=True
            )
            dld = jnp.sum(jnp.where(later, dgr, 0.0), axis=1, keepdims=True) + total
            dlds.append(dld)
            dbes.append(dbe)
            dq = dq * scale
            dqa = rq * (dq - q * jnp.sum(q * dq, axis=1, keepdims=True))
            dka = rk * (dk - k * jnp.sum(k * dk, axis=1, keepdims=True))
            buf[s, 0:CHUNK, h * DK : (h + 1) * DK] = dqa * sq * (1.0 + pq * (1.0 - sq))
            buf[s, 0:CHUNK, qw + h * DK : qw + (h + 1) * DK] = dka * sk * (1.0 + pk * (1.0 - sk))
            buf[s, 0:CHUNK, 2 * qw + h * DV : 2 * qw + (h + 1) * DV] = dv * sv * (1.0 + pv * (1.0 - sv))
        dld2 = jnp.concatenate(dlds, axis=1) if heads > 1 else dlds[0]
        dbe2 = jnp.concatenate(dbes, axis=1) if heads > 1 else dbes[0]
        gdw_ref[s] = jnp.concatenate(
            [dld2 * soft * sg[:, :heads], dbe2 * be2 * (1.0 - sg[:, heads:])], axis=1
        ).astype(BF16)
        gdl_ref[...] += jnp.sum(dld2 * ld2, axis=0, keepdims=True)
        for (ref, a, b), out in zip(pieces, (gq_ref, gk_ref, gv_ref)):
            raw = ref[s]
            draw = None
            for j in range(4):
                shifted = buf[s, 3 - j : 3 - j + CHUNK, a:b]
                gconv_ref[j, :, a:b] += jnp.sum(
                    (raw * shifted).reshape(CHUNK // 8, 8, b - a), axis=0
                )
                term = conv_ref[j : j + 1, a:b] * shifted
                draw = term if draw is None else draw + term
            out[s] = draw.astype(BF16)
        buf[s, CHUNK : CHUNK + 8, :] = buf[s, 0:8, :]
    x = group_ref[...].reshape(seqs * CHUNK, -1)
    flat = lambda ref: ref[...].reshape(seqs * CHUNK, -1)
    joined = jnp.concatenate([flat(ref) for ref in (gq_ref, gk_ref, gv_ref, gg_ref)], axis=1)
    for a in range(0, x.shape[1], 256):
        weights[a : a + 256, :] += mm(x[:, a : a + 256], joined, ta=True)
    thin_ref[...] += mm(gdw_ref[...].reshape(seqs * CHUNK, -1), x, ta=True)

    @pl.when(c == 0)
    def _():
        at = 0
        for out in (wq_ref, wk_ref, wv_ref, wg_ref):
            out[...] = weights[:, at : at + out.shape[1]].astype(BF16)
            at += out.shape[1]

        summing.drain()
        reduce.drain()


def mixer_fwd(lengths, q, k, v, g, dw, conv, dl, gain):
    count = SEQ_LEN // CHUNK
    seqs = q.shape[0]
    heads = dl.shape[1]
    raws, vw, n = conv.shape[1], heads * DV, seqs * heads
    full = lambda shape: pl.BlockSpec(shape, lambda c: (0,) * len(shape))
    seq = lambda width: pl.BlockSpec((seqs, CHUNK, width), lambda c: (0, c, 0))
    return pl.pallas_call(
        mix_fwd_kernel,
        grid=(count,),
        in_specs=[
            pl.BlockSpec(memory_space=pltpu.SMEM),
            seq(q.shape[2]),
            seq(k.shape[2]),
            seq(vw),
            seq(vw),
            seq(2 * heads),
            full((4, raws)),
            full((1, heads)),
            full((1, DV)),
        ],
        out_specs=[
            seq(vw),
            seq(raws),
            seq(vw),
            seq(vw),
            pl.BlockSpec((n, None, CHUNK, CHUNK), lambda c: (0, c, 0, 0)),
            pl.BlockSpec((n, None, DK, DV), lambda c: (0, c, 0, 0)),
        ],
        out_shape=[
            jax.ShapeDtypeStruct((seqs, SEQ_LEN, vw), BF16),
            jax.ShapeDtypeStruct((seqs, SEQ_LEN, raws), F32),
            jax.ShapeDtypeStruct((seqs, SEQ_LEN, vw), F32),
            jax.ShapeDtypeStruct((seqs, SEQ_LEN, vw), BF16),
            jax.ShapeDtypeStruct((n, count, CHUNK, CHUNK), BF16),
            jax.ShapeDtypeStruct((n, count, DK, DV), BF16),
        ],
        scratch_shapes=[
            pltpu.VMEM((seqs, CHUNK + 8, raws), F32),
            pltpu.VMEM((n, DK, DV), F32),
        ],
        compiler_params=pltpu.CompilerParams(
            dimension_semantics=("arbitrary",), vmem_limit_bytes=48 * 1024 * 1024
        ),
        name="mixer_forward",
    )(lengths, q, k, v, g, dw, conv, dl, gain)


def mixer_bwd(lengths, q, k, v, g, dw, conv, dl, gain, gm, pre, o, u, t, s, group, resid, down, grad_out, items):
    count = SEQ_LEN // CHUNK
    seqs = q.shape[0]
    heads = dl.shape[1]
    raws, vw, n = conv.shape[1], heads * DV, seqs * heads
    depth = group.shape[2]
    blocks, chunks, rows, _ = down.shape
    early = 3 * chunks // 4
    wide = [(depth, value.shape[2]) for value in (q, k, v, g)] + [(dw.shape[2], depth)]
    full = lambda shape: pl.BlockSpec(shape, lambda c: (0,) * len(shape))
    seq = lambda width: pl.BlockSpec((seqs, CHUNK, width), lambda c: (0, count - 1 - c, 0))
    return pl.pallas_call(
        functools.partial(mix_bwd_kernel, items),
        grid=(count,),
        in_specs=[
            pl.BlockSpec(memory_space=pltpu.SMEM),
            seq(q.shape[2]),
            seq(k.shape[2]),
            seq(vw),
            seq(vw),
            seq(2 * heads),
            full((4, raws)),
            full((1, heads)),
            full((1, DV)),
            seq(vw),
            seq(raws),
            seq(vw),
            seq(vw),
            pl.BlockSpec((n, None, CHUNK, CHUNK), lambda c: (0, count - 1 - c, 0, 0)),
            pl.BlockSpec((n, None, DK, DV), lambda c: (0, count - 1 - c, 0, 0)),
            seq(group.shape[2]),
            full((early * rows, depth)),
            pl.BlockSpec(memory_space=pl.ANY),
            pl.BlockSpec(memory_space=pl.ANY),
        ],
        out_specs=[
            seq(q.shape[2]),
            seq(k.shape[2]),
            seq(vw),
            seq(vw),
            seq(2 * heads),
            full((4, 8, raws)), full((1, heads)),
            full((8, DV)),
            *[full(shape) for shape in wide],
            full((early * rows, depth)),
            pl.BlockSpec(memory_space=pl.ANY),
        ],
        out_shape=[
            jax.ShapeDtypeStruct(q.shape, BF16),
            jax.ShapeDtypeStruct(k.shape, BF16),
            jax.ShapeDtypeStruct(v.shape, BF16),
            jax.ShapeDtypeStruct(g.shape, BF16),
            jax.ShapeDtypeStruct(dw.shape, BF16),
            jax.ShapeDtypeStruct((4, 8, raws), F32),
            jax.ShapeDtypeStruct((1, heads), F32),
            jax.ShapeDtypeStruct((8, DV), F32),
            *[jax.ShapeDtypeStruct(shape, BF16) for shape in wide[:4]],
            jax.ShapeDtypeStruct(wide[4], F32),
            jax.ShapeDtypeStruct((early * rows, depth), BF16),
            jax.ShapeDtypeStruct(grad_out.shape, BF16),
        ],
        scratch_shapes=[
            pltpu.VMEM((seqs, CHUNK + 8, raws), F32),
            pltpu.VMEM((n, DK, DV), F32),
            pltpu.VMEM((depth, sum(shape[1] for shape in wide[:4])), F32),
            *late_scratch(early, min(early, blocks // 2), blocks, rows, depth),
            pltpu.VMEM((rows, depth), F32),
            *reduce_scratch(items, *grad_out.shape),
        ],
        compiler_params=pltpu.CompilerParams(
            dimension_semantics=("arbitrary",),
            vmem_limit_bytes=62 * 1024 * 1024,
            collective_id=5,
            has_side_effects=True,
        ),
        name="mixer_backward",
    )(
        lengths,
        q,
        k,
        v,
        g,
        dw,
        conv,
        dl,
        gain,
        gm,
        pre,
        o,
        u,
        t,
        s,
        group,
        resid,
        down.reshape(blocks // 2, 2, chunks, rows, depth),
        grad_out,
    )


MESH = pl.DeviceIdType.MESH


class Place:
    def __init__(self, blocks):
        head = lax.axis_index("head")
        self.n = blocks // 2
        self.me = head
        self.z = head // 2
        self.c = head % 2
        self.mate = 2 * self.z + 1 - self.c
        self.right = head + 2
        self.left = head - 2
        self.has_right = self.z < self.n - 1
        self.has_left = self.z > 0

    def greet(self, items=1):
        barrier = pltpu.get_barrier_semaphore()
        item = lax.axis_index("item")
        for k in range(1, items):
            pl.semaphore_signal(
                barrier, inc=1, device_id={"item": (item + k) % items}, device_id_type=MESH
            )

        def hello(device):
            pl.semaphore_signal(barrier, inc=1, device_id={"head": device}, device_id_type=MESH)

        hello(self.mate)
        pl.when(self.has_right)(lambda: hello(self.right))
        pl.when(self.has_left)(lambda: hello(self.left))
        n = self.n
        pl.semaphore_wait(barrier, items + (self.z + n - 1) // n + (2 * n - 2 - self.z) // n)


def remote(src, dst, send, recv, device):
    return pltpu.make_async_remote_copy(
        src_ref=src,
        dst_ref=dst,
        send_sem=send,
        recv_sem=recv,
        device_id={"head": device},
        device_id_type=MESH,
    )


class Scatter:
    def __init__(self, place, own, stage, cross, line, xs, xr, ls, lr):
        self.p = place
        self.own, self.stage, self.cross, self.line = own, stage, cross, line
        self.xs, self.xr, self.ls, self.lr = xs, xr, ls, lr

    def swap(self, q):
        return remote(
            self.stage, self.cross.at[q], self.xs.at[q], self.xr.at[q], self.p.mate
        )

    def hop(self, q, slot, device):
        ref = self.line.at[q, slot]
        return remote(ref, ref, self.ls.at[q, slot], self.lr.at[q, slot], device)

    def share(self, q, t):
        return self.own[q % self.own.shape[0], t].astype(F32) + self.cross[q, t].astype(F32)

    def pass_on(self, q, t, slot, first, device):
        @pl.when(first)
        def _():
            self.line[q, slot] = self.share(q, t).astype(BF16)

        @pl.when(jnp.logical_not(first))
        def _():
            self.hop(q, slot, device).wait_recv()
            self.line[q, slot] = (self.share(q, t) + self.line[q, slot].astype(F32)).astype(BF16)

        self.hop(q, slot, device).start()

    def right_at(self, s):
        return self.p.n - 1 - s + self.p.z

    def left_at(self, s):
        n = self.p.n
        t = s + 1 - n + self.p.z
        return t, (t + n) % (n + 1)

    def step(self, q, s):
        p = self.p

        @pl.when(p.z <= s)
        def _():
            t = self.right_at(s)
            self.pass_on(q, t, t, p.z == 0, p.right)

        @pl.when(p.n - 1 - p.z <= s)
        def _():
            t, slot = self.left_at(s)
            self.pass_on(q, t, slot, p.z == p.n - 1, p.left)

    def result(self, q, total):
        p = self.p
        total[...] = self.share(q, p.z)

        @pl.when(p.has_left)
        def _():
            self.hop(q, p.z, p.right).wait_recv()
            total[...] += self.line[q, p.z].astype(F32)

        @pl.when(p.has_right)
        def _():
            slot = (p.z + p.n) % (p.n + 1)
            self.hop(q, slot, p.left).wait_recv()
            total[...] += self.line[q, slot].astype(F32)

    def drain(self, q):
        p = self.p
        for s in range(p.n - 1):

            @pl.when(p.z <= s)
            def _():
                self.hop(q, self.right_at(s), p.right).wait_send()

            @pl.when(p.n - 1 - p.z <= s)
            def _():
                self.hop(q, self.left_at(s)[1], p.left).wait_send()


class Late:
    def __init__(self, place, src, first, own, cross, line, xs, xr, ls, lr, osem):
        self.p, self.src, self.first = place, src, first
        self.count = cross.shape[0]
        self.own, self.cross, self.osem = own, cross, osem
        self.xs, self.xr = xs, xr
        self.scatter = Scatter(place, own, None, cross, line, xs, xr, ls, lr)

    def swap(self, q):
        return remote(
            self.src.at[:, 1 - self.p.c, self.first + q],
            self.cross.at[q],
            self.xs.at[q],
            self.xr.at[q],
            self.p.mate,
        )

    def load(self, q):
        slot = q % self.own.shape[0]
        return pltpu.make_async_copy(
            self.src.at[:, self.p.c, self.first + q], self.own.at[slot], self.osem.at[slot]
        )

    def start(self):
        for q in range(self.count):
            self.swap(q).start()
        for q in range(self.own.shape[0]):
            self.load(q).start()

    def enter(self, q):
        self.load(q).wait()
        self.swap(q).wait_recv()
        self.scatter.step(q, 0)

    def tick(self, w, result):
        n = self.p.n

        @pl.when(within(w - n + 1, self.count))
        def _():
            result(w - n + 1)
            slots = self.own.shape[0]

            @pl.when(w - n + 1 + slots < self.count)
            def _():
                self.load(w - n + 1 + slots).start()

        for s in range(n - 2, 0, -1):

            @pl.when(within(w - s, self.count))
            def _():
                self.scatter.step(w - s, s)

        @pl.when(w < self.count)
        def _():
            self.enter(w)

    def drain(self):
        def body(q, _):
            self.scatter.drain(q)
            self.swap(q).wait_send()
            return 0

        lax.fori_loop(0, self.count, body, 0)


def late_scratch(count, slots, blocks, rows, depth):
    n = blocks // 2
    dma = pltpu.SemaphoreType.DMA
    return [
        pltpu.VMEM((slots, n, rows, depth), BF16),
        pltpu.VMEM((count, n, rows, depth), BF16),
        pltpu.VMEM((count, n + 1, rows, depth), BF16),
        dma((count,)),
        dma((count,)),
        dma((count, n + 1)),
        dma((count, n + 1)),
        dma((slots,)),
    ]


class Gather:
    def __init__(self, place, held, ss, rr):
        self.p, self.held, self.ss, self.rr = place, held, ss, rr

    def copy(self, q, kind, z):
        p = self.p
        block = 2 * z + p.c
        ref = self.held.at[q, block]
        device = (p.right, p.left, p.mate)[kind]
        return remote(ref, ref, self.ss.at[q, kind, z], self.rr.at[q, block], device)

    def step(self, q, s):
        p = self.p
        if s == 0:
            pl.when(p.has_right)(lambda: self.copy(q, 0, p.z).start())
            pl.when(p.has_left)(lambda: self.copy(q, 1, p.z).start())
            self.copy(q, 2, p.z).start()
            return

        @pl.when(p.z >= s)
        def _():
            z = p.z - s
            self.copy(q, 0, z).wait_recv()
            pl.when(p.has_right)(lambda: self.copy(q, 0, z).start())
            self.copy(q, 2, z).start()

        @pl.when(p.z + s <= p.n - 1)
        def _():
            z = p.z + s
            self.copy(q, 1, z).wait_recv()
            pl.when(p.has_left)(lambda: self.copy(q, 1, z).start())
            self.copy(q, 2, z).start()

    def finish(self, q):
        p = self.p
        for z in range(p.n):
            block = 2 * z + 1 - p.c
            ref = self.held.at[q, block]
            remote(ref, ref, self.ss.at[q, 2, z], self.rr.at[q, block], p.mate).wait_recv()

    def drain(self, q):
        p = self.p
        for z in range(p.n):
            self.copy(q, 2, z).wait_send()

            @pl.when(jnp.logical_and(p.has_right, p.z >= z))
            def _():
                self.copy(q, 0, z).wait_send()

            @pl.when(jnp.logical_and(p.has_left, p.z <= z))
            def _():
                self.copy(q, 1, z).wait_send()


def lane_tiles(width, size=256):
    return [(at, min(at + size, width)) for at in range(0, width, size)]


def put_share(place, own, stage, q, values, a, b):
    slots, n, rows, _ = own.shape
    parts = values.astype(BF16).reshape(n, 2, rows, b - a)

    @pl.when(place.c == 0)
    def _():
        own[q % slots, :, :, a:b] = parts[:, 0]
        stage[:, :, a:b] = parts[:, 1]

    @pl.when(place.c == 1)
    def _():
        own[q % slots, :, :, a:b] = parts[:, 1]
        stage[:, :, a:b] = parts[:, 0]


def ring_scratch(chunks, blocks, rows, depth):
    n = blocks // 2
    dma = pltpu.SemaphoreType.DMA
    return [
        pltpu.VMEM((min(chunks, n), n, rows, depth), BF16),
        pltpu.VMEM((n, rows, depth), BF16),
        pltpu.VMEM((chunks, n, rows, depth), BF16),
        pltpu.VMEM((chunks, n + 1, rows, depth), BF16),
        dma((chunks,)),
        dma((chunks,)),
        dma((chunks, n + 1)),
        dma((chunks, n + 1)),
    ]


def gather_scratch(chunks, blocks, rows, depth):
    dma = pltpu.SemaphoreType.DMA
    return [
        pltpu.VMEM((chunks, blocks, rows, depth), BF16),
        dma((chunks, 3, blocks // 2)),
        dma((chunks, blocks)),
    ]


def within(q, chunks):
    return jnp.logical_and(q >= 0, q < chunks)


def ticks(chunks, n, scatter, gather, partial, middle, consume, also=None):
    partial(0)
    scatter.swap(0).start()

    def tick(w, _):
        v = w - n + 1

        @pl.when(within(v, chunks))
        def _():
            middle(v)
            gather.step(v, 0)

        for s in range(n - 2, 0, -1):

            @pl.when(within(w - s, chunks))
            def _():
                scatter.step(w - s, s)

        @pl.when(w < chunks)
        def _():
            scatter.swap(w).wait_recv()
            scatter.step(w, 0)

        for s in range(n - 1, 0, -1):

            @pl.when(within(v - s, chunks))
            def _():
                gather.step(v - s, s)

        if also is not None:
            also(w)

        @pl.when(w + 1 < chunks)
        def _():
            scatter.swap(w).wait_send()
            partial(w + 1)
            scatter.swap(w + 1).start()

        @pl.when(v >= n - 1)
        def _():
            gather.finish(v - n + 1)
            consume(v - n + 1)

        return 0

    lax.fori_loop(0, chunks + 2 * n - 2, tick, 0)
    scatter.swap(chunks - 1).wait_send()

    def drain(q, _):
        scatter.drain(q)
        gather.drain(q)
        return 0

    lax.fori_loop(0, chunks, drain, 0)


def ffn_kernel(
    fuse, mixed_hbm, w_out_ref, input_hbm, gain_ref, w_gate_hbm, w_up_hbm, w_down_hbm, late_hbm,
    cot_hbm, resid_hbm, dgate_hbm, dup_hbm, down_hbm, gdown_hbm, *refs,
):
    outs, refs = refs[: 1 + fuse], refs[1 + fuse :]
    own, stage, cross, line, xs, xr, ls, lr, held, gs, gr, held2, gs2, gr2, *refs = refs
    w_gate, w_up, w_down, cot, hid, dg, du, down, gdown, total, mix, inp, res, *refs = refs
    wsem, csem, osem, dsem, msem, hsem, isem, rsem, *wide = refs
    chunks, blocks, rows, depth = held.shape
    units = w_gate.shape[0]
    p = Place(blocks)
    scatter = Scatter(p, own, stage, cross, line, xs, xr, ls, lr)
    gather = Gather(p, held, gs, gr)
    loads = [
        pltpu.make_async_copy(src, dst, wsem.at[i])
        for i, (src, dst) in enumerate(
            ((w_gate_hbm, w_gate), (w_up_hbm, w_up), (w_down_hbm, w_down))
        )
    ]
    for load in loads:
        load.start()
    cot_load = lambda q: pltpu.make_async_copy(cot_hbm.at[:, q], cot.at[q % 2], csem.at[q % 2])
    cot_load(0).start()
    early = cot_hbm.shape[1]
    mix_load = lambda q: pltpu.make_async_copy(mixed_hbm.at[:, q], mix, msem)
    mix_load(0).start()

    def own_rows(q):
        return pl.ds(pl.multiple_of(q * rows, rows), rows)

    in_load = lambda q: pltpu.make_async_copy(
        input_hbm.at[own_rows(q)], inp, isem
    )
    res_save = lambda q: pltpu.make_async_copy(
        res.at[q % 2], resid_hbm.at[own_rows(q)], rsem.at[q % 2]
    )
    in_load(0).start()

    def late_load(j):
        here = pl.ds(pl.multiple_of((early + j) * rows, rows), rows)
        return pltpu.make_async_copy(late_hbm.at[here], held2.at[j, p.me], hsem.at[j])

    for j in range(chunks - early):
        late_load(j).start()
    p.greet()
    later = Gather(p, held2, gs2, gr2)

    def also(w):
        for s in range(p.n - 1, -1, -1):

            @pl.when(within(w - s, chunks - early))
            def _():
                if s == 0:
                    late_load(w).wait()
                later.step(w - s, s)
                if s == p.n - 1:
                    later.finish(w - s)

    def partial(q):
        mix_load(q).wait()
        x = mix[...].reshape(blocks * rows, -1)
        for a, b in lane_tiles(depth, 512):
            put_share(
                p, own, stage, q, jnp.dot(x, w_out_ref[:, a:b], preferred_element_type=F32), a, b
            )

        @pl.when(q + 1 < chunks)
        def _():
            mix_load(q + 1).start()

    def middle(q):
        scatter.result(q, total)
        in_load(q).wait()
        @pl.when(q >= 2)
        def _():
            res_save(q - 2).wait()

        resid = inp[...].astype(F32) + total[...]
        res[q % 2] = resid
        res_save(q).start()

        @pl.when(q + 1 < chunks)
        def _():
            in_load(q + 1).start()

        normed = resid * lax.rsqrt(jnp.mean(resid * resid, axis=1, keepdims=True) + 1e-05)
        held[q, p.me] = (normed * gain_ref[...]).astype(BF16)

    def saves(q):
        slot = q % 2
        return [
            pltpu.make_async_copy(src.at[slot], dst.at[:, q], osem.at[slot, i])
            for i, (src, dst) in enumerate(((dg, dgate_hbm), (du, dup_hbm)))
        ] + [
            pltpu.make_async_copy(held.at[q], out.at[:, q], osem.at[slot, 3])
            for out in outs
            if not fuse
        ]

    def add_grad(acc, left, right):
        both = 2 * blocks * rows
        left, right = left[...].reshape(both, units), right.reshape(both, depth)
        for a, b in lane_tiles(depth, 256):
            acc[:, a:b] += mm(left, right[:, a:b], ta=True)

    def down_save(q):
        return pltpu.make_async_copy(down, down_hbm.at[:, q], osem.at[0, 2])

    def consume(q):
        slot = q % 2

        @pl.when(q == 0)
        def _():
            for load in loads:
                load.wait()
            for ref in (gdown, *wide):
                ref[...] = jnp.zeros_like(ref)

        @pl.when(q < early)
        def _():
            cot_load(q).wait()

        @pl.when(q >= early)
        def _():
            cot[slot] = held2[q - early]

        @pl.when(q >= 2)
        def _():
            for save in saves(q - 2):
                save.wait()

        if fuse:

            @pl.when(jnp.logical_and(slot == 0, q >= 2))
            def _():
                add_grad(wide[1], du, held[pl.ds(q - 2, 2)])

        x = held[q].reshape(blocks * rows, depth)
        g = cot[slot].reshape(blocks * rows, depth)
        for a, b in lane_tiles(units):
            gate = mm(x, w_gate[a:b, :], tb=True)
            up = mm(x, w_up[a:b, :], tb=True)
            gh = mm(g, w_down[a:b, :], tb=True)
            sg = sigmoid(gate)
            act = gate * sg
            shape = (blocks, rows, b - a)
            hid[slot, :, a:b] = (act * up).astype(BF16)
            dg[slot, :, :, a:b] = (
                (gh * up * sg * (1.0 + gate * (1.0 - sg))).astype(BF16).reshape(shape)
            )
            du[slot, :, :, a:b] = (gh * act).astype(BF16).reshape(shape)
        h = hid[slot]

        @pl.when(q >= 1)
        def _():
            down_save(q - 1).wait()

        for a, b in lane_tiles(depth, 512):
            down[:, :, a:b] = (
                jnp.dot(h, w_down[:, a:b], preferred_element_type=F32)
                .astype(BF16)
                .reshape(blocks, rows, b - a)
            )
        down_save(q).start()
        for save in saves(q):
            save.start()

        @pl.when(slot == 1)
        def _():
            add_grad(gdown, hid, cot[...])
            if fuse:
                add_grad(wide[0], dg, held[pl.ds(q - 1, 2)])

        @pl.when(q + 1 < early)
        def _():
            cot_load(q + 1).start()

    ticks(chunks, p.n, scatter, gather, partial, middle, consume, also)
    if fuse:
        add_grad(wide[1], du, held[pl.ds(chunks - 2, 2)])
    ends = []
    pairs = ((gdown, w_down, gdown_hbm), *zip(wide, (w_gate, w_up), outs))
    for i, (acc, low, out) in enumerate(pairs):
        low[...] = acc[...].astype(BF16)
        ends.append(pltpu.make_async_copy(low, out, dsem.at[i]))
        ends[-1].start()
    lax.fori_loop(0, chunks - early, lambda q, _: later.drain(q), None)
    for end in ends:
        end.wait()
    down_save(chunks - 1).wait()
    for q in range(max(chunks - 2, 0), chunks):
        res_save(q).wait()
    for q in range(max(chunks - 2, 0), chunks):
        for save in saves(q):
            save.wait()


def chunk_rows(blocks, owned):
    return min(owned, max(16, 2048 // (blocks * blocks)))


def early_chunks(chunks, blocks):
    return chunks - 32 * chunks // (blocks * blocks)


ANY = pl.BlockSpec(memory_space=pl.ANY)
WHOLE = pl.BlockSpec(memory_space=pltpu.VMEM)


def ffn(mixed, w_out, inputs, gain, w_gate, w_up, w_down, cot, early):
    owned, depth = inputs.shape
    blocks = mixed.shape[0] // owned
    rows = chunk_rows(blocks, owned)
    chunks = owned // rows
    units = w_gate.shape[0]
    fuse = blocks <= 8
    cut = lambda width: jax.ShapeDtypeStruct((blocks, chunks, rows, width), BF16)
    dma = pltpu.SemaphoreType.DMA
    return pl.pallas_call(
        functools.partial(ffn_kernel, fuse),
        in_specs=[ANY, WHOLE, ANY, WHOLE] + [ANY] * 5,
        out_specs=[ANY] * (6 + fuse),
        out_shape=[
            jax.ShapeDtypeStruct((owned, depth), F32),
            cut(units),
            cut(units),
            cut(depth),
            jax.ShapeDtypeStruct((units, depth), BF16),
            *([jax.ShapeDtypeStruct((units, depth), BF16)] * 2 if fuse else [cut(depth)]),
        ],
        scratch_shapes=ring_scratch(chunks, blocks, rows, depth)
        + gather_scratch(chunks, blocks, rows, depth)
        + gather_scratch(chunks - early_chunks(chunks, blocks), blocks, rows, depth)
        + [
            pltpu.VMEM(w_gate.shape, BF16),
            pltpu.VMEM(w_up.shape, BF16),
            pltpu.VMEM(w_down.shape, BF16),
            pltpu.VMEM((2, blocks, rows, depth), BF16),
            pltpu.VMEM((2, blocks * rows, units), BF16),
            pltpu.VMEM((2, blocks, rows, units), BF16),
            pltpu.VMEM((2, blocks, rows, units), BF16),
            pltpu.VMEM((blocks, rows, depth), BF16),
            pltpu.VMEM((units, depth), F32),
            pltpu.VMEM((rows, depth), F32),
            pltpu.VMEM((blocks, rows, mixed.shape[1]), BF16),
            pltpu.VMEM((rows, depth), BF16),
            pltpu.VMEM((2, rows, depth), F32),
            dma((3,)),
            dma((2,)),
            dma((2, 4)),
            dma((3,)),
            dma,
            dma((chunks - early_chunks(chunks, blocks),)),
            dma,
            dma((2,)),
            *[pltpu.VMEM((units, depth), F32)] * (2 * fuse),
        ],
        compiler_params=pltpu.CompilerParams(
            collective_id=1, has_side_effects=True, vmem_limit_bytes=127 * 512 * 1024
        ),
        name="ffn_rounds",
    )(
        mixed.reshape(blocks, chunks, rows, -1),
        w_out,
        inputs,
        gain,
        w_gate,
        w_up,
        w_down,
        cot,
        early.reshape(blocks, -1, rows, depth),
    )


def back_kernel(
    items, dgate_hbm, dup_hbm, w_gate_ref, w_up_ref, resid_hbm, gain_ref, cot_hbm, w_out_hbm, mixed_hbm, sd_hbm,
    gres_ref, ggain_ref, gout_ref, gm_hbm, rd_hbm,
    own, stage, cross, line, xs, xr, ls, lr, held, gs, gr, gm, total, gout, osem,
    dgate_ref, dup_ref, resid_ref, cot_ref, w_out_ref, mixed_ref, asem, bsem, done, *sums,
):
    chunks, blocks, rows, depth = held.shape
    p = Place(blocks)
    scatter = Scatter(p, own, stage, cross, line, xs, xr, ls, lr)
    gather = Gather(p, held, gs, gr)
    def shares(q):
        return [
            pltpu.make_async_copy(src.at[:, q], dst.at[:, q], asem.at[q, i])
            for i, (src, dst) in enumerate(((dgate_hbm, dgate_ref), (dup_hbm, dup_ref)))
        ]

    for load in shares(0):
        load.start()
    rest = [
        pltpu.make_async_copy(src, dst, bsem.at[i])
        for i, (src, dst) in enumerate(
            (
                (resid_hbm, resid_ref),
                (cot_hbm, cot_ref),
                (w_out_hbm, w_out_ref),
                (mixed_hbm, mixed_ref),
            )
        )
    ]
    p.greet(items)
    bits = items.bit_length() - 1
    reduce = Reduce(items, sd_hbm, sums[:bits], done, rd_hbm, *sums[bits:], axis=1)
    reduce.start()
    ggain_ref[...] = jnp.zeros_like(ggain_ref)

    def partial(q):
        for load in shares(q):
            load.wait()

        @pl.when(q == 0)
        def _():
            for i in range(1, chunks):
                for load in shares(i):
                    load.start()
            for load in rest:
                load.start()

        g = dgate_ref[:, q].reshape(blocks * rows, -1)
        u = dup_ref[:, q].reshape(blocks * rows, -1)
        for a, b in lane_tiles(depth, 512):
            put_share(
                p,
                own,
                stage,
                q,
                mm(g, w_gate_ref[:, a:b]) + mm(u, w_up_ref[:, a:b]),
                a,
                b,
            )

    def middle(q):
        @pl.when(q == 0)
        def _():
            for load in rest:
                load.wait()

        scatter.result(q, total)
        here = pl.ds(pl.multiple_of(q * rows, rows), rows)
        resid = resid_ref[here, :]
        n = lax.rsqrt(jnp.mean(resid * resid, axis=1, keepdims=True) + 1e-05)
        u = resid * n
        grad = total[...]
        ggain_ref[...] += jnp.sum((grad * u).reshape(rows // 8, 8, depth), axis=0)
        e = grad * gain_ref[...]
        gres = cot_ref[here, :].astype(F32) + n * (e - u * jnp.mean(e * u, axis=1, keepdims=True))
        gres_ref[here, :] = gres
        held[q, p.me] = gres.astype(BF16)

    def save(q):
        return pltpu.make_async_copy(gm.at[q % 2], gm_hbm.at[:, q], osem.at[q % 2])

    def consume(q):
        @pl.when(q >= 2)
        def _():
            save(q - 2).wait()

        @pl.when(q == 0)
        def _():
            gout[...] = jnp.zeros_like(gout)

        x = held[q].reshape(blocks * rows, depth)
        gm[q % 2] = mm(x, w_out_ref[...], tb=True).reshape(blocks, rows, -1)
        save(q).start()
        m = mixed_ref[:, q].reshape(blocks * rows, -1)
        for a, b in lane_tiles(depth, 1024):
            gout[:, a:b] += mm(m, x[:, a:b], ta=True)

    steps = reduce.handlers()

    def also(w):
        for i, step in enumerate(steps):
            at = 4 * len(steps) - 4 if i == len(steps) - 1 else 4 + 2 * i
            pl.when(w == at)(step)

    ticks(chunks, p.n, scatter, gather, partial, middle, consume, also)
    reduce.drain()
    for q in range(max(chunks - 2, 0), chunks):
        save(q).wait()
    gout_ref[...] = gout[...].astype(BF16)


def back(dgate, dup, w_gate, w_up, resid, gain, cot, w_out, mixed, grad_down, items):
    blocks, chunks, rows, _ = dgate.shape
    owned, depth = resid.shape
    width = w_out.shape[0]
    dma = pltpu.SemaphoreType.DMA
    return pl.pallas_call(
        functools.partial(back_kernel, items),
        in_specs=[ANY] * 2 + [WHOLE] * 2 + [ANY, WHOLE] + [ANY] * 4,
        out_specs=[WHOLE, WHOLE, WHOLE, ANY, ANY],
        out_shape=[
            jax.ShapeDtypeStruct((owned, depth), F32),
            jax.ShapeDtypeStruct((8, depth), F32),
            jax.ShapeDtypeStruct((width, depth), BF16),
            jax.ShapeDtypeStruct((blocks, chunks, rows, width), F32),
            jax.ShapeDtypeStruct(grad_down.shape, BF16),
        ],
        scratch_shapes=ring_scratch(chunks, blocks, rows, depth)
        + gather_scratch(chunks, blocks, rows, depth)
        + [
            pltpu.VMEM((2, blocks, rows, width), F32),
            pltpu.VMEM((rows, depth), F32),
            pltpu.VMEM((width, depth), F32),
            dma((2,)),
            pltpu.VMEM(dgate.shape, BF16),
            pltpu.VMEM(dup.shape, BF16),
            pltpu.VMEM(resid.shape, F32),
            pltpu.VMEM(cot.shape, BF16),
            pltpu.VMEM(w_out.shape, BF16),
            pltpu.VMEM((blocks, chunks, rows, width), BF16),
            dma((chunks, 2)),
            dma((4,)),
            *reduce_scratch(items, *grad_down.shape, axis=1),
        ],
        compiler_params=pltpu.CompilerParams(
            collective_id=2, has_side_effects=True, vmem_limit_bytes=63 * 1024 * 1024
        ),
        name="back_rounds",
    )(
        dgate,
        dup,
        w_gate,
        w_up,
        resid,
        gain,
        cot,
        w_out,
        mixed.reshape(blocks, chunks, rows, width),
        grad_down,
    )


def add_rows(out, left, right, count):
    size = 64 if count % 64 == 0 else 16

    def body(i, _):
        rows = lambda at: pl.ds(pl.multiple_of(at + i * size, 16), size)
        value = left[0][rows(left[1]), :].astype(F32) + right[0][rows(right[1]), :].astype(F32)
        out[0][rows(out[1]), :] = value.astype(out[0].dtype)
        return 0

    lax.fori_loop(0, count // size, body, 0)


def add_columns(out, left, right, count):
    size = 32
    total = out[0].shape[0]

    def body(i, _):
        rows = pl.ds(pl.multiple_of(i * size, size), size)
        cols = lambda at: pl.ds(pl.multiple_of(at, 128), count)
        value = left[0][rows, cols(left[1])].astype(F32) + right[0][rows, cols(right[1])].astype(F32)
        out[0][rows, cols(out[1])] = value.astype(out[0].dtype)
        return 0

    lax.fori_loop(0, total // size, body, 0)


class Reduce:
    def __init__(self, count, src, parts, done, out, ss, rr, load, save, axis=0):
        self.axis = axis
        self.add = (add_rows, add_columns)[axis]
        self.src, self.parts, self.done, self.out = src, parts, done, out
        self.ss, self.rr, self.load_sem, self.save_sem = ss, rr, load, save
        self.bits = count.bit_length() - 1
        item = lax.axis_index("item")
        total = src.shape[axis]
        self.plan = []
        for half in range(2):
            start = half * (total // 2)
            size = total // 2
            steps = []
            for k in range(self.bits):
                unit = 2 ** (k if half == 0 else self.bits - 1 - k)
                bit = (item // unit) % 2
                size //= 2
                keep = start + bit * size
                give = start + (1 - bit) * size
                steps.append((size, keep, give, bit * size, (1 - bit) * size, item + unit - 2 * unit * bit))
                start = keep
            self.plan.append(steps)

    def rows(self, ref, at, size):
        if self.axis:
            return ref.at[:, pl.ds(pl.multiple_of(at, 128), size)]
        return ref.at[pl.ds(pl.multiple_of(at, 16), size)]

    def load(self, half):
        size, keep = self.plan[half][0][:2]
        return pltpu.make_async_copy(
            self.rows(self.src, keep, size), self.rows(self.done, keep, size), self.load_sem.at[half]
        )

    def down(self, half, k):
        size, _, give, _, local, partner = self.plan[half][k]
        source = self.rows(self.src, give, size) if k == 0 else self.rows(self.parts[k - 1].at[half], local, size)
        return pltpu.make_async_remote_copy(
            src_ref=source,
            dst_ref=self.parts[k].at[half],
            send_sem=self.ss.at[half, k],
            recv_sem=self.rr.at[half, k],
            device_id={"item": partner},
            device_id_type=MESH,
        )

    def up(self, half, k, back=False):
        size, keep, give, _, _, partner = self.plan[half][k]
        ref = self.rows(self.done, give if back else keep, size)
        return pltpu.make_async_remote_copy(
            src_ref=ref,
            dst_ref=ref,
            send_sem=self.ss.at[half, self.bits + k],
            recv_sem=self.rr.at[half, self.bits + k],
            device_id={"item": partner},
            device_id_type=MESH,
        )

    def start(self):
        for half in range(2):
            self.load(half).start()
            self.down(half, 0).start()

    def halve(self, k):
        for half in range(2):
            size, keep, _, local, _, _ = self.plan[half][k]
            if k == 0:
                self.load(half).wait()
                mine = (self.done, keep)
            else:
                mine = (self.parts[k - 1].at[half], local)
            self.down(half, k).wait_recv()
            part = (self.parts[k].at[half], 0)
            if k + 1 < self.bits:
                self.add(part, mine, part, size)
                self.down(half, k + 1).start()
            else:
                self.add((self.done, keep), mine, part, size)
                self.up(half, k).start()

    def double(self, k):
        for half in range(2):
            self.up(half, k, True).wait_recv()
            self.up(half, k - 1).start()

    def save(self):
        return pltpu.make_async_copy(self.done, self.out, self.save_sem)

    def finish(self):
        for half in range(2):
            self.up(half, 0, True).wait_recv()
        self.save().start()

    def drain(self):
        for half in range(2):
            for k in range(self.bits):
                self.down(half, k).wait_send()
                self.up(half, k).wait_send()
        self.save().wait()

    def handlers(self):
        return (
            [functools.partial(self.halve, k) for k in range(self.bits)]
            + [functools.partial(self.double, k) for k in range(self.bits - 1, 0, -1)]
            + [self.finish]
        )


def reduce_scratch(count, total, width, axis=0):
    dma = pltpu.SemaphoreType.DMA
    bits = count.bit_length() - 1
    return [
        pltpu.VMEM((total, width), BF16),
        *[
            pltpu.VMEM(
                (2, total, width // 2 ** (k + 2)) if axis else (2, total // 2 ** (k + 2), width), BF16
            )
            for k in range(bits)
        ],
        dma((2, 2 * bits)),
        dma((2, 2 * bits)),
        dma((2,)),
        dma,
    ]


class Peers:
    def __init__(self, axis, count, held, ss, rr):
        self.axis, self.count, self.held, self.ss, self.rr = axis, count, held, ss, rr
        self.me = lax.axis_index(axis)

    def other(self, k):
        return (self.me + k) % self.count

    def copy(self, slot, k):
        ref = self.held.at[slot]
        return pltpu.make_async_remote_copy(
            src_ref=ref,
            dst_ref=ref,
            send_sem=self.ss.at[k],
            recv_sem=self.rr.at[slot],
            device_id={self.axis: self.other(k)},
            device_id_type=MESH,
        )

    def greet(self):
        barrier = pltpu.get_barrier_semaphore()
        for k in range(1, self.count):
            pl.semaphore_signal(
                barrier, inc=1, device_id={self.axis: self.other(k)}, device_id_type=MESH
            )

    def send(self):
        for k in range(1, self.count):
            self.copy(self.me, k).start()

    def total(self):
        for k in range(1, self.count):
            self.copy(self.other(k), k).wait_recv()
        out = self.held[0]
        for slot in range(1, self.count):
            out = out + self.held[slot]
        return out

    def drain(self):
        for k in range(1, self.count):
            self.copy(self.me, k).wait_send()


def tail_kernel(
    gq_hbm, gk_hbm, gv_hbm, gg_hbm, gdw_hbm, wq_ref, wk_ref, wv_ref, wg_ref, wdw_ref,
    input_hbm, gain_ref, gres_hbm, resid_hbm, fgain_ref, ogain_ref, conv_ref, dl_ref, wide_ref, down_hbm,
    output_ref, igrad_ref, small_ref,
    own, stage, cross, line, xs, xr, ls, lr, own2, cross2, line2, xs2, xr2, ls2, lr2, osem,
    total, ngain, held1, held2, s1, r1, s2, r2,
    gq_ref, gk_ref, gv_ref, gg_ref, gdw_ref, input_ref, gres_ref, resid_ref, asem, bsem,
):
    chunks, n, rows, depth = cross.shape
    blocks = 2 * n
    p = Place(blocks)
    first = Scatter(p, own, stage, cross, line, xs, xr, ls, lr)
    first_late = chunks - cross2.shape[0]
    second = Late(p, down_hbm, first_late, own2, cross2, line2, xs2, xr2, ls2, lr2, osem)
    sources = (
        (gq_hbm, gq_ref), (gk_hbm, gk_ref), (gv_hbm, gv_ref), (gg_hbm, gg_ref), (gdw_hbm, gdw_ref)
    )

    def shares(q):
        return [
            pltpu.make_async_copy(src.at[:, q], dst.at[:, q], asem.at[q, i])
            for i, (src, dst) in enumerate(sources)
        ]

    for load in shares(0):
        load.start()
    rest = [
        pltpu.make_async_copy(src, dst, bsem.at[i])
        for i, (src, dst) in enumerate(
            ((input_hbm, input_ref), (gres_hbm, gres_ref), (resid_hbm, resid_ref))
        )
    ]
    heads = Peers("head", held1.shape[0], held1, s1, r1)
    items = Peers("item", held2.shape[0], held2, s2, r2)
    heads.greet()
    items.greet()
    pl.semaphore_wait(pltpu.get_barrier_semaphore(), heads.count + items.count - 2)
    ngain[...] = jnp.zeros_like(ngain)
    width1 = held1.shape[2]
    half = conv_ref.shape[2] // 2
    held1[heads.me] = jnp.zeros(held1.shape[1:], F32)
    held2[items.me] = jnp.zeros(held2.shape[1:], F32)

    second.start()
    def finish_late(j):
        here = pl.ds(pl.multiple_of(j * rows, rows), rows)
        second.scatter.result(j, total)
        there = pl.ds(pl.multiple_of((first_late + j) * rows, rows), rows)
        output_ref[here, :] = (resid_ref[there, :] + total[...]).astype(BF16)

    def partial(q):
        for load in shares(q):
            load.wait()

        @pl.when(q == 0)
        def _():
            for i in range(1, chunks):
                for load in shares(i):
                    load.start()
            for load in rest:
                load.start()

        pairs = [
            (ref[:, q].reshape(blocks * rows, -1), w)
            for ref, w in ((gq_ref, wq_ref), (gk_ref, wk_ref), (gv_ref, wv_ref), (gg_ref, wg_ref))
        ]
        dw = gdw_ref[:, q].reshape(blocks * rows, -1)
        for a, b in lane_tiles(depth, 512):
            value = mm(dw, wdw_ref[:, a:b])
            for x, w in pairs:
                value = value + mm(x, w[a:b, :], tb=True)
            put_share(p, own, stage, q, value, a, b)

    partial(0)
    first.swap(0).start()
    for load in rest:
        load.wait()

    def end(q):
        here = pl.ds(pl.multiple_of(q * rows, rows), rows)
        first.result(q, total)
        x = input_ref[here, :].astype(F32)
        scale = lax.rsqrt(jnp.mean(x * x, axis=1, keepdims=True) + 1e-05)
        u = x * scale
        grad = total[...]
        ngain[...] += jnp.sum((grad * u).reshape(rows // 8, 8, depth), axis=0)
        e = grad * gain_ref[...]
        igrad_ref[here, :] = gres_ref[here, :] + scale * (
            e - u * jnp.mean(e * u, axis=1, keepdims=True)
        )

    def turn(w, _):
        pl.when(within(w - n + 1, chunks))(lambda: end(w - n + 1))
        for s in range(n - 2, 0, -1):
            pl.when(within(w - s, chunks))(lambda: first.step(w - s, s))

        @pl.when(w < chunks)
        def _():
            first.swap(w).wait_recv()
            first.step(w, 0)

        second.tick(w, finish_late)

        @pl.when(w + 1 < chunks)
        def _():
            first.swap(w).wait_send()
            partial(w + 1)
            first.swap(w + 1).start()

        return 0

    lax.fori_loop(0, chunks + n - 1, turn, 0)
    part = depth // 8
    for at, ref in ((0, ngain), (part, fgain_ref)):
        row = jnp.sum(ref[...], axis=0, keepdims=True)
        for i in range(8):
            held1[heads.me, i : i + 1, at : at + part] = row[:, i * part : (i + 1) * part]
    row = jnp.sum(ogain_ref[...], axis=0, keepdims=True)
    for i in range(2):
        held1[heads.me, i : i + 1, 2 * part : 2 * part + 128] = row[:, i * 128 : (i + 1) * 128]
    heads.send()
    for j in range(4):
        row = jnp.sum(conv_ref[j], axis=0, keepdims=True)
        for i in range(2):
            held2[items.me, 4 * i + j : 4 * i + j + 1, width1 : width1 + half] = row[
                :, i * half : (i + 1) * half
            ]
    at = width1 + half + 128
    held2[items.me, 0:1, width1 + half : at] = dl_ref[...]
    held2[items.me, :, at:] = wide_ref[...]
    held2[items.me, :, 0:width1] = heads.total()
    items.send()

    def drain(q, _):
        first.drain(q)
        return 0

    lax.fori_loop(0, chunks, drain, 0)
    second.drain()
    first.swap(chunks - 1).wait_send()
    small_ref[...] = items.total()
    heads.drain()
    items.drain()


def tail(grads, weights, inputs, gain, gres, resid, fgain, ogain, gconv, gdl, wide, down, items):
    blocks, chunks, rows, depth = down.shape
    owned = inputs.shape[0]
    n = blocks // 2
    cut = lambda value: value.reshape(blocks, chunks, rows, -1)
    width1 = depth // 4 + 128
    width2 = width1 + gconv.shape[2] // 2 + 128 + wide.size // 8
    gdl = jnp.pad(gdl, ((0, 0), (0, 128 - gdl.shape[1])))
    dma = pltpu.SemaphoreType.DMA
    one = ring_scratch(chunks, blocks, rows, depth)
    late = chunks - 3 * chunks // 4
    output, igrad, small = pl.pallas_call(
        tail_kernel,
        in_specs=[ANY] * 5 + [WHOLE] * 5 + [ANY, WHOLE, ANY, ANY] + [WHOLE] * 5 + [ANY],
        out_specs=[WHOLE] * 3,
        out_shape=[
            jax.ShapeDtypeStruct((late * rows, depth), BF16),
            jax.ShapeDtypeStruct((owned, depth), F32),
            jax.ShapeDtypeStruct((8, width2), F32),
        ],
        scratch_shapes=one
        + late_scratch(late, min(late, n), blocks, rows, depth)
        + [
            pltpu.VMEM((rows, depth), F32),
            pltpu.VMEM((8, depth), F32),
            pltpu.VMEM((blocks, 8, width1), F32),
            pltpu.VMEM((items, 8, width2), F32),
            dma((blocks,)),
            dma((blocks,)),
            dma((items,)),
            dma((items,)),
            *[pltpu.VMEM(cut(value).shape, BF16) for value in grads],
            pltpu.VMEM(inputs.shape, BF16),
            pltpu.VMEM(gres.shape, F32),
            pltpu.VMEM(resid.shape, F32),
            dma((chunks, 5)),
            dma((3,)),
        ],
        compiler_params=pltpu.CompilerParams(
            collective_id=3, has_side_effects=True, vmem_limit_bytes=63 * 1024 * 1024
        ),
        name="tail_rounds",
    )(
        *[cut(value) for value in grads],
        *weights,
        inputs,
        gain,
        gres,
        resid,
        fgain,
        ogain,
        gconv,
        gdl,
        wide.reshape(8, -1),
        down.reshape(n, 2, chunks, rows, depth),
    )
    part = depth // 8
    half = gconv.shape[2] // 2
    conv = small[:, width1 : width1 + half]
    return (
        output,
        igrad,
        small[:, :part].reshape(-1),
        small[:, part : 2 * part].reshape(-1),
        small[:2, 2 * part : 2 * part + 128].reshape(-1),
        jnp.concatenate([conv[:4], conv[4:]], axis=1),
        small[0, width1 + half : width1 + half + 128],
        small[:, width1 + half + 128 :].reshape(wide.shape),
    )


def head_kernel(
    input_ref, gain_ref, cot_hbm, wq_hbm, wk_hbm, wv_hbm, wg_hbm, wdw_ref,
    dw_ref, early_hbm, group_hbm, q_hbm, k_hbm, v_hbm, g_hbm,
    held, gs, gr, pq, pk, pv, pg, gsem, osem, esem, wsem, wq_ref, wk_ref, wv_ref, wg_ref,
):
    chunks, blocks, rows, depth = held.shape
    p = Place(blocks)
    gather = Gather(p, held, gs, gr)
    early = pltpu.make_async_copy(cot_hbm.at[0 : early_hbm.shape[0]], early_hbm, esem)
    early.start()
    loads = [
        pltpu.make_async_copy(src, dst, wsem.at[i])
        for i, (src, dst) in enumerate(
            ((wq_hbm, wq_ref), (wk_hbm, wk_ref), (wv_hbm, wv_ref), (wg_hbm, wg_ref))
        )
    ]
    p.greet()
    for q in range(chunks):
        x = input_ref[q * rows : (q + 1) * rows, :].astype(F32)
        x = x * lax.rsqrt(jnp.mean(x * x, axis=1, keepdims=True) + 1e-05)
        held[q, p.me] = (x * gain_ref[...]).astype(BF16)
        gather.step(q, 0)
    for load in loads:
        load.start()

    def saves(q):
        slot = q % 2
        return [
            pltpu.make_async_copy(src.at[slot], dst.at[:, q], osem.at[slot, i])
            for i, (src, dst) in enumerate(((pq, q_hbm), (pk, k_hbm), (pv, v_hbm), (pg, g_hbm)))
        ]

    def group_save(q):
        return pltpu.make_async_copy(held.at[q], group_hbm.at[:, q], gsem.at[q])

    def consume(q):
        gather.finish(q)
        group_save(q).start()

        @pl.when(q == 0)
        def _():
            for load in loads:
                load.wait()

        @pl.when(q >= 2)
        def _():
            for save in saves(q - 2):
                save.wait()

        x = held[q].reshape(blocks * rows, depth)
        for out, weight in ((pq, wq_ref), (pk, wk_ref), (pv, wv_ref), (pg, wg_ref)):
            for a, b in lane_tiles(weight.shape[1]):
                out[q % 2, :, :, a:b] = jnp.dot(
                    x, weight[:, a:b], preferred_element_type=F32
                ).reshape(blocks, rows, b - a)
        dw_ref[:, q] = mm(x, wdw_ref[...], tb=True).reshape(blocks, rows, -1)
        for save in saves(q):
            save.start()

    last = p.n - 1

    def turn(w, _):
        for s in range(1, p.n):

            @pl.when(jnp.logical_and(w >= s - 1, w - s + 1 < chunks))
            def _():
                gather.step(w - s + 1, s)

        @pl.when(w >= last)
        def _():
            consume(w - last)

        return 0

    lax.fori_loop(0, chunks + last, turn, 0)
    for q in range(max(chunks - 2, 0), chunks):
        for save in saves(q):
            save.wait()
    early.wait()

    def drain(q, _):
        gather.drain(q)
        group_save(q).wait()
        return 0

    lax.fori_loop(0, chunks, drain, 0)


def head(inputs, gain, cot, weights, thin, blocks):
    owned, depth = inputs.shape
    rows = chunk_rows(blocks, owned)
    chunks = owned // rows
    cut = lambda width, kind: jax.ShapeDtypeStruct((blocks, chunks, rows, width), kind)
    dma = pltpu.SemaphoreType.DMA
    return pl.pallas_call(
        head_kernel,
        in_specs=[WHOLE] * 2 + [ANY] * 5 + [WHOLE],
        out_specs=[WHOLE] + [ANY] * 6,
        out_shape=[
            cut(thin.shape[0], F32),
            jax.ShapeDtypeStruct((early_chunks(chunks, blocks) * rows, depth), BF16),
            cut(depth, BF16),
        ]
        + [cut(weight.shape[1], F32) for weight in weights],
        scratch_shapes=gather_scratch(chunks, blocks, rows, depth)
        + [pltpu.VMEM((2, blocks, rows, weight.shape[1]), F32) for weight in weights]
        + [dma((chunks,)), dma((2, 4)), dma, dma((4,))]
        + [pltpu.VMEM(weight.shape, BF16) for weight in weights],
        compiler_params=pltpu.CompilerParams(
            collective_id=4, has_side_effects=True, vmem_limit_bytes=62 * 1024 * 1024
        ),
        name="head_rounds",
    )(inputs, gain, cot, *weights, thin)


def widen_kernel(count, *refs):
    for source, out in zip(refs[:count], refs[count:]):
        out[...] = source[...].astype(F32)


def widen(values, parts):
    spec = [
        pl.BlockSpec((value.shape[0] // parts, value.shape[1]), lambda i: (i, 0)) for value in values
    ]
    return pl.pallas_call(
        functools.partial(widen_kernel, len(values)),
        grid=(parts,),
        in_specs=spec,
        out_specs=spec,
        out_shape=[jax.ShapeDtypeStruct(value.shape, F32) for value in values],
        compiler_params=pltpu.CompilerParams(
            dimension_semantics=("arbitrary",), vmem_limit_bytes=63 * 1024 * 1024
        ),
        name="widen",
    )(*values)


def inner_rows(left, right):
    return lax.dot_general(
        left, right, (((0,), (0,)), ((), ())), preferred_element_type=jnp.float32
    )


def gather(values):
    return lax.all_gather(values.astype(jnp.bfloat16), "head", axis=0, tiled=True)


def scatter(values):
    return lax.psum_scatter(values, "head", scatter_dimension=0, tiled=True)


def total(values):
    return lax.psum([value.astype(jnp.bfloat16) for value in values], "item")


def after(values, *earlier):
    return lax.optimization_barrier((values, earlier))[0]


def local(
    items,
    blocks,
    layer_input,
    lengths,
    norm_gain,
    w_query,
    w_key,
    w_value,
    w_outgate,
    w_decay,
    w_write,
    conv_query,
    conv_key,
    conv_value,
    decay_log,
    out_gain,
    w_out,
    ffn_gain,
    w_gate,
    w_up,
    w_down,
    cotangent,
):
    ng = norm_gain.astype(F32).reshape(1, -1)
    fg = ffn_gain.astype(F32).reshape(1, -1)
    og = out_gain.astype(F32).reshape(1, DV)
    conv = jnp.concatenate([conv_query, conv_key, conv_value], axis=1).astype(F32)
    dl = decay_log.reshape(1, -1)
    w_dw = jnp.concatenate([w_decay.T, w_write.T], axis=0)
    gate_t, up_t = w_gate.T, w_up.T
    owned, depth = layer_input.shape
    tokens = owned * blocks
    flat = lambda value: value.reshape(tokens, -1)
    by_seq = lambda value: value.reshape(-1, SEQ_LEN, value.shape[-1])
    raw_dw, early, group, *raw = head(
        layer_input, ng, cotangent, (w_query, w_key, w_value, w_outgate), w_dw, blocks
    )
    group = flat(group)
    early = gather(early)
    raw = [by_seq(flat(value)) for value in (*raw, raw_dw)]
    mixed, *kept = mixer_fwd(lengths, *raw, conv, dl, og)
    mixed = flat(mixed)
    resid, dgate, dup, down, grad_down, *rest = ffn(
        mixed, w_out, layer_input, fg, gate_t, up_t, w_down, cotangent, early
    )
    if len(rest) == 1:
        rest = [inner_rows(flat(value), flat(rest[0])) for value in (dgate, dup)]
    ffn_sums = total(rest)
    grad_resid, fgain, grad_w_out, grad_mixed, down_sum = back(
        dgate, dup, gate_t, up_t, resid, fg, cotangent, w_out, mixed, grad_down, items
    )
    backward = mixer_bwd(
        lengths, *raw, conv, dl, og, by_seq(flat(grad_mixed)), *kept, by_seq(group), resid, down,
        grad_w_out, items
    )
    grads, (gconv, gdl, ogain), wide, thin = backward[:5], backward[5:8], backward[8:12], backward[12]
    first, out_sum = backward[13:]
    mix_sums = total(after(list(wide), ffn_sums))
    grads = [flat(value) for value in grads]
    output, input_grad, ngain, fgain, ogain, conv_grad, dl_grad, thin = tail(
        grads,
        (w_query, w_key, w_value, w_outgate, w_dw),
        layer_input,
        ng,
        grad_resid,
        resid,
        fgain,
        ogain,
        gconv,
        gdl,
        thin,
        down,
        items,
    )
    output = jnp.concatenate([first, output])
    gate_sum, up_sum, down_sum, out_sum = widen(
        (*ffn_sums, down_sum, out_sum), w_down.shape[0] // 176
    )
    heads = dl.shape[1]
    qw = w_query.shape[1]
    return (
        output,
        input_grad,
        ngain,
        *widen(mix_sums, 8),
        thin[:heads].T,
        thin[heads:].T,
        conv_grad[:, :qw],
        conv_grad[:, qw : 2 * qw],
        conv_grad[:, 2 * qw :],
        dl_grad[:heads],
        ogain,
        out_sum,
        fgain,
        gate_sum.T,
        up_sum.T,
        down_sum,
    )


def solution(mesh):
    rows = P(("item", "head"), None)
    cols = P(None, "head")
    deep = P("head", None)
    return jax.shard_map(
        functools.partial(local, mesh.shape["item"], mesh.shape["head"]),
        mesh=mesh,
        in_specs=(rows, P("item"), P(), *[cols] * 9, P("head"), P(), deep, P(), cols, cols, deep, rows),
        out_specs=(rows, rows, P(), *[cols] * 9, P("head"), P(), deep, P(), cols, cols, deep),
        check_vma=False,
    )
```

```python
import functools

import jax
import jax.numpy as jnp
from jax import lax
from jax.experimental import pallas as pl
from jax.experimental.pallas import tpu as pltpu
from jax.sharding import PartitionSpec as P

DK = 128
DV = 256
SEQ_LEN = 1024
CHUNK = 128
F32 = jnp.float32
BF16 = jnp.bfloat16


def mm(left, right, ta=False, tb=False):
    return lax.dot_general(
        left.astype(BF16),
        right.astype(BF16),
        (((0 if ta else 1,), (1 if tb else 0,)), ((), ())),
        preferred_element_type=F32,
    )


def split(value):
    high = value.astype(BF16)
    return high, (value - high.astype(F32)).astype(BF16)


def mm3(left, right):
    lh, ll = left
    rh, rl = right
    return mm(lh, rh) + (mm(lh, rl) + mm(ll, rh))


def sigmoid(x):
    return 1.0 / (1.0 + jnp.exp(-x))


def grids():
    rows = lax.broadcasted_iota(jnp.int32, (CHUNK, CHUNK), 0)
    cols = lax.broadcasted_iota(jnp.int32, (CHUNK, CHUNK), 1)
    return rows, cols


def to_row(col, eye):
    return jnp.sum(jnp.where(eye, col, 0.0), axis=0, keepdims=True)


def inverses(mats, rows, cols):
    eye = jnp.where(rows == cols, 1.0, 0.0)
    near = rows // 8 == cols // 8
    n1 = [jnp.where(near, -a, 0.0) for a in mats]
    n1s = [split(n) for n in n1]
    n2 = [mm3(n, n) for n in n1s]
    n2s = [split(n) for n in n2]
    n3 = [mm3(a, b) for a, b in zip(n1s, n2s)]
    n4s = [split(mm3(n, n)) for n in n2s]
    p1 = [eye + a + b + c for a, b, c in zip(n1, n2, n3)]
    x = [p + mm3(split(p), n) for p, n in zip(p1, n4s)]
    size = 8
    while size < CHUNK:
        pair = (rows // (2 * size) == cols // (2 * size)) & (rows // size != cols // size)
        xs = [v.astype(BF16) for v in x]
        bx = [mm(jnp.where(pair, a, 0.0), v) for a, v in zip(mats, xs)]
        x = [v - mm(vs, w) for v, vs, w in zip(x, xs, bx)]
        size *= 2
    return x


def decays(ld, eye, causal):
    row = to_row(ld, eye)
    g = jnp.sum(jnp.where(causal, row, 0.0), axis=1, keepdims=True)
    grow = to_row(g, eye)
    d = jnp.where(causal, jnp.exp(jnp.where(causal, g - grow, 0.0)), 0.0)
    last = g[CHUNK - 1 : CHUNK, :]
    return d, jnp.exp(g), jnp.exp(last - g), jnp.exp(last)


def live_mask(len_ref, s, c):
    spot = lax.broadcasted_iota(jnp.int32, (CHUNK, 1), 0) + c * CHUNK
    return jnp.where(spot < len_ref[s], 1.0, 0.0)


def softplus(x):
    return jnp.maximum(x, 0.0) + jnp.log1p(jnp.exp(-jnp.abs(x)))


def mix_fwd_kernel(
    len_ref, q_ref, k_ref, v_ref, g_ref, dw_ref, conv_ref, dl_ref, gain_ref,
    mixed_ref, pre_ref, o_ref, u_ref, t_ref, s_ref, buf, state,
):
    c = pl.program_id(0)
    seqs, _, raws = buf.shape
    heads = dl_ref.shape[1]
    qw = heads * DK
    pieces = ((q_ref, 0, qw), (k_ref, qw, 2 * qw), (v_ref, 2 * qw, raws))

    @pl.when(c == 0)
    def _():
        buf[:, 0:8, :] = jnp.zeros((seqs, 8, raws), F32)
        state[...] = jnp.zeros_like(state)

    rows, cols = grids()
    eye = rows == cols
    causal = rows >= cols
    lower = rows > cols
    rate = jnp.exp(dl_ref[...])
    st = []
    for s in range(seqs):
        for ref, a, b in pieces:
            buf[s, 8 : 8 + CHUNK, a:b] = ref[s]
        pre = conv_ref[0:1, :] * buf[s, 5 : 5 + CHUNK, :]
        for j in range(1, 4):
            pre = pre + conv_ref[j : j + 1, :] * buf[s, 5 + j : 5 + j + CHUNK, :]
        pre_ref[s] = pre
        buf[s, 0:8, :] = buf[s, CHUNK : CHUNK + 8, :]
        act = pre * sigmoid(pre)
        mask = live_mask(len_ref, s, c)
        x = dw_ref[s]
        ld2 = -rate * softplus(x[:, :heads]) * mask
        be2 = sigmoid(x[:, heads:]) * mask
        for h in range(heads):
            q = act[:, h * DK : (h + 1) * DK]
            k = act[:, qw + h * DK : qw + (h + 1) * DK]
            v = act[:, 2 * qw + h * DV : 2 * qw + (h + 1) * DV]
            q = q * (lax.rsqrt(jnp.sum(q * q, axis=1, keepdims=True) + 1e-06) * DK ** (-0.5))
            k = k * lax.rsqrt(jnp.sum(k * k, axis=1, keepdims=True) + 1e-06)
            be = be2[:, h : h + 1]
            d, ga, e, el = decays(ld2[:, h : h + 1], eye, causal)
            qb = q.astype(BF16)
            kb = k.astype(BF16)
            qk = jnp.concatenate([qb, kb], axis=0)
            both = mm(qk, kb, tb=True)
            w = d * both[:CHUNK]
            a = jnp.where(lower, d * both[CHUNK:], 0.0) * be
            st.append((s, h, mask, v, be, ga, e, el, qk, kb, w, a))
    inv = inverses([z[-1] for z in st], rows, cols)
    for i, (s, h, mask, v, be, ga, e, el, qk, kb, w, a) in enumerate(st):
        t = inv[i].astype(BF16)
        old = state[i]
        oldb = old.astype(BF16)
        s_ref[i] = oldb
        t_ref[i] = t
        qks = mm(qk, oldb)
        r = be * (v - ga * qks[CHUNK:])
        u = mm(t, r)
        ub = u.astype(BF16)
        u_ref[s, :, h * DV : (h + 1) * DV] = ub
        o = ga * qks[:CHUNK] + mm(w, ub)
        state[i] = el * old + mm(kb, e * u, ta=True)
        o = o * mask
        o_ref[s, :, h * DV : (h + 1) * DV] = o
        rg = g_ref[s, :, h * DV : (h + 1) * DV]
        n = o * lax.rsqrt(jnp.mean(o * o, axis=1, keepdims=True) + 1e-05) * gain_ref[...]
        mixed_ref[s, :, h * DV : (h + 1) * DV] = (n * (rg * sigmoid(rg))).astype(BF16)


def mix_bwd_kernel(
    items, len_ref, q_ref, k_ref, v_ref, g_ref, dw_ref, conv_ref, dl_ref, gain_ref,
    gm_ref, pre_ref, o_ref, u_ref, t_ref, s_ref, group_ref, resid_ref, down_hbm, so_hbm,
    gq_ref, gk_ref, gv_ref, gg_ref, gdw_ref, gconv_ref, gdl_ref, ggain_ref,
    wq_ref, wk_ref, wv_ref, wg_ref, thin_ref, output_ref, ro_hbm, buf, dstate, weights,
    own, cross, line, xs, xr, ls, lr, osem, spare, done, *sums,
):
    step = pl.program_id(0)
    c = pl.num_programs(0) - 1 - step
    place = Place(2 * cross.shape[1])
    summing = Late(place, down_hbm, 0, own, cross, line, xs, xr, ls, lr, osem)

    bits = items.bit_length() - 1
    reduce = Reduce(items, so_hbm, sums[:bits], done, ro_hbm, *sums[bits:])

    @pl.when(step == 0)
    def _():
        place.greet(items)
        reduce.start()
        summing.start()

    steps = reduce.handlers()
    for i, handler in enumerate(steps):
        at = SEQ_LEN // CHUNK - 1 if i == len(steps) - 1 else SEQ_LEN // CHUNK - 1 - len(steps) + i
        pl.when(step == at)(handler)

    def add_output(q):
        size = spare.shape[0]
        here = pl.ds(pl.multiple_of(q * size, size), size)
        summing.scatter.result(q, spare)
        output_ref[here, :] = (resid_ref[here, :] + spare[...]).astype(BF16)

    total_ticks = cross.shape[0] + place.n - 1
    spans = 2 * (SEQ_LEN // CHUNK) - 1

    def run_ticks(place_at):
        def tick(w, _):
            summing.tick(w, add_output)
            return 0

        first = (place_at * total_ticks + spans - 1) // spans
        lax.fori_loop(first, ((place_at + 1) * total_ticks + spans - 1) // spans, tick, 0)

    pl.when(step >= 1)(lambda: run_ticks(2 * step - 1))
    seqs, _, raws = buf.shape
    heads = dl_ref.shape[1]
    qw = heads * DK
    pieces = ((q_ref, 0, qw), (k_ref, qw, 2 * qw), (v_ref, 2 * qw, raws))

    @pl.when(step == 0)
    def _():
        buf[:, CHUNK : CHUNK + 8, :] = jnp.zeros((seqs, 8, raws), F32)
        dstate[...] = jnp.zeros_like(dstate)
        gconv_ref[...] = jnp.zeros_like(gconv_ref)
        gdl_ref[...] = jnp.zeros_like(gdl_ref)
        ggain_ref[...] = jnp.zeros_like(ggain_ref)
        weights[...] = jnp.zeros_like(weights)
        thin_ref[...] = jnp.zeros_like(thin_ref)

    rows, cols = grids()
    eye = rows == cols
    causal = rows >= cols
    lower = rows > cols
    later = rows <= cols
    rate = jnp.exp(dl_ref[...])
    gain = gain_ref[...]
    for s in range(seqs):
        if s == seqs // 2:
            run_ticks(2 * step)
        mask = live_mask(len_ref, s, c)
        x = dw_ref[s]
        soft = -rate * mask
        ld2 = soft * softplus(x[:, :heads])
        sg = sigmoid(x)
        be2 = sg[:, heads:] * mask
        dlds = []
        dbes = []
        for h in range(heads):
            i = heads * s + h
            vs = slice(h * DV, (h + 1) * DV)
            gm = gm_ref[s, :, vs]
            o = o_ref[s, :, vs]
            rg = g_ref[s, :, h * DV : (h + 1) * DV]
            sr = sigmoid(rg)
            r = lax.rsqrt(jnp.mean(o * o, axis=1, keepdims=True) + 1e-05)
            un = o * r
            gsg = gm * sr
            gg_ref[s, :, h * DV : (h + 1) * DV] = (
                gsg * (un * gain) * (1.0 + rg * (1.0 - sr))
            ).astype(BF16)
            dn = gsg * rg
            dnu = dn * un
            ggain_ref[...] += jnp.sum(dnu.reshape(CHUNK // 8, 8, DV), axis=0)
            do = (r * mask) * (dn * gain - un * jnp.mean(dnu * gain, axis=1, keepdims=True))
            pq = pre_ref[s, :, h * DK : (h + 1) * DK]
            pk = pre_ref[s, :, qw + h * DK : qw + (h + 1) * DK]
            pv = pre_ref[s, :, 2 * qw + h * DV : 2 * qw + (h + 1) * DV]
            sq = sigmoid(pq)
            sk = sigmoid(pk)
            sv = sigmoid(pv)
            q = pq * sq
            k = pk * sk
            v = pv * sv
            rq = lax.rsqrt(jnp.sum(q * q, axis=1, keepdims=True) + 1e-06)
            rk = lax.rsqrt(jnp.sum(k * k, axis=1, keepdims=True) + 1e-06)
            q = q * rq
            k = k * rk
            scale = DK ** (-0.5)
            be = be2[:, h : h + 1]
            d, ga, e, el = decays(ld2[:, h : h + 1], eye, causal)
            qb = (q * scale).astype(BF16)
            kb = k.astype(BF16)
            qk = jnp.concatenate([qb, kb], axis=0)
            both = mm(qk, kb, tb=True)
            w = d * both[:CHUNK]
            ab = jnp.where(lower, d * both[CHUNK:], 0.0)
            a = ab * be
            t = t_ref[i]
            st = s_ref[i]
            u = u_ref[s, :, vs]
            dh = dstate[i]
            dhb = dh.astype(BF16)
            qks = mm(qk, st)
            dob = do.astype(BF16)
            kdh = e * mm(kb, dhb)
            ubar = mm(w, dob, ta=True) + kdh
            rbar = mm(t, ubar, ta=True)
            rb = rbar.astype(BF16)
            uu = mm(jnp.concatenate([dob, rb], axis=0), u, tb=True)
            wbar = jnp.where(causal, uu[:CHUNK], 0.0)
            abar = -jnp.where(lower, uu[CHUNK:], 0.0)
            gks = ga * qks[CHUNK:]
            dv = be * rbar
            y = -ga * dv
            z = ga * do
            zy = jnp.concatenate([z.astype(BF16), y.astype(BF16)], axis=0)
            zys = mm(zy, st, tb=True)
            p = (wbar * d).astype(BF16)
            m = abar * d * be
            eu = e * u.astype(F32)
            dq = zys[:CHUNK] + mm(p, kb)
            dk = (
                zys[CHUNK:]
                + mm(p, qb, ta=True)
                + mm(m, kb)
                + mm(m, kb, ta=True)
                + mm(eu, dhb, tb=True)
            )
            dstate[i] = el * dh + mm(qk, zy, ta=True)
            ee = wbar * w + abar * a
            f = jnp.sum(u.astype(F32) * kdh, axis=1, keepdims=True)
            dbe = jnp.sum(rbar * (v - gks), axis=1, keepdims=True) + jnp.sum(
                abar * ab, axis=1, keepdims=True
            )
            dgc = (
                jnp.sum(ee, axis=1, keepdims=True)
                + jnp.sum(z * qks[:CHUNK] - dv * gks, axis=1, keepdims=True)
                - f
            )
            dgr = to_row(dgc, eye) - jnp.sum(ee, axis=0, keepdims=True)
            total = jnp.sum(f, axis=0, keepdims=True) + el * jnp.sum(
                jnp.sum(st.astype(F32) * dh, axis=1, keepdims=True), axis=0, keepdims=True
            )
            dld = jnp.sum(jnp.where(later, dgr, 0.0), axis=1, keepdims=True) + total
            dlds.append(dld)
            dbes.append(dbe)
            dq = dq * scale
            dqa = rq * (dq - q * jnp.sum(q * dq, axis=1, keepdims=True))
            dka = rk * (dk - k * jnp.sum(k * dk, axis=1, keepdims=True))
            buf[s, 0:CHUNK, h * DK : (h + 1) * DK] = dqa * sq * (1.0 + pq * (1.0 - sq))
            buf[s, 0:CHUNK, qw + h * DK : qw + (h + 1) * DK] = dka * sk * (1.0 + pk * (1.0 - sk))
            buf[s, 0:CHUNK, 2 * qw + h * DV : 2 * qw + (h + 1) * DV] = dv * sv * (1.0 + pv * (1.0 - sv))
        dld2 = jnp.concatenate(dlds, axis=1) if heads > 1 else dlds[0]
        dbe2 = jnp.concatenate(dbes, axis=1) if heads > 1 else dbes[0]
        gdw_ref[s] = jnp.concatenate(
            [dld2 * soft * sg[:, :heads], dbe2 * be2 * (1.0 - sg[:, heads:])], axis=1
        ).astype(BF16)
        gdl_ref[...] += jnp.sum(dld2 * ld2, axis=0, keepdims=True)
        for (ref, a, b), out in zip(pieces, (gq_ref, gk_ref, gv_ref)):
            raw = ref[s]
            draw = None
            for j in range(4):
                shifted = buf[s, 3 - j : 3 - j + CHUNK, a:b]
                gconv_ref[j, :, a:b] += jnp.sum(
                    (raw * shifted).reshape(CHUNK // 8, 8, b - a), axis=0
                )
                term = conv_ref[j : j + 1, a:b] * shifted
                draw = term if draw is None else draw + term
            out[s] = draw.astype(BF16)
        buf[s, CHUNK : CHUNK + 8, :] = buf[s, 0:8, :]
    x = group_ref[...].reshape(seqs * CHUNK, -1)
    flat = lambda ref: ref[...].reshape(seqs * CHUNK, -1)
    joined = jnp.concatenate([flat(ref) for ref in (gq_ref, gk_ref, gv_ref, gg_ref)], axis=1)
    for a in range(0, x.shape[1], 256):
        weights[a : a + 256, :] += mm(x[:, a : a + 256], joined, ta=True)
    thin_ref[...] += mm(gdw_ref[...].reshape(seqs * CHUNK, -1), x, ta=True)

    @pl.when(c == 0)
    def _():
        at = 0
        for out in (wq_ref, wk_ref, wv_ref, wg_ref):
            out[...] = weights[:, at : at + out.shape[1]].astype(BF16)
            at += out.shape[1]

        summing.drain()
        reduce.drain()


def mixer_fwd(lengths, q, k, v, g, dw, conv, dl, gain):
    count = SEQ_LEN // CHUNK
    seqs = q.shape[0]
    heads = dl.shape[1]
    raws, vw, n = conv.shape[1], heads * DV, seqs * heads
    full = lambda shape: pl.BlockSpec(shape, lambda c: (0,) * len(shape))
    seq = lambda width: pl.BlockSpec((seqs, CHUNK, width), lambda c: (0, c, 0))
    return pl.pallas_call(
        mix_fwd_kernel,
        grid=(count,),
        in_specs=[
            pl.BlockSpec(memory_space=pltpu.SMEM),
            seq(q.shape[2]),
            seq(k.shape[2]),
            seq(vw),
            seq(vw),
            seq(2 * heads),
            full((4, raws)),
            full((1, heads)),
            full((1, DV)),
        ],
        out_specs=[
            seq(vw),
            seq(raws),
            seq(vw),
            seq(vw),
            pl.BlockSpec((n, None, CHUNK, CHUNK), lambda c: (0, c, 0, 0)),
            pl.BlockSpec((n, None, DK, DV), lambda c: (0, c, 0, 0)),
        ],
        out_shape=[
            jax.ShapeDtypeStruct((seqs, SEQ_LEN, vw), BF16),
            jax.ShapeDtypeStruct((seqs, SEQ_LEN, raws), F32),
            jax.ShapeDtypeStruct((seqs, SEQ_LEN, vw), F32),
            jax.ShapeDtypeStruct((seqs, SEQ_LEN, vw), BF16),
            jax.ShapeDtypeStruct((n, count, CHUNK, CHUNK), BF16),
            jax.ShapeDtypeStruct((n, count, DK, DV), BF16),
        ],
        scratch_shapes=[
            pltpu.VMEM((seqs, CHUNK + 8, raws), F32),
            pltpu.VMEM((n, DK, DV), F32),
        ],
        compiler_params=pltpu.CompilerParams(
            dimension_semantics=("arbitrary",), vmem_limit_bytes=48 * 1024 * 1024
        ),
        name="mixer_forward",
    )(lengths, q, k, v, g, dw, conv, dl, gain)


def mixer_bwd(lengths, q, k, v, g, dw, conv, dl, gain, gm, pre, o, u, t, s, group, resid, down, grad_out, items):
    count = SEQ_LEN // CHUNK
    seqs = q.shape[0]
    heads = dl.shape[1]
    raws, vw, n = conv.shape[1], heads * DV, seqs * heads
    depth = group.shape[2]
    blocks, chunks, rows, _ = down.shape
    early = 3 * chunks // 4
    wide = [(depth, value.shape[2]) for value in (q, k, v, g)] + [(dw.shape[2], depth)]
    full = lambda shape: pl.BlockSpec(shape, lambda c: (0,) * len(shape))
    seq = lambda width: pl.BlockSpec((seqs, CHUNK, width), lambda c: (0, count - 1 - c, 0))
    return pl.pallas_call(
        functools.partial(mix_bwd_kernel, items),
        grid=(count,),
        in_specs=[
            pl.BlockSpec(memory_space=pltpu.SMEM),
            seq(q.shape[2]),
            seq(k.shape[2]),
            seq(vw),
            seq(vw),
            seq(2 * heads),
            full((4, raws)),
            full((1, heads)),
            full((1, DV)),
            seq(vw),
            seq(raws),
            seq(vw),
            seq(vw),
            pl.BlockSpec((n, None, CHUNK, CHUNK), lambda c: (0, count - 1 - c, 0, 0)),
            pl.BlockSpec((n, None, DK, DV), lambda c: (0, count - 1 - c, 0, 0)),
            seq(group.shape[2]),
            full((early * rows, depth)),
            pl.BlockSpec(memory_space=pl.ANY),
            pl.BlockSpec(memory_space=pl.ANY),
        ],
        out_specs=[
            seq(q.shape[2]),
            seq(k.shape[2]),
            seq(vw),
            seq(vw),
            seq(2 * heads),
            full((4, 8, raws)), full((1, heads)),
            full((8, DV)),
            *[full(shape) for shape in wide],
            full((early * rows, depth)),
            pl.BlockSpec(memory_space=pl.ANY),
        ],
        out_shape=[
            jax.ShapeDtypeStruct(q.shape, BF16),
            jax.ShapeDtypeStruct(k.shape, BF16),
            jax.ShapeDtypeStruct(v.shape, BF16),
            jax.ShapeDtypeStruct(g.shape, BF16),
            jax.ShapeDtypeStruct(dw.shape, BF16),
            jax.ShapeDtypeStruct((4, 8, raws), F32),
            jax.ShapeDtypeStruct((1, heads), F32),
            jax.ShapeDtypeStruct((8, DV), F32),
            *[jax.ShapeDtypeStruct(shape, BF16) for shape in wide[:4]],
            jax.ShapeDtypeStruct(wide[4], F32),
            jax.ShapeDtypeStruct((early * rows, depth), BF16),
            jax.ShapeDtypeStruct(grad_out.shape, BF16),
        ],
        scratch_shapes=[
            pltpu.VMEM((seqs, CHUNK + 8, raws), F32),
            pltpu.VMEM((n, DK, DV), F32),
            pltpu.VMEM((depth, sum(shape[1] for shape in wide[:4])), F32),
            *late_scratch(early, min(early, blocks // 2), blocks, rows, depth),
            pltpu.VMEM((rows, depth), F32),
            *reduce_scratch(items, *grad_out.shape),
        ],
        compiler_params=pltpu.CompilerParams(
            dimension_semantics=("arbitrary",),
            vmem_limit_bytes=62 * 1024 * 1024,
            collective_id=5,
            has_side_effects=True,
        ),
        name="mixer_backward",
    )(
        lengths,
        q,
        k,
        v,
        g,
        dw,
        conv,
        dl,
        gain,
        gm,
        pre,
        o,
        u,
        t,
        s,
        group,
        resid,
        down.reshape(blocks // 2, 2, chunks, rows, depth),
        grad_out,
    )


MESH = pl.DeviceIdType.MESH


class Place:
    def __init__(self, blocks):
        head = lax.axis_index("head")
        self.n = blocks // 2
        self.me = head
        self.z = head // 2
        self.c = head % 2
        self.mate = 2 * self.z + 1 - self.c
        self.right = head + 2
        self.left = head - 2
        self.has_right = self.z < self.n - 1
        self.has_left = self.z > 0

    def greet(self, items=1):
        barrier = pltpu.get_barrier_semaphore()
        item = lax.axis_index("item")
        for k in range(1, items):
            pl.semaphore_signal(
                barrier, inc=1, device_id={"item": (item + k) % items}, device_id_type=MESH
            )

        def hello(device):
            pl.semaphore_signal(barrier, inc=1, device_id={"head": device}, device_id_type=MESH)

        hello(self.mate)
        pl.when(self.has_right)(lambda: hello(self.right))
        pl.when(self.has_left)(lambda: hello(self.left))
        n = self.n
        pl.semaphore_wait(barrier, items + (self.z + n - 1) // n + (2 * n - 2 - self.z) // n)


def remote(src, dst, send, recv, device):
    return pltpu.make_async_remote_copy(
        src_ref=src,
        dst_ref=dst,
        send_sem=send,
        recv_sem=recv,
        device_id={"head": device},
        device_id_type=MESH,
    )


class Scatter:
    def __init__(self, place, own, stage, cross, line, xs, xr, ls, lr):
        self.p = place
        self.own, self.stage, self.cross, self.line = own, stage, cross, line
        self.xs, self.xr, self.ls, self.lr = xs, xr, ls, lr

    def swap(self, q):
        return remote(
            self.stage, self.cross.at[q], self.xs.at[q], self.xr.at[q], self.p.mate
        )

    def hop(self, q, slot, device):
        ref = self.line.at[q, slot]
        return remote(ref, ref, self.ls.at[q, slot], self.lr.at[q, slot], device)

    def share(self, q, t):
        return self.own[q % self.own.shape[0], t].astype(F32) + self.cross[q, t].astype(F32)

    def pass_on(self, q, t, slot, first, device):
        @pl.when(first)
        def _():
            self.line[q, slot] = self.share(q, t).astype(BF16)

        @pl.when(jnp.logical_not(first))
        def _():
            self.hop(q, slot, device).wait_recv()
            self.line[q, slot] = (self.share(q, t) + self.line[q, slot].astype(F32)).astype(BF16)

        self.hop(q, slot, device).start()

    def right_at(self, s):
        return self.p.n - 1 - s + self.p.z

    def left_at(self, s):
        n = self.p.n
        t = s + 1 - n + self.p.z
        return t, (t + n) % (n + 1)

    def step(self, q, s):
        p = self.p

        @pl.when(p.z <= s)
        def _():
            t = self.right_at(s)
            self.pass_on(q, t, t, p.z == 0, p.right)

        @pl.when(p.n - 1 - p.z <= s)
        def _():
            t, slot = self.left_at(s)
            self.pass_on(q, t, slot, p.z == p.n - 1, p.left)

    def result(self, q, total):
        p = self.p
        total[...] = self.share(q, p.z)

        @pl.when(p.has_left)
        def _():
            self.hop(q, p.z, p.right).wait_recv()
            total[...] += self.line[q, p.z].astype(F32)

        @pl.when(p.has_right)
        def _():
            slot = (p.z + p.n) % (p.n + 1)
            self.hop(q, slot, p.left).wait_recv()
            total[...] += self.line[q, slot].astype(F32)

    def drain(self, q):
        p = self.p
        for s in range(p.n - 1):

            @pl.when(p.z <= s)
            def _():
                self.hop(q, self.right_at(s), p.right).wait_send()

            @pl.when(p.n - 1 - p.z <= s)
            def _():
                self.hop(q, self.left_at(s)[1], p.left).wait_send()


class Late:
    def __init__(self, place, src, first, own, cross, line, xs, xr, ls, lr, osem):
        self.p, self.src, self.first = place, src, first
        self.count = cross.shape[0]
        self.own, self.cross, self.osem = own, cross, osem
        self.xs, self.xr = xs, xr
        self.scatter = Scatter(place, own, None, cross, line, xs, xr, ls, lr)

    def swap(self, q):
        return remote(
            self.src.at[:, 1 - self.p.c, self.first + q],
            self.cross.at[q],
            self.xs.at[q],
            self.xr.at[q],
            self.p.mate,
        )

    def load(self, q):
        slot = q % self.own.shape[0]
        return pltpu.make_async_copy(
            self.src.at[:, self.p.c, self.first + q], self.own.at[slot], self.osem.at[slot]
        )

    def start(self):
        for q in range(self.count):
            self.swap(q).start()
        for q in range(self.own.shape[0]):
            self.load(q).start()

    def enter(self, q):
        self.load(q).wait()
        self.swap(q).wait_recv()
        self.scatter.step(q, 0)

    def tick(self, w, result):
        n = self.p.n

        @pl.when(within(w - n + 1, self.count))
        def _():
            result(w - n + 1)
            slots = self.own.shape[0]

            @pl.when(w - n + 1 + slots < self.count)
            def _():
                self.load(w - n + 1 + slots).start()

        for s in range(n - 2, 0, -1):

            @pl.when(within(w - s, self.count))
            def _():
                self.scatter.step(w - s, s)

        @pl.when(w < self.count)
        def _():
            self.enter(w)

    def drain(self):
        def body(q, _):
            self.scatter.drain(q)
            self.swap(q).wait_send()
            return 0

        lax.fori_loop(0, self.count, body, 0)


def late_scratch(count, slots, blocks, rows, depth):
    n = blocks // 2
    dma = pltpu.SemaphoreType.DMA
    return [
        pltpu.VMEM((slots, n, rows, depth), BF16),
        pltpu.VMEM((count, n, rows, depth), BF16),
        pltpu.VMEM((count, n + 1, rows, depth), BF16),
        dma((count,)),
        dma((count,)),
        dma((count, n + 1)),
        dma((count, n + 1)),
        dma((slots,)),
    ]


class Gather:
    def __init__(self, place, held, ss, rr):
        self.p, self.held, self.ss, self.rr = place, held, ss, rr

    def copy(self, q, kind, z):
        p = self.p
        block = 2 * z + p.c
        ref = self.held.at[q, block]
        device = (p.right, p.left, p.mate)[kind]
        return remote(ref, ref, self.ss.at[q, kind, z], self.rr.at[q, block], device)

    def step(self, q, s):
        p = self.p
        if s == 0:
            pl.when(p.has_right)(lambda: self.copy(q, 0, p.z).start())
            pl.when(p.has_left)(lambda: self.copy(q, 1, p.z).start())
            self.copy(q, 2, p.z).start()
            return

        @pl.when(p.z >= s)
        def _():
            z = p.z - s
            self.copy(q, 0, z).wait_recv()
            pl.when(p.has_right)(lambda: self.copy(q, 0, z).start())
            self.copy(q, 2, z).start()

        @pl.when(p.z + s <= p.n - 1)
        def _():
            z = p.z + s
            self.copy(q, 1, z).wait_recv()
            pl.when(p.has_left)(lambda: self.copy(q, 1, z).start())
            self.copy(q, 2, z).start()

    def finish(self, q):
        p = self.p
        for z in range(p.n):
            block = 2 * z + 1 - p.c
            ref = self.held.at[q, block]
            remote(ref, ref, self.ss.at[q, 2, z], self.rr.at[q, block], p.mate).wait_recv()

    def drain(self, q):
        p = self.p
        for z in range(p.n):
            self.copy(q, 2, z).wait_send()

            @pl.when(jnp.logical_and(p.has_right, p.z >= z))
            def _():
                self.copy(q, 0, z).wait_send()

            @pl.when(jnp.logical_and(p.has_left, p.z <= z))
            def _():
                self.copy(q, 1, z).wait_send()


def lane_tiles(width, size=256):
    return [(at, min(at + size, width)) for at in range(0, width, size)]


def put_share(place, own, stage, q, values, a, b):
    slots, n, rows, _ = own.shape
    parts = values.astype(BF16).reshape(n, 2, rows, b - a)

    @pl.when(place.c == 0)
    def _():
        own[q % slots, :, :, a:b] = parts[:, 0]
        stage[:, :, a:b] = parts[:, 1]

    @pl.when(place.c == 1)
    def _():
        own[q % slots, :, :, a:b] = parts[:, 1]
        stage[:, :, a:b] = parts[:, 0]


def ring_scratch(chunks, blocks, rows, depth):
    n = blocks // 2
    dma = pltpu.SemaphoreType.DMA
    return [
        pltpu.VMEM((min(chunks, n), n, rows, depth), BF16),
        pltpu.VMEM((n, rows, depth), BF16),
        pltpu.VMEM((chunks, n, rows, depth), BF16),
        pltpu.VMEM((chunks, n + 1, rows, depth), BF16),
        dma((chunks,)),
        dma((chunks,)),
        dma((chunks, n + 1)),
        dma((chunks, n + 1)),
    ]


def gather_scratch(chunks, blocks, rows, depth):
    dma = pltpu.SemaphoreType.DMA
    return [
        pltpu.VMEM((chunks, blocks, rows, depth), BF16),
        dma((chunks, 3, blocks // 2)),
        dma((chunks, blocks)),
    ]


def within(q, chunks):
    return jnp.logical_and(q >= 0, q < chunks)


def ticks(chunks, n, scatter, gather, partial, middle, consume, also=None):
    partial(0)
    scatter.swap(0).start()

    def tick(w, _):
        v = w - n + 1

        @pl.when(within(v, chunks))
        def _():
            middle(v)
            gather.step(v, 0)

        for s in range(n - 2, 0, -1):

            @pl.when(within(w - s, chunks))
            def _():
                scatter.step(w - s, s)

        @pl.when(w < chunks)
        def _():
            scatter.swap(w).wait_recv()
            scatter.step(w, 0)

        for s in range(n - 1, 0, -1):

            @pl.when(within(v - s, chunks))
            def _():
                gather.step(v - s, s)

        if also is not None:
            also(w)

        @pl.when(w + 1 < chunks)
        def _():
            scatter.swap(w).wait_send()
            partial(w + 1)
            scatter.swap(w + 1).start()

        @pl.when(v >= n - 1)
        def _():
            gather.finish(v - n + 1)
            consume(v - n + 1)

        return 0

    lax.fori_loop(0, chunks + 2 * n - 2, tick, 0)
    scatter.swap(chunks - 1).wait_send()

    def drain(q, _):
        scatter.drain(q)
        gather.drain(q)
        return 0

    lax.fori_loop(0, chunks, drain, 0)


def ffn_kernel(
    fuse, mixed_hbm, w_out_ref, input_hbm, gain_ref, w_gate_hbm, w_up_hbm, w_down_hbm, late_hbm,
    cot_hbm, resid_hbm, dgate_hbm, dup_hbm, down_hbm, gdown_hbm, *refs,
):
    outs, refs = refs[: 1 + fuse], refs[1 + fuse :]
    own, stage, cross, line, xs, xr, ls, lr, held, gs, gr, held2, gs2, gr2, *refs = refs
    w_gate, w_up, w_down, cot, hid, dg, du, down, gdown, total, mix, inp, res, *refs = refs
    wsem, csem, osem, dsem, msem, hsem, isem, rsem, *wide = refs
    chunks, blocks, rows, depth = held.shape
    units = w_gate.shape[0]
    p = Place(blocks)
    scatter = Scatter(p, own, stage, cross, line, xs, xr, ls, lr)
    gather = Gather(p, held, gs, gr)
    loads = [
        pltpu.make_async_copy(src, dst, wsem.at[i])
        for i, (src, dst) in enumerate(
            ((w_gate_hbm, w_gate), (w_up_hbm, w_up), (w_down_hbm, w_down))
        )
    ]
    for load in loads:
        load.start()
    cot_load = lambda q: pltpu.make_async_copy(cot_hbm.at[:, q], cot.at[q % 2], csem.at[q % 2])
    cot_load(0).start()
    early = cot_hbm.shape[1]
    mix_load = lambda q: pltpu.make_async_copy(mixed_hbm.at[:, q], mix, msem)
    mix_load(0).start()

    def own_rows(q):
        return pl.ds(pl.multiple_of(q * rows, rows), rows)

    in_load = lambda q: pltpu.make_async_copy(
        input_hbm.at[own_rows(q)], inp, isem
    )
    res_save = lambda q: pltpu.make_async_copy(
        res.at[q % 2], resid_hbm.at[own_rows(q)], rsem.at[q % 2]
    )
    in_load(0).start()

    def late_load(j):
        here = pl.ds(pl.multiple_of((early + j) * rows, rows), rows)
        return pltpu.make_async_copy(late_hbm.at[here], held2.at[j, p.me], hsem.at[j])

    for j in range(chunks - early):
        late_load(j).start()
    p.greet()
    later = Gather(p, held2, gs2, gr2)

    def also(w):
        for s in range(p.n - 1, -1, -1):

            @pl.when(within(w - s, chunks - early))
            def _():
                if s == 0:
                    late_load(w).wait()
                later.step(w - s, s)
                if s == p.n - 1:
                    later.finish(w - s)

    def partial(q):
        mix_load(q).wait()
        x = mix[...].reshape(blocks * rows, -1)
        for a, b in lane_tiles(depth, 512):
            put_share(
                p, own, stage, q, jnp.dot(x, w_out_ref[:, a:b], preferred_element_type=F32), a, b
            )

        @pl.when(q + 1 < chunks)
        def _():
            mix_load(q + 1).start()

    def middle(q):
        scatter.result(q, total)
        in_load(q).wait()
        @pl.when(q >= 2)
        def _():
            res_save(q - 2).wait()

        resid = inp[...].astype(F32) + total[...]
        res[q % 2] = resid
        res_save(q).start()

        @pl.when(q + 1 < chunks)
        def _():
            in_load(q + 1).start()

        normed = resid * lax.rsqrt(jnp.mean(resid * resid, axis=1, keepdims=True) + 1e-05)
        held[q, p.me] = (normed * gain_ref[...]).astype(BF16)

    def saves(q):
        slot = q % 2
        return [
            pltpu.make_async_copy(src.at[slot], dst.at[:, q], osem.at[slot, i])
            for i, (src, dst) in enumerate(((dg, dgate_hbm), (du, dup_hbm)))
        ] + [
            pltpu.make_async_copy(held.at[q], out.at[:, q], osem.at[slot, 3])
            for out in outs
            if not fuse
        ]

    def add_grad(acc, left, right):
        both = 2 * blocks * rows
        left, right = left[...].reshape(both, units), right.reshape(both, depth)
        for a, b in lane_tiles(depth, 256):
            acc[:, a:b] += mm(left, right[:, a:b], ta=True)

    def down_save(q):
        return pltpu.make_async_copy(down, down_hbm.at[:, q], osem.at[0, 2])

    def consume(q):
        slot = q % 2

        @pl.when(q == 0)
        def _():
            for load in loads:
                load.wait()
            for ref in (gdown, *wide):
                ref[...] = jnp.zeros_like(ref)

        @pl.when(q < early)
        def _():
            cot_load(q).wait()

        @pl.when(q >= early)
        def _():
            cot[slot] = held2[q - early]

        @pl.when(q >= 2)
        def _():
            for save in saves(q - 2):
                save.wait()

        if fuse:

            @pl.when(jnp.logical_and(slot == 0, q >= 2))
            def _():
                add_grad(wide[1], du, held[pl.ds(q - 2, 2)])

        x = held[q].reshape(blocks * rows, depth)
        g = cot[slot].reshape(blocks * rows, depth)
        for a, b in lane_tiles(units):
            gate = mm(x, w_gate[a:b, :], tb=True)
            up = mm(x, w_up[a:b, :], tb=True)
            gh = mm(g, w_down[a:b, :], tb=True)
            sg = sigmoid(gate)
            act = gate * sg
            shape = (blocks, rows, b - a)
            hid[slot, :, a:b] = (act * up).astype(BF16)
            dg[slot, :, :, a:b] = (
                (gh * up * sg * (1.0 + gate * (1.0 - sg))).astype(BF16).reshape(shape)
            )
            du[slot, :, :, a:b] = (gh * act).astype(BF16).reshape(shape)
        h = hid[slot]

        @pl.when(q >= 1)
        def _():
            down_save(q - 1).wait()

        for a, b in lane_tiles(depth, 512):
            down[:, :, a:b] = (
                jnp.dot(h, w_down[:, a:b], preferred_element_type=F32)
                .astype(BF16)
                .reshape(blocks, rows, b - a)
            )
        down_save(q).start()
        for save in saves(q):
            save.start()

        @pl.when(slot == 1)
        def _():
            add_grad(gdown, hid, cot[...])
            if fuse:
                add_grad(wide[0], dg, held[pl.ds(q - 1, 2)])

        @pl.when(q + 1 < early)
        def _():
            cot_load(q + 1).start()

    ticks(chunks, p.n, scatter, gather, partial, middle, consume, also)
    if fuse:
        add_grad(wide[1], du, held[pl.ds(chunks - 2, 2)])
    ends = []
    pairs = ((gdown, w_down, gdown_hbm), *zip(wide, (w_gate, w_up), outs))
    for i, (acc, low, out) in enumerate(pairs):
        low[...] = acc[...].astype(BF16)
        ends.append(pltpu.make_async_copy(low, out, dsem.at[i]))
        ends[-1].start()
    lax.fori_loop(0, chunks - early, lambda q, _: later.drain(q), None)
    for end in ends:
        end.wait()
    down_save(chunks - 1).wait()
    for q in range(max(chunks - 2, 0), chunks):
        res_save(q).wait()
    for q in range(max(chunks - 2, 0), chunks):
        for save in saves(q):
            save.wait()


def chunk_rows(blocks, owned):
    return min(owned, max(16, 2048 // (blocks * blocks)))


def early_chunks(chunks, blocks):
    return chunks - 32 * chunks // (blocks * blocks)


ANY = pl.BlockSpec(memory_space=pl.ANY)
WHOLE = pl.BlockSpec(memory_space=pltpu.VMEM)


def ffn(mixed, w_out, inputs, gain, w_gate, w_up, w_down, cot, early):
    owned, depth = inputs.shape
    blocks = mixed.shape[0] // owned
    rows = chunk_rows(blocks, owned)
    chunks = owned // rows
    units = w_gate.shape[0]
    fuse = blocks <= 8
    cut = lambda width: jax.ShapeDtypeStruct((blocks, chunks, rows, width), BF16)
    dma = pltpu.SemaphoreType.DMA
    return pl.pallas_call(
        functools.partial(ffn_kernel, fuse),
        in_specs=[ANY, WHOLE, ANY, WHOLE] + [ANY] * 5,
        out_specs=[ANY] * (6 + fuse),
        out_shape=[
            jax.ShapeDtypeStruct((owned, depth), F32),
            cut(units),
            cut(units),
            cut(depth),
            jax.ShapeDtypeStruct((units, depth), BF16),
            *([jax.ShapeDtypeStruct((units, depth), BF16)] * 2 if fuse else [cut(depth)]),
        ],
        scratch_shapes=ring_scratch(chunks, blocks, rows, depth)
        + gather_scratch(chunks, blocks, rows, depth)
        + gather_scratch(chunks - early_chunks(chunks, blocks), blocks, rows, depth)
        + [
            pltpu.VMEM(w_gate.shape, BF16),
            pltpu.VMEM(w_up.shape, BF16),
            pltpu.VMEM(w_down.shape, BF16),
            pltpu.VMEM((2, blocks, rows, depth), BF16),
            pltpu.VMEM((2, blocks * rows, units), BF16),
            pltpu.VMEM((2, blocks, rows, units), BF16),
            pltpu.VMEM((2, blocks, rows, units), BF16),
            pltpu.VMEM((blocks, rows, depth), BF16),
            pltpu.VMEM((units, depth), F32),
            pltpu.VMEM((rows, depth), F32),
            pltpu.VMEM((blocks, rows, mixed.shape[1]), BF16),
            pltpu.VMEM((rows, depth), BF16),
            pltpu.VMEM((2, rows, depth), F32),
            dma((3,)),
            dma((2,)),
            dma((2, 4)),
            dma((3,)),
            dma,
            dma((chunks - early_chunks(chunks, blocks),)),
            dma,
            dma((2,)),
            *[pltpu.VMEM((units, depth), F32)] * (2 * fuse),
        ],
        compiler_params=pltpu.CompilerParams(
            collective_id=1, has_side_effects=True, vmem_limit_bytes=127 * 512 * 1024
        ),
        name="ffn_rounds",
    )(
        mixed.reshape(blocks, chunks, rows, -1),
        w_out,
        inputs,
        gain,
        w_gate,
        w_up,
        w_down,
        cot,
        early.reshape(blocks, -1, rows, depth),
    )


def back_kernel(
    items, dgate_hbm, dup_hbm, w_gate_ref, w_up_ref, resid_hbm, gain_ref, cot_hbm, w_out_hbm, mixed_hbm, sd_hbm,
    gres_ref, ggain_ref, gout_ref, gm_hbm, rd_hbm,
    own, stage, cross, line, xs, xr, ls, lr, held, gs, gr, gm, total, gout, osem,
    dgate_ref, dup_ref, resid_ref, cot_ref, w_out_ref, mixed_ref, asem, bsem, done, *sums,
):
    chunks, blocks, rows, depth = held.shape
    p = Place(blocks)
    scatter = Scatter(p, own, stage, cross, line, xs, xr, ls, lr)
    gather = Gather(p, held, gs, gr)
    def shares(q):
        return [
            pltpu.make_async_copy(src.at[:, q], dst.at[:, q], asem.at[q, i])
            for i, (src, dst) in enumerate(((dgate_hbm, dgate_ref), (dup_hbm, dup_ref)))
        ]

    for load in shares(0):
        load.start()
    rest = [
        pltpu.make_async_copy(src, dst, bsem.at[i])
        for i, (src, dst) in enumerate(
            (
                (resid_hbm, resid_ref),
                (cot_hbm, cot_ref),
                (w_out_hbm, w_out_ref),
                (mixed_hbm, mixed_ref),
            )
        )
    ]
    p.greet(items)
    bits = items.bit_length() - 1
    reduce = Reduce(items, sd_hbm, sums[:bits], done, rd_hbm, *sums[bits:], axis=1)
    reduce.start()
    ggain_ref[...] = jnp.zeros_like(ggain_ref)

    def partial(q):
        for load in shares(q):
            load.wait()

        @pl.when(q == 0)
        def _():
            for i in range(1, chunks):
                for load in shares(i):
                    load.start()
            for load in rest:
                load.start()

        g = dgate_ref[:, q].reshape(blocks * rows, -1)
        u = dup_ref[:, q].reshape(blocks * rows, -1)
        for a, b in lane_tiles(depth, 512):
            put_share(
                p,
                own,
                stage,
                q,
                mm(g, w_gate_ref[:, a:b]) + mm(u, w_up_ref[:, a:b]),
                a,
                b,
            )

    def middle(q):
        @pl.when(q == 0)
        def _():
            for load in rest:
                load.wait()

        scatter.result(q, total)
        here = pl.ds(pl.multiple_of(q * rows, rows), rows)
        resid = resid_ref[here, :]
        n = lax.rsqrt(jnp.mean(resid * resid, axis=1, keepdims=True) + 1e-05)
        u = resid * n
        grad = total[...]
        ggain_ref[...] += jnp.sum((grad * u).reshape(rows // 8, 8, depth), axis=0)
        e = grad * gain_ref[...]
        gres = cot_ref[here, :].astype(F32) + n * (e - u * jnp.mean(e * u, axis=1, keepdims=True))
        gres_ref[here, :] = gres
        held[q, p.me] = gres.astype(BF16)

    def save(q):
        return pltpu.make_async_copy(gm.at[q % 2], gm_hbm.at[:, q], osem.at[q % 2])

    def consume(q):
        @pl.when(q >= 2)
        def _():
            save(q - 2).wait()

        @pl.when(q == 0)
        def _():
            gout[...] = jnp.zeros_like(gout)

        x = held[q].reshape(blocks * rows, depth)
        gm[q % 2] = mm(x, w_out_ref[...], tb=True).reshape(blocks, rows, -1)
        save(q).start()
        m = mixed_ref[:, q].reshape(blocks * rows, -1)
        for a, b in lane_tiles(depth, 1024):
            gout[:, a:b] += mm(m, x[:, a:b], ta=True)

    steps = reduce.handlers()

    def also(w):
        for i, step in enumerate(steps):
            at = 4 * len(steps) - 4 if i == len(steps) - 1 else 4 + 2 * i
            pl.when(w == at)(step)

    ticks(chunks, p.n, scatter, gather, partial, middle, consume, also)
    reduce.drain()
    for q in range(max(chunks - 2, 0), chunks):
        save(q).wait()
    gout_ref[...] = gout[...].astype(BF16)


def back(dgate, dup, w_gate, w_up, resid, gain, cot, w_out, mixed, grad_down, items):
    blocks, chunks, rows, _ = dgate.shape
    owned, depth = resid.shape
    width = w_out.shape[0]
    dma = pltpu.SemaphoreType.DMA
    return pl.pallas_call(
        functools.partial(back_kernel, items),
        in_specs=[ANY] * 2 + [WHOLE] * 2 + [ANY, WHOLE] + [ANY] * 4,
        out_specs=[WHOLE, WHOLE, WHOLE, ANY, ANY],
        out_shape=[
            jax.ShapeDtypeStruct((owned, depth), F32),
            jax.ShapeDtypeStruct((8, depth), F32),
            jax.ShapeDtypeStruct((width, depth), BF16),
            jax.ShapeDtypeStruct((blocks, chunks, rows, width), F32),
            jax.ShapeDtypeStruct(grad_down.shape, BF16),
        ],
        scratch_shapes=ring_scratch(chunks, blocks, rows, depth)
        + gather_scratch(chunks, blocks, rows, depth)
        + [
            pltpu.VMEM((2, blocks, rows, width), F32),
            pltpu.VMEM((rows, depth), F32),
            pltpu.VMEM((width, depth), F32),
            dma((2,)),
            pltpu.VMEM(dgate.shape, BF16),
            pltpu.VMEM(dup.shape, BF16),
            pltpu.VMEM(resid.shape, F32),
            pltpu.VMEM(cot.shape, BF16),
            pltpu.VMEM(w_out.shape, BF16),
            pltpu.VMEM((blocks, chunks, rows, width), BF16),
            dma((chunks, 2)),
            dma((4,)),
            *reduce_scratch(items, *grad_down.shape, axis=1),
        ],
        compiler_params=pltpu.CompilerParams(
            collective_id=2, has_side_effects=True, vmem_limit_bytes=63 * 1024 * 1024
        ),
        name="back_rounds",
    )(
        dgate,
        dup,
        w_gate,
        w_up,
        resid,
        gain,
        cot,
        w_out,
        mixed.reshape(blocks, chunks, rows, width),
        grad_down,
    )


def add_rows(out, left, right, count):
    size = 64 if count % 64 == 0 else 16

    def body(i, _):
        rows = lambda at: pl.ds(pl.multiple_of(at + i * size, 16), size)
        value = left[0][rows(left[1]), :].astype(F32) + right[0][rows(right[1]), :].astype(F32)
        out[0][rows(out[1]), :] = value.astype(out[0].dtype)
        return 0

    lax.fori_loop(0, count // size, body, 0)


def add_columns(out, left, right, count):
    size = 32
    total = out[0].shape[0]

    def body(i, _):
        rows = pl.ds(pl.multiple_of(i * size, size), size)
        cols = lambda at: pl.ds(pl.multiple_of(at, 128), count)
        value = left[0][rows, cols(left[1])].astype(F32) + right[0][rows, cols(right[1])].astype(F32)
        out[0][rows, cols(out[1])] = value.astype(out[0].dtype)
        return 0

    lax.fori_loop(0, total // size, body, 0)


class Reduce:
    def __init__(self, count, src, parts, done, out, ss, rr, load, save, axis=0):
        self.axis = axis
        self.add = (add_rows, add_columns)[axis]
        self.src, self.parts, self.done, self.out = src, parts, done, out
        self.ss, self.rr, self.load_sem, self.save_sem = ss, rr, load, save
        self.bits = count.bit_length() - 1
        item = lax.axis_index("item")
        total = src.shape[axis]
        self.plan = []
        for half in range(2):
            start = half * (total // 2)
            size = total // 2
            steps = []
            for k in range(self.bits):
                unit = 2 ** (k if half == 0 else self.bits - 1 - k)
                bit = (item // unit) % 2
                size //= 2
                keep = start + bit * size
                give = start + (1 - bit) * size
                steps.append((size, keep, give, bit * size, (1 - bit) * size, item + unit - 2 * unit * bit))
                start = keep
            self.plan.append(steps)

    def rows(self, ref, at, size):
        if self.axis:
            return ref.at[:, pl.ds(pl.multiple_of(at, 128), size)]
        return ref.at[pl.ds(pl.multiple_of(at, 16), size)]

    def load(self, half):
        size, keep = self.plan[half][0][:2]
        return pltpu.make_async_copy(
            self.rows(self.src, keep, size), self.rows(self.done, keep, size), self.load_sem.at[half]
        )

    def down(self, half, k):
        size, _, give, _, local, partner = self.plan[half][k]
        source = self.rows(self.src, give, size) if k == 0 else self.rows(self.parts[k - 1].at[half], local, size)
        return pltpu.make_async_remote_copy(
            src_ref=source,
            dst_ref=self.parts[k].at[half],
            send_sem=self.ss.at[half, k],
            recv_sem=self.rr.at[half, k],
            device_id={"item": partner},
            device_id_type=MESH,
        )

    def up(self, half, k, back=False):
        size, keep, give, _, _, partner = self.plan[half][k]
        ref = self.rows(self.done, give if back else keep, size)
        return pltpu.make_async_remote_copy(
            src_ref=ref,
            dst_ref=ref,
            send_sem=self.ss.at[half, self.bits + k],
            recv_sem=self.rr.at[half, self.bits + k],
            device_id={"item": partner},
            device_id_type=MESH,
        )

    def start(self):
        for half in range(2):
            self.load(half).start()
            self.down(half, 0).start()

    def halve(self, k):
        for half in range(2):
            size, keep, _, local, _, _ = self.plan[half][k]
            if k == 0:
                self.load(half).wait()
                mine = (self.done, keep)
            else:
                mine = (self.parts[k - 1].at[half], local)
            self.down(half, k).wait_recv()
            part = (self.parts[k].at[half], 0)
            if k + 1 < self.bits:
                self.add(part, mine, part, size)
                self.down(half, k + 1).start()
            else:
                self.add((self.done, keep), mine, part, size)
                self.up(half, k).start()

    def double(self, k):
        for half in range(2):
            self.up(half, k, True).wait_recv()
            self.up(half, k - 1).start()

    def save(self):
        return pltpu.make_async_copy(self.done, self.out, self.save_sem)

    def finish(self):
        for half in range(2):
            self.up(half, 0, True).wait_recv()
        self.save().start()

    def drain(self):
        for half in range(2):
            for k in range(self.bits):
                self.down(half, k).wait_send()
                self.up(half, k).wait_send()
        self.save().wait()

    def handlers(self):
        return (
            [functools.partial(self.halve, k) for k in range(self.bits)]
            + [functools.partial(self.double, k) for k in range(self.bits - 1, 0, -1)]
            + [self.finish]
        )


def reduce_scratch(count, total, width, axis=0):
    dma = pltpu.SemaphoreType.DMA
    bits = count.bit_length() - 1
    return [
        pltpu.VMEM((total, width), BF16),
        *[
            pltpu.VMEM(
                (2, total, width // 2 ** (k + 2)) if axis else (2, total // 2 ** (k + 2), width), BF16
            )
            for k in range(bits)
        ],
        dma((2, 2 * bits)),
        dma((2, 2 * bits)),
        dma((2,)),
        dma,
    ]


class Peers:
    def __init__(self, axis, count, held, ss, rr):
        self.axis, self.count, self.held, self.ss, self.rr = axis, count, held, ss, rr
        self.me = lax.axis_index(axis)

    def other(self, k):
        return (self.me + k) % self.count

    def copy(self, slot, k):
        ref = self.held.at[slot]
        return pltpu.make_async_remote_copy(
            src_ref=ref,
            dst_ref=ref,
            send_sem=self.ss.at[k],
            recv_sem=self.rr.at[slot],
            device_id={self.axis: self.other(k)},
            device_id_type=MESH,
        )

    def greet(self):
        barrier = pltpu.get_barrier_semaphore()
        for k in range(1, self.count):
            pl.semaphore_signal(
                barrier, inc=1, device_id={self.axis: self.other(k)}, device_id_type=MESH
            )

    def send(self):
        for k in range(1, self.count):
            self.copy(self.me, k).start()

    def total(self):
        for k in range(1, self.count):
            self.copy(self.other(k), k).wait_recv()
        out = self.held[0]
        for slot in range(1, self.count):
            out = out + self.held[slot]
        return out

    def drain(self):
        for k in range(1, self.count):
            self.copy(self.me, k).wait_send()


def tail_kernel(
    gq_hbm, gk_hbm, gv_hbm, gg_hbm, gdw_hbm, wq_ref, wk_ref, wv_ref, wg_ref, wdw_ref,
    input_hbm, gain_ref, gres_hbm, resid_hbm, fgain_ref, ogain_ref, conv_ref, dl_ref, wide_ref, down_hbm,
    output_ref, igrad_ref, small_ref,
    own, stage, cross, line, xs, xr, ls, lr, own2, cross2, line2, xs2, xr2, ls2, lr2, osem,
    total, ngain, held1, held2, s1, r1, s2, r2,
    gq_ref, gk_ref, gv_ref, gg_ref, gdw_ref, input_ref, gres_ref, resid_ref, asem, bsem,
):
    chunks, n, rows, depth = cross.shape
    blocks = 2 * n
    p = Place(blocks)
    first = Scatter(p, own, stage, cross, line, xs, xr, ls, lr)
    first_late = chunks - cross2.shape[0]
    second = Late(p, down_hbm, first_late, own2, cross2, line2, xs2, xr2, ls2, lr2, osem)
    sources = (
        (gq_hbm, gq_ref), (gk_hbm, gk_ref), (gv_hbm, gv_ref), (gg_hbm, gg_ref), (gdw_hbm, gdw_ref)
    )

    def shares(q):
        return [
            pltpu.make_async_copy(src.at[:, q], dst.at[:, q], asem.at[q, i])
            for i, (src, dst) in enumerate(sources)
        ]

    for load in shares(0):
        load.start()
    rest = [
        pltpu.make_async_copy(src, dst, bsem.at[i])
        for i, (src, dst) in enumerate(
            ((input_hbm, input_ref), (gres_hbm, gres_ref), (resid_hbm, resid_ref))
        )
    ]
    heads = Peers("head", held1.shape[0], held1, s1, r1)
    items = Peers("item", held2.shape[0], held2, s2, r2)
    heads.greet()
    items.greet()
    pl.semaphore_wait(pltpu.get_barrier_semaphore(), heads.count + items.count - 2)
    ngain[...] = jnp.zeros_like(ngain)
    width1 = held1.shape[2]
    half = conv_ref.shape[2] // 2
    held1[heads.me] = jnp.zeros(held1.shape[1:], F32)
    held2[items.me] = jnp.zeros(held2.shape[1:], F32)

    second.start()
    def finish_late(j):
        here = pl.ds(pl.multiple_of(j * rows, rows), rows)
        second.scatter.result(j, total)
        there = pl.ds(pl.multiple_of((first_late + j) * rows, rows), rows)
        output_ref[here, :] = (resid_ref[there, :] + total[...]).astype(BF16)

    def partial(q):
        for load in shares(q):
            load.wait()

        @pl.when(q == 0)
        def _():
            for i in range(1, chunks):
                for load in shares(i):
                    load.start()
            for load in rest:
                load.start()

        pairs = [
            (ref[:, q].reshape(blocks * rows, -1), w)
            for ref, w in ((gq_ref, wq_ref), (gk_ref, wk_ref), (gv_ref, wv_ref), (gg_ref, wg_ref))
        ]
        dw = gdw_ref[:, q].reshape(blocks * rows, -1)
        for a, b in lane_tiles(depth, 512):
            value = mm(dw, wdw_ref[:, a:b])
            for x, w in pairs:
                value = value + mm(x, w[a:b, :], tb=True)
            put_share(p, own, stage, q, value, a, b)

    partial(0)
    first.swap(0).start()
    for load in rest:
        load.wait()

    def end(q):
        here = pl.ds(pl.multiple_of(q * rows, rows), rows)
        first.result(q, total)
        x = input_ref[here, :].astype(F32)
        scale = lax.rsqrt(jnp.mean(x * x, axis=1, keepdims=True) + 1e-05)
        u = x * scale
        grad = total[...]
        ngain[...] += jnp.sum((grad * u).reshape(rows // 8, 8, depth), axis=0)
        e = grad * gain_ref[...]
        igrad_ref[here, :] = gres_ref[here, :] + scale * (
            e - u * jnp.mean(e * u, axis=1, keepdims=True)
        )

    def turn(w, _):
        pl.when(within(w - n + 1, chunks))(lambda: end(w - n + 1))
        for s in range(n - 2, 0, -1):
            pl.when(within(w - s, chunks))(lambda: first.step(w - s, s))

        @pl.when(w < chunks)
        def _():
            first.swap(w).wait_recv()
            first.step(w, 0)

        second.tick(w, finish_late)

        @pl.when(w + 1 < chunks)
        def _():
            first.swap(w).wait_send()
            partial(w + 1)
            first.swap(w + 1).start()

        return 0

    lax.fori_loop(0, chunks + n - 1, turn, 0)
    part = depth // 8
    for at, ref in ((0, ngain), (part, fgain_ref)):
        row = jnp.sum(ref[...], axis=0, keepdims=True)
        for i in range(8):
            held1[heads.me, i : i + 1, at : at + part] = row[:, i * part : (i + 1) * part]
    row = jnp.sum(ogain_ref[...], axis=0, keepdims=True)
    for i in range(2):
        held1[heads.me, i : i + 1, 2 * part : 2 * part + 128] = row[:, i * 128 : (i + 1) * 128]
    heads.send()
    for j in range(4):
        row = jnp.sum(conv_ref[j], axis=0, keepdims=True)
        for i in range(2):
            held2[items.me, 4 * i + j : 4 * i + j + 1, width1 : width1 + half] = row[
                :, i * half : (i + 1) * half
            ]
    at = width1 + half + 128
    held2[items.me, 0:1, width1 + half : at] = dl_ref[...]
    held2[items.me, :, at:] = wide_ref[...]
    held2[items.me, :, 0:width1] = heads.total()
    items.send()

    def drain(q, _):
        first.drain(q)
        return 0

    lax.fori_loop(0, chunks, drain, 0)
    second.drain()
    first.swap(chunks - 1).wait_send()
    small_ref[...] = items.total()
    heads.drain()
    items.drain()


def tail(grads, weights, inputs, gain, gres, resid, fgain, ogain, gconv, gdl, wide, down, items):
    blocks, chunks, rows, depth = down.shape
    owned = inputs.shape[0]
    n = blocks // 2
    cut = lambda value: value.reshape(blocks, chunks, rows, -1)
    width1 = depth // 4 + 128
    width2 = width1 + gconv.shape[2] // 2 + 128 + wide.size // 8
    gdl = jnp.pad(gdl, ((0, 0), (0, 128 - gdl.shape[1])))
    dma = pltpu.SemaphoreType.DMA
    one = ring_scratch(chunks, blocks, rows, depth)
    late = chunks - 3 * chunks // 4
    output, igrad, small = pl.pallas_call(
        tail_kernel,
        in_specs=[ANY] * 5 + [WHOLE] * 5 + [ANY, WHOLE, ANY, ANY] + [WHOLE] * 5 + [ANY],
        out_specs=[WHOLE] * 3,
        out_shape=[
            jax.ShapeDtypeStruct((late * rows, depth), BF16),
            jax.ShapeDtypeStruct((owned, depth), F32),
            jax.ShapeDtypeStruct((8, width2), F32),
        ],
        scratch_shapes=one
        + late_scratch(late, min(late, n), blocks, rows, depth)
        + [
            pltpu.VMEM((rows, depth), F32),
            pltpu.VMEM((8, depth), F32),
            pltpu.VMEM((blocks, 8, width1), F32),
            pltpu.VMEM((items, 8, width2), F32),
            dma((blocks,)),
            dma((blocks,)),
            dma((items,)),
            dma((items,)),
            *[pltpu.VMEM(cut(value).shape, BF16) for value in grads],
            pltpu.VMEM(inputs.shape, BF16),
            pltpu.VMEM(gres.shape, F32),
            pltpu.VMEM(resid.shape, F32),
            dma((chunks, 5)),
            dma((3,)),
        ],
        compiler_params=pltpu.CompilerParams(
            collective_id=3, has_side_effects=True, vmem_limit_bytes=63 * 1024 * 1024
        ),
        name="tail_rounds",
    )(
        *[cut(value) for value in grads],
        *weights,
        inputs,
        gain,
        gres,
        resid,
        fgain,
        ogain,
        gconv,
        gdl,
        wide.reshape(8, -1),
        down.reshape(n, 2, chunks, rows, depth),
    )
    part = depth // 8
    half = gconv.shape[2] // 2
    conv = small[:, width1 : width1 + half]
    return (
        output,
        igrad,
        small[:, :part].reshape(-1),
        small[:, part : 2 * part].reshape(-1),
        small[:2, 2 * part : 2 * part + 128].reshape(-1),
        jnp.concatenate([conv[:4], conv[4:]], axis=1),
        small[0, width1 + half : width1 + half + 128],
        small[:, width1 + half + 128 :].reshape(wide.shape),
    )


def head_kernel(
    input_ref, gain_ref, cot_hbm, wq_hbm, wk_hbm, wv_hbm, wg_hbm, wdw_ref,
    dw_ref, early_hbm, group_hbm, q_hbm, k_hbm, v_hbm, g_hbm,
    held, gs, gr, pq, pk, pv, pg, gsem, osem, esem, wsem, wq_ref, wk_ref, wv_ref, wg_ref,
):
    chunks, blocks, rows, depth = held.shape
    p = Place(blocks)
    gather = Gather(p, held, gs, gr)
    early = pltpu.make_async_copy(cot_hbm.at[0 : early_hbm.shape[0]], early_hbm, esem)
    early.start()
    loads = [
        pltpu.make_async_copy(src, dst, wsem.at[i])
        for i, (src, dst) in enumerate(
            ((wq_hbm, wq_ref), (wk_hbm, wk_ref), (wv_hbm, wv_ref), (wg_hbm, wg_ref))
        )
    ]
    p.greet()
    for q in range(chunks):
        x = input_ref[q * rows : (q + 1) * rows, :].astype(F32)
        x = x * lax.rsqrt(jnp.mean(x * x, axis=1, keepdims=True) + 1e-05)
        held[q, p.me] = (x * gain_ref[...]).astype(BF16)
        gather.step(q, 0)
    for load in loads:
        load.start()

    def saves(q):
        slot = q % 2
        return [
            pltpu.make_async_copy(src.at[slot], dst.at[:, q], osem.at[slot, i])
            for i, (src, dst) in enumerate(((pq, q_hbm), (pk, k_hbm), (pv, v_hbm), (pg, g_hbm)))
        ]

    def group_save(q):
        return pltpu.make_async_copy(held.at[q], group_hbm.at[:, q], gsem.at[q])

    def consume(q):
        gather.finish(q)
        group_save(q).start()

        @pl.when(q == 0)
        def _():
            for load in loads:
                load.wait()

        @pl.when(q >= 2)
        def _():
            for save in saves(q - 2):
                save.wait()

        x = held[q].reshape(blocks * rows, depth)
        for out, weight in ((pq, wq_ref), (pk, wk_ref), (pv, wv_ref), (pg, wg_ref)):
            for a, b in lane_tiles(weight.shape[1]):
                out[q % 2, :, :, a:b] = jnp.dot(
                    x, weight[:, a:b], preferred_element_type=F32
                ).reshape(blocks, rows, b - a)
        dw_ref[:, q] = mm(x, wdw_ref[...], tb=True).reshape(blocks, rows, -1)
        for save in saves(q):
            save.start()

    last = p.n - 1

    def turn(w, _):
        for s in range(1, p.n):

            @pl.when(jnp.logical_and(w >= s - 1, w - s + 1 < chunks))
            def _():
                gather.step(w - s + 1, s)

        @pl.when(w >= last)
        def _():
            consume(w - last)

        return 0

    lax.fori_loop(0, chunks + last, turn, 0)
    for q in range(max(chunks - 2, 0), chunks):
        for save in saves(q):
            save.wait()
    early.wait()

    def drain(q, _):
        gather.drain(q)
        group_save(q).wait()
        return 0

    lax.fori_loop(0, chunks, drain, 0)


def head(inputs, gain, cot, weights, thin, blocks):
    owned, depth = inputs.shape
    rows = chunk_rows(blocks, owned)
    chunks = owned // rows
    cut = lambda width, kind: jax.ShapeDtypeStruct((blocks, chunks, rows, width), kind)
    dma = pltpu.SemaphoreType.DMA
    return pl.pallas_call(
        head_kernel,
        in_specs=[WHOLE] * 2 + [ANY] * 5 + [WHOLE],
        out_specs=[WHOLE] + [ANY] * 6,
        out_shape=[
            cut(thin.shape[0], F32),
            jax.ShapeDtypeStruct((early_chunks(chunks, blocks) * rows, depth), BF16),
            cut(depth, BF16),
        ]
        + [cut(weight.shape[1], F32) for weight in weights],
        scratch_shapes=gather_scratch(chunks, blocks, rows, depth)
        + [pltpu.VMEM((2, blocks, rows, weight.shape[1]), F32) for weight in weights]
        + [dma((chunks,)), dma((2, 4)), dma, dma((4,))]
        + [pltpu.VMEM(weight.shape, BF16) for weight in weights],
        compiler_params=pltpu.CompilerParams(
            collective_id=4, has_side_effects=True, vmem_limit_bytes=62 * 1024 * 1024
        ),
        name="head_rounds",
    )(inputs, gain, cot, *weights, thin)


def widen_kernel(count, *refs):
    for source, out in zip(refs[:count], refs[count:]):
        out[...] = source[...].astype(F32)


def widen(values, parts):
    spec = [
        pl.BlockSpec((value.shape[0] // parts, value.shape[1]), lambda i: (i, 0)) for value in values
    ]
    return pl.pallas_call(
        functools.partial(widen_kernel, len(values)),
        grid=(parts,),
        in_specs=spec,
        out_specs=spec,
        out_shape=[jax.ShapeDtypeStruct(value.shape, F32) for value in values],
        compiler_params=pltpu.CompilerParams(
            dimension_semantics=("arbitrary",), vmem_limit_bytes=63 * 1024 * 1024
        ),
        name="widen",
    )(*values)


def inner_rows(left, right):
    return lax.dot_general(
        left, right, (((0,), (0,)), ((), ())), preferred_element_type=jnp.float32
    )


def gather(values):
    return lax.all_gather(values.astype(jnp.bfloat16), "head", axis=0, tiled=True)


def scatter(values):
    return lax.psum_scatter(values, "head", scatter_dimension=0, tiled=True)


def total(values):
    return lax.psum([value.astype(jnp.bfloat16) for value in values], "item")


def after(values, *earlier):
    return lax.optimization_barrier((values, earlier))[0]


def local(
    items,
    blocks,
    layer_input,
    lengths,
    norm_gain,
    w_query,
    w_key,
    w_value,
    w_outgate,
    w_decay,
    w_write,
    conv_query,
    conv_key,
    conv_value,
    decay_log,
    out_gain,
    w_out,
    ffn_gain,
    w_gate,
    w_up,
    w_down,
    cotangent,
):
    ng = norm_gain.astype(F32).reshape(1, -1)
    fg = ffn_gain.astype(F32).reshape(1, -1)
    og = out_gain.astype(F32).reshape(1, DV)
    conv = jnp.concatenate([conv_query, conv_key, conv_value], axis=1).astype(F32)
    dl = decay_log.reshape(1, -1)
    w_dw = jnp.concatenate([w_decay.T, w_write.T], axis=0)
    gate_t, up_t = w_gate.T, w_up.T
    owned, depth = layer_input.shape
    tokens = owned * blocks
    flat = lambda value: value.reshape(tokens, -1)
    by_seq = lambda value: value.reshape(-1, SEQ_LEN, value.shape[-1])
    raw_dw, early, group, *raw = head(
        layer_input, ng, cotangent, (w_query, w_key, w_value, w_outgate), w_dw, blocks
    )
    group = flat(group)
    early = gather(early)
    raw = [by_seq(flat(value)) for value in (*raw, raw_dw)]
    mixed, *kept = mixer_fwd(lengths, *raw, conv, dl, og)
    mixed = flat(mixed)
    resid, dgate, dup, down, grad_down, *rest = ffn(
        mixed, w_out, layer_input, fg, gate_t, up_t, w_down, cotangent, early
    )
    if len(rest) == 1:
        rest = [inner_rows(flat(value), flat(rest[0])) for value in (dgate, dup)]
    ffn_sums = total(rest)
    grad_resid, fgain, grad_w_out, grad_mixed, down_sum = back(
        dgate, dup, gate_t, up_t, resid, fg, cotangent, w_out, mixed, grad_down, items
    )
    backward = mixer_bwd(
        lengths, *raw, conv, dl, og, by_seq(flat(grad_mixed)), *kept, by_seq(group), resid, down,
        grad_w_out, items
    )
    grads, (gconv, gdl, ogain), wide, thin = backward[:5], backward[5:8], backward[8:12], backward[12]
    first, out_sum = backward[13:]
    mix_sums = total(after(list(wide), ffn_sums))
    grads = [flat(value) for value in grads]
    output, input_grad, ngain, fgain, ogain, conv_grad, dl_grad, thin = tail(
        grads,
        (w_query, w_key, w_value, w_outgate, w_dw),
        layer_input,
        ng,
        grad_resid,
        resid,
        fgain,
        ogain,
        gconv,
        gdl,
        thin,
        down,
        items,
    )
    output = jnp.concatenate([first, output])
    gate_sum, up_sum, down_sum, out_sum, input_grad = widen(
        (*ffn_sums, down_sum, out_sum, input_grad), w_down.shape[0] // 176
    )
    heads = dl.shape[1]
    qw = w_query.shape[1]
    return (
        output,
        input_grad,
        ngain,
        *widen(mix_sums, 4),
        thin[:heads].T,
        thin[heads:].T,
        conv_grad[:, :qw],
        conv_grad[:, qw : 2 * qw],
        conv_grad[:, 2 * qw :],
        dl_grad[:heads],
        ogain,
        out_sum,
        fgain,
        gate_sum.T,
        up_sum.T,
        down_sum,
    )


def solution(mesh):
    rows = P(("item", "head"), None)
    cols = P(None, "head")
    deep = P("head", None)
    return jax.shard_map(
        functools.partial(local, mesh.shape["item"], mesh.shape["head"]),
        mesh=mesh,
        in_specs=(rows, P("item"), P(), *[cols] * 9, P("head"), P(), deep, P(), cols, cols, deep, rows),
        out_specs=(rows, rows, P(), *[cols] * 9, P("head"), P(), deep, P(), cols, cols, deep),
        check_vma=False,
    )
```
